32 devices in a mesh: dp: 4 (over z), expert: 8 (over y, x, core).
Axes of the slice: x: 2, y: 2, z: 4, core: 2. Of those that a mesh axis runs over, the one named last changes fastest.
Arguments:
- tokens: bfloat16 [4096, 2048], P(('dp', 'expert')), may hold values from -6 to 6
- norm1_gain: float32 [2048], replicated, may hold values from 0.25 to 1.75
- w_query: bfloat16 [2048, 4096], P('dp', 'expert'), may hold values from -0.125 to 0.125
- key_weight: bfloat16 [2048, 512], P('dp', 'expert'), may hold values from -0.125 to 0.125
- value_weight: bfloat16 [2048, 512], P('dp', 'expert'), may hold values from -0.125 to 0.125
- w_out: bfloat16 [4096, 2048], P('expert', 'dp'), may hold values from -1 to 1
- query_gain: float32 [128], replicated, may hold values from 0.25 to 1.75
- key_gain: float32 [128], replicated, may hold values from 0.25 to 1.75
- norm2_gain: float32 [2048], replicated, may hold values from 0.25 to 1.75
- w_router: bfloat16 [2048, 32], replicated, may hold values from -0.0625 to 0.0625
- w_gate: bfloat16 [32, 2048, 768], P(('dp', 'expert')), may hold values from -0.125 to 0.125
- w_up: bfloat16 [32, 2048, 768], P(('dp', 'expert')), may hold values from -0.125 to 0.125
- w_down: bfloat16 [32, 768, 2048], P(('dp', 'expert')), may hold values from -0.625 to 0.625
- routes: int32 [4096, 8], P(('dp', 'expert')), may hold values from 0 to 31, all different within a row; in each aligned block of 128 rows (0 to 127, 128 to 255, ...) at most 36 rows name the same one
- out_grad: bfloat16 [4096, 2048], P(('dp', 'expert')), may hold values from -6 to 6
Outputs:
- layer_out: bfloat16 [4096, 2048], P(('dp', 'expert'))
- grad_tokens: float32 [4096, 2048], P(('dp', 'expert'))
- grad_norm1_gain: float32 [2048], replicated
- grad_w_query: float32 [2048, 4096], P('dp', 'expert')
- grad_w_key: float32 [2048, 512], P('dp', 'expert')
- grad_w_value: float32 [2048, 512], P('dp', 'expert')
- grad_w_out: float32 [4096, 2048], P('expert', 'dp')
- grad_query_gain: float32 [128], replicated
- grad_key_gain: float32 [128], replicated
- grad_norm2_gain: float32 [2048], replicated
- grad_w_router: float32 [2048, 32], replicated
- grad_w_gate: float32 [32, 2048, 768], P(('dp', 'expert'))
- grad_w_up: float32 [32, 2048, 768], P(('dp', 'expert'))
- grad_w_down: float32 [32, 768, 2048], P(('dp', 'expert'))
The draws below stay inside these ranges and needn't reach their ends.
Inputs may be any that keep to these rules, and one draw needn't show every extreme that they name: `routes`: each row names 8 different experts. In the rows of one device (aligned blocks of 128 rows) no expert is named by more than 36 rows, and in every draw some block names some expert exactly 36 times.
All inputs are finite; a program needn't handle non-finite values.
Results may differ from the reference program's by a relative error of at most 0.019.
Values may be sent and summed in bfloat16 or wider, within the bound.
A program may use at most 192 MiB of HBM per device.

```python
import math
import jax
import jax.numpy as jnp
import numpy as np
from jax import lax

MODEL_DIMENSION = 2048
QUERY_HEADS = 32
KEY_VALUE_HEADS = 4
HEAD_DIMENSION = 128
FF = 768
TOPK = 8
TOK_DEV = 128
TOKENS = 4096
EXPERTS = 32
SEQ = 1024
CAP = 36
N_EXPERT = 8


def block_scale(rng, extent, shards, low, largest):
    gain = 1.0
    for axis_at, blocks in shards:
        draws = jax.random.uniform(jax.random.fold_in(jax.random.fold_in(rng, 6), axis_at), (blocks,), jnp.float32, low / len(shards), largest / len(shards))
        gain = gain * jnp.repeat(jnp.exp(draws), extent[axis_at] // blocks).reshape((-1,) + (1,) * (len(extent) - 1 - axis_at))
    return gain


def assign_block(key, own, number, rows, amount, top, reach, slope):
    order = jax.random.permutation(key, amount)
    packed, usual = shares(amount, rows * top, reach, slope, True), shares(amount, rows * top, reach, slope, False)
    places = jnp.arange(amount)

    def named(sizes, offset_by):
        used = int((sizes > 0).sum())
        fixed = max(1, used // 4)
        passed = fixed + (places - fixed + offset_by * (used - fixed)) % max(1, amount - fixed)
        return jnp.zeros((amount,), jnp.int32).at[order[jnp.where(places < fixed, places, passed)]].set(jnp.asarray(sizes, jnp.int32))

    sizes = jnp.where(number % 4 == 0, named(packed, number // 4), named(usual, number - number // 4 - 1))
    mixed = jax.random.permutation(jax.random.fold_in(own, 3), amount)
    source_of, sink = mixed[0:amount // 2 * 2:2], mixed[1:amount // 2 * 2:2]
    room = jnp.minimum(sizes[source_of] - 1, reach - sizes[sink]) // 2
    room = jnp.where((source_of == order[0]) | (sink == order[0]) | (sizes[sink] == 0), 0, jnp.maximum(room, 0))
    passed = jax.random.randint(jax.random.fold_in(own, 4), (amount // 2,), 0, 1 << 20) % (room + 1)
    sizes = sizes.at[source_of].add(-passed).at[sink].add(passed)
    members = jnp.searchsorted(jnp.cumsum(sizes), jnp.arange(rows * top), side="right").astype(jnp.int32)
    table = members.reshape(top, rows).T
    table = table[jax.random.permutation(jax.random.fold_in(own, 1), rows)]
    offset_by = jax.random.randint(jax.random.fold_in(own, 2), (rows, 1), 0, top)
    return jnp.take_along_axis(table, (jnp.arange(top)[None, :] + offset_by) % top, axis=1)


def shares(amount, total, limit, skew, full):
    weights = [(1 << 20) // math.isqrt(rank ** skew) + 1 for rank in range(1, amount + 1)]
    largest = limit if full else min(limit, max(-(-total // amount), total * weights[0] // sum(weights)))
    least = 1 if total - largest >= amount - 1 else 0
    holding, rest = [largest] + [least] * (amount - 1), total - largest - least * (amount - 1)
    while rest > 0:
        movable = [i for i in range(1, amount) if holding[i] < largest] or [i for i in range(1, amount) if holding[i] < limit]
        mass, budget = sum([weights[i] for i in movable]), rest
        for i in movable:
            addition = min(limit - holding[i], max(1, budget * weights[i] // mass), rest)
            holding[i] = holding[i] + addition
            rest = rest - addition
    return np.array(holding)


def scatter_about(key, dims, width, most, cuts=(), kind=jnp.bfloat16):
    array = jax.random.normal(key, dims, jnp.float32) * width
    if len(cuts) > 0:
        array = block_scale(key, dims, cuts, -0.22, 0.18) * array
    return jnp.clip(array, min=-most, max=most).astype(kind)


def setup_inputs(seed: int = 0) -> dict:
    seeds = jax.random.split(jax.random.key(seed), 16)
    tokens = scatter_about(seeds[0], (TOKENS, MODEL_DIMENSION), 1.0, 6.0, ((0, 32),))
    norm1_gain = jnp.clip(1.0 + 0.15 * jax.random.normal(seeds[1], (MODEL_DIMENSION,), jnp.float32), 0.25, 1.75)
    w_query = scatter_about(seeds[2], (MODEL_DIMENSION, QUERY_HEADS * HEAD_DIMENSION), MODEL_DIMENSION ** -0.5, 0.125, ((0, 4), (1, 8)))
    key_weight = scatter_about(seeds[3], (MODEL_DIMENSION, KEY_VALUE_HEADS * HEAD_DIMENSION), MODEL_DIMENSION ** -0.5, 0.125, ((0, 4), (1, 8)))
    value_weight = scatter_about(seeds[4], (MODEL_DIMENSION, KEY_VALUE_HEADS * HEAD_DIMENSION), MODEL_DIMENSION ** -0.5, 0.125, ((0, 4), (1, 8)))
    w_out = scatter_about(seeds[5], (QUERY_HEADS * HEAD_DIMENSION, MODEL_DIMENSION), (QUERY_HEADS * HEAD_DIMENSION // 128) ** -0.5, 1.0, ((0, 8), (1, 4)))
    query_gain = jnp.clip(1.0 + 0.15 * jax.random.normal(seeds[6], (HEAD_DIMENSION,), jnp.float32), 0.25, 1.75)
    key_gain = jnp.clip(1.0 + 0.15 * jax.random.normal(seeds[7], (HEAD_DIMENSION,), jnp.float32), 0.25, 1.75)
    norm2_gain = jnp.clip(1.0 + 0.15 * jax.random.normal(seeds[8], (MODEL_DIMENSION,), jnp.float32), 0.25, 1.75)
    w_router = scatter_about(seeds[9], (MODEL_DIMENSION, EXPERTS), (4 * MODEL_DIMENSION) ** -0.5, 0.0625)
    w_gate = scatter_about(seeds[10], (EXPERTS, MODEL_DIMENSION, FF), MODEL_DIMENSION ** -0.5, 0.125, ((0, 32),))
    w_up = scatter_about(seeds[11], (EXPERTS, MODEL_DIMENSION, FF), MODEL_DIMENSION ** -0.5, 0.125, ((0, 32),))
    w_down = scatter_about(seeds[12], (EXPERTS, FF, MODEL_DIMENSION), (FF // 8) ** -0.5, 0.625, ((0, 32),))
    routes_keys = jax.random.split(jax.random.fold_in(seeds[13], 1), TOKENS // TOK_DEV)
    routes_turns = jax.random.permutation(jax.random.fold_in(seeds[13], 3), TOKENS // TOK_DEV)
    routes = jax.vmap(lambda own, number: assign_block(jax.random.fold_in(seeds[13], 2), own, number, TOK_DEV, EXPERTS, TOPK, CAP, 1))(routes_keys, routes_turns).reshape((TOKENS, TOPK))
    out_grad = scatter_about(seeds[14], (TOKENS, MODEL_DIMENSION), 1.0, 6.0, ((0, 32),))
    return {"tokens": tokens, "norm1_gain": norm1_gain, "w_query": w_query, "key_weight": key_weight, "value_weight": value_weight, "w_out": w_out, "query_gain": query_gain, "key_gain": key_gain, "norm2_gain": norm2_gain, "w_router": w_router, "w_gate": w_gate, "w_up": w_up, "w_down": w_down, "routes": routes, "out_grad": out_grad}


NORM_EPS = 1e-06
ROPE_THETA = 1000000.0

@jax.custom_vjp
def low(v):
    return lax.optimization_barrier(v.astype(jnp.bfloat16)).astype(jnp.float32)

@jax.custom_vjp
def low_back(v):
    return v

def low_keep(v):
    return (low(v), None)

def low_pass(kept, grad):
    return (grad,)

def back_keep(v):
    return (v, None)

def back_low(kept, grad):
    return (low(grad),)
low.defvjp(low_keep, low_pass)
low_back.defvjp(back_keep, back_low)

def precise_product(left, right):
    return jnp.dot(left, right, precision=lax.Precision.HIGHEST, preferred_element_type=jnp.float32)

def row_norm(value_tensor, gain_vec):
    return value_tensor * lax.rsqrt(lax.optimization_barrier(jnp.mean(value_tensor * value_tensor, axis=-1, keepdims=True)) + NORM_EPS) * gain_vec

def rope_tables(count_of_rows, head_size):
    position = (jnp.arange(count_of_rows) % SEQ).astype(jnp.float32)
    half_size = head_size // 2
    frequency = ROPE_THETA ** (-(jnp.arange(half_size).astype(jnp.float32) * 2.0) / head_size)
    angles = position[:, None] * frequency[None, :]
    angles = jnp.concatenate([angles, angles], axis=-1)
    return (jnp.cos(angles), jnp.sin(angles))

def rotate(value_tensor, cos_table, sine_table):
    half_size = value_tensor.shape[-1] // 2
    turned = jnp.concatenate([-value_tensor[..., half_size:], value_tensor[..., :half_size]], axis=-1)
    return value_tensor * cos_table + turned * sine_table

def attend(seq_block):
    queries, rotated_keys, value_tensor = seq_block
    scores = low_back(jnp.einsum('qchd,kcd->chqk', queries, rotated_keys, precision=lax.Precision.HIGHEST)) * HEAD_DIMENSION ** (-0.5)
    places = jnp.arange(SEQ)
    allowed = places[None, :] <= places[:, None]
    scores = jnp.where(allowed, scores, -jnp.inf)
    row_max = lax.optimization_barrier(jnp.max(scores, axis=-1, keepdims=True))
    weights = jnp.exp(scores - row_max)
    weights = weights / lax.optimization_barrier(jnp.sum(weights, axis=-1, keepdims=True))
    attended = jnp.einsum('chqk,kcd->qchd', low(weights), value_tensor, precision=lax.Precision.HIGHEST)
    return low(low_back(attended))

def reference(tokens, norm1_gain, w_query, key_weight, value_weight, w_out, query_gain, key_gain, norm2_gain, w_router, w_gate, w_up, w_down, routes, out_grad):
    devices = TOKENS // TOK_DEV
    slot_count = devices * CAP
    entries = routes.reshape(devices, TOK_DEV * TOPK)
    one_hot = (entries[:, :, None] == jnp.arange(EXPERTS)[None, None, :]).astype(jnp.int32)
    slot_rank = lax.optimization_barrier(jnp.sum((jnp.cumsum(one_hot, axis=1) - one_hot) * one_hot, axis=-1))
    slot_index = jnp.arange(devices)[:, None] * CAP + slot_rank
    flat_place = (entries * slot_count + slot_index).reshape(TOKENS, TOPK).astype(jnp.int32)
    token_of = (jnp.arange(TOKENS * TOPK) // TOPK).astype(jnp.int32)
    slot_token = jnp.full((EXPERTS * slot_count,), TOKENS, jnp.int32).at[flat_place.reshape(-1)].set(token_of).reshape(EXPERTS, slot_count)
    query_groups = N_EXPERT
    heads_per_group = QUERY_HEADS // query_groups
    group_key_value = np.arange(query_groups) * heads_per_group // (QUERY_HEADS // KEY_VALUE_HEADS)

    def forward(token_f, gain_one, w_q, key_matrix, value_matrix, w_o, gain_q, gain_k, gain_two, w_r, w_g, w_u, w_d):
        count_of_rows = token_f.shape[0]
        cos_table, sine_table = rope_tables(count_of_rows, HEAD_DIMENSION)
        cos_three = cos_table[:, None, :]
        sine_three = sine_table[:, None, :]
        normed_input = low(row_norm(token_f, gain_one))
        queries = low_back(precise_product(normed_input, w_q).reshape(count_of_rows, QUERY_HEADS, HEAD_DIMENSION))
        queries = low(rotate(row_norm(queries, gain_q), cos_three, sine_three))
        rotated_keys = low_back(precise_product(normed_input, key_matrix).reshape(count_of_rows, KEY_VALUE_HEADS, HEAD_DIMENSION)[:, group_key_value])
        rotated_keys = low(rotate(row_norm(rotated_keys, gain_k), cos_three, sine_three))
        value_tensor = low(low_back(precise_product(normed_input, value_matrix).reshape(count_of_rows, KEY_VALUE_HEADS, HEAD_DIMENSION)[:, group_key_value]))
        seq_count = count_of_rows // SEQ
        attended = lax.map(jax.checkpoint(attend), (queries.reshape(seq_count, SEQ, query_groups, heads_per_group, HEAD_DIMENSION), rotated_keys.reshape(seq_count, SEQ, query_groups, HEAD_DIMENSION), value_tensor.reshape(seq_count, SEQ, query_groups, HEAD_DIMENSION)))
        branch = low_back(precise_product(attended.reshape(count_of_rows, QUERY_HEADS * HEAD_DIMENSION), w_o))
        hidden = token_f + branch
        second = low(row_norm(hidden, gain_two))
        logits = low_back(precise_product(second, w_r))
        chosen = jnp.take_along_axis(logits, routes, axis=1)
        gate_probs = jax.nn.softmax(chosen, axis=-1)
        padded = jnp.concatenate([second, jnp.zeros((1, MODEL_DIMENSION), jnp.float32)], axis=0)

        def run_expert(pieces):
            token_index, gate_w, up_w, down_w = pieces
            expert_rows = low_back(padded[token_index])
            gate_h = low_back(precise_product(expert_rows, gate_w))
            up_h = low_back(precise_product(expert_rows, up_w))
            active = low(jax.nn.silu(gate_h) * up_h)
            return low(low_back(precise_product(active, down_w)))
        returned = lax.map(jax.checkpoint(run_expert), (slot_token, w_g, w_u, w_d))
        picked = returned.reshape(EXPERTS * slot_count, MODEL_DIMENSION)[flat_place]
        mixture = jnp.einsum('tk,tkd->td', gate_probs, picked, precision=lax.Precision.HIGHEST)
        return hidden + mixture
    floats = [item.astype(jnp.float32) for item in (tokens, norm1_gain, w_query, key_weight, value_weight, w_out, query_gain, key_gain, norm2_gain, w_router, w_gate, w_up, w_down)]
    output, pull_back = jax.vjp(forward, *floats)
    gradients = pull_back(out_grad.astype(jnp.float32))
    return (output.astype(jnp.bfloat16), gradients[0], gradients[1], gradients[2], gradients[3], gradients[4], gradients[5], gradients[6], gradients[7], gradients[8], gradients[9], gradients[10], gradients[11], gradients[12])
```

```python
import jax
import jax.numpy as jnp
import numpy as np
from jax import lax
from jax.experimental import pallas as pl
from jax.experimental.pallas import tpu as pltpu
from jax.sharding import PartitionSpec as P

SEQ_LEN = 1024


NORM_EPS = 1e-06
ROPE_THETA = 1000000.0
LOG2_E = 1.4426950408889634


def whole_up(value, unit):
    return -(-value // unit) * unit


def whole_up(value, unit):
    return -(-value // unit) * unit


VMEM_LIMIT = 61 * 1024 * 1024


def flipped(index, mask):
    moved = index
    bit = 1
    while bit <= mask:
        if mask & bit:
            moved = moved + bit * (1 - 2 * ((index // bit) % 2))
        bit *= 2
    return moved


def remote(src, dst, send_sem, recv_sem, axis, target):
    return pltpu.make_async_remote_copy(
        src_ref=src,
        dst_ref=dst,
        send_sem=send_sem,
        recv_sem=recv_sem,
        device_id={axis: target},
        device_id_type=pl.DeviceIdType.MESH,
    )


def greet(line=True, plane=True, far=False):
    barrier = pltpu.get_barrier_semaphore()
    count = 0
    if line:
        size, me = lax.axis_size("dp"), lax.axis_index("dp")
        for step in range(1, size) if far else (1, size - 1):
            pl.semaphore_signal(
                barrier,
                inc=1,
                device_id={"dp": (me + step) % size},
                device_id_type=pl.DeviceIdType.MESH,
            )
            count += 1
    if plane:
        size, me = lax.axis_size("expert"), lax.axis_index("expert")
        for mask in range(1, size):
            pl.semaphore_signal(
                barrier,
                inc=1,
                device_id={"expert": flipped(me, mask)},
                device_id_type=pl.DeviceIdType.MESH,
            )
            count += 1
    pl.semaphore_wait(barrier, count)


class LineGather:
    def __init__(self, own, slot, sems):
        self.size, self.me = lax.axis_size("dp"), lax.axis_index("dp")
        self.own, self.slot, self.sems = own, slot, sems

    def copy(self, way, k, s, src, block):
        target = self.me + 1 if way == 0 else self.me - 1
        dst = self.slot(k, block)
        return remote(src, dst, self.sems.at[way, k, s], self.sems.at[2 + way, k, s], "dp", target)

    def can_send(self, way, s):
        if way == 0:
            return (self.me < self.size - 1) & (self.me - s >= 0)
        return (self.me > 0) & (self.me + s < self.size)

    def start(self, k):
        for way in range(2):

            @pl.when(self.can_send(way, 0))
            def _():
                self.copy(way, k, 0, self.own(k), self.me).start()

    def step(self, k, s):
        for way in range(2):
            block = self.me - s if way == 0 else self.me + s
            present = block >= 0 if way == 0 else block < self.size

            @pl.when(present)
            def _():
                self.copy(way, k, s - 1, self.slot(k, block), block).wait_recv()

            if s < self.size - 1:

                @pl.when(self.can_send(way, s))
                def _():
                    self.copy(way, k, s, self.slot(k, block), block).start()

    def finish(self, k):
        for s in range(self.size - 1):
            for way in range(2):

                @pl.when(self.can_send(way, s))
                def _():
                    self.copy(way, k, s, self.own(k), self.me).wait_send()

    def run(self, count, window, done):
        for k in range(min(window, count)):
            self.start(k)
        for k in range(count):
            for s in range(1, self.size):
                self.step(k, s)
            if k + window < count:
                self.start(k + window)
            done(k)
        for k in range(count):
            self.finish(k)


class LineReduce:
    def __init__(self, part, inbox, sems):
        self.size, self.me = lax.axis_size("dp"), lax.axis_index("dp")
        self.part, self.inbox, self.sems = part, inbox, sems

    def copy(self, way, k, j):
        target = self.me + 1 if way == 0 else self.me - 1
        return remote(
            self.part(k, j),
            self.inbox(way, k, j),
            self.sems.at[way, k, j],
            self.sems.at[2 + way, k, j],
            "dp",
            target,
        )

    def begin(self, k):
        last = self.size - 1
        for turn in range(last):
            for way, j, end in ((0, last - turn, 0), (1, turn, last)):

                @pl.when(self.me == end)
                def _():
                    self.copy(way, k, j).start()

    def begin_block(self, k, j):
        for way, end in ((0, 0), (1, self.size - 1)):
            if j != end:

                @pl.when(self.me == end)
                def _():
                    self.copy(way, k, j).start()

    def sweep(self, k, way):
        last = self.size - 1
        for turn in range(last):
            j = last - turn if way == 0 else turn
            inner = (self.me > 0) if way == 0 else (self.me < last)
            passing = (j > self.me) if way == 0 else (j < self.me)

            @pl.when(inner & (passing | (self.me == j)))
            def _():
                self.copy(way, k, j).wait_recv()

            @pl.when(inner & passing)
            def _():
                total = self.part(k, j)[...].astype(jnp.float32) + self.inbox(way, k, j)[
                    ...
                ].astype(jnp.float32)
                self.part(k, j)[...] = total.astype(self.part(k, j).dtype)
                self.copy(way, k, j).start()

    def near(self, k):
        @pl.when(self.me < self.size // 2)
        def _():
            self.sweep(k, 0)

        @pl.when(self.me >= self.size // 2)
        def _():
            self.sweep(k, 1)

    def far(self, k):
        @pl.when(self.me < self.size // 2)
        def _():
            self.sweep(k, 1)

        @pl.when(self.me >= self.size // 2)
        def _():
            self.sweep(k, 0)

    def result(self, k, out):
        last = self.size - 1
        out[...] = self.part(k, self.me)[...].astype(jnp.float32)

        @pl.when(self.me > 0)
        def _():
            out[...] += self.inbox(0, k, self.me)[...].astype(jnp.float32)

        @pl.when(self.me < last)
        def _():
            out[...] += self.inbox(1, k, self.me)[...].astype(jnp.float32)

    def finish(self, k):
        last = self.size - 1
        for j in range(self.size):
            for way in range(2):
                sent = (j > self.me) if way == 0 else (j < self.me)

                @pl.when(sent)
                def _():
                    self.copy(way, k, j).wait_send()


def bit_orders(size):
    bits = [1 << i for i in range(size.bit_length() - 1)]
    bits.reverse()
    half = max(1, len(bits) // 2)
    if len(bits) == 3:
        return [bits, [bits[1], bits[0], bits[2]]]
    return [bits, bits[half:] + bits[:half]]


class PlaneGather:
    def __init__(self, own, slot, sems, orders):
        self.size, self.me = lax.axis_size("expert"), lax.axis_index("expert")
        self.own, self.slot, self.sems, self.orders = own, slot, sems, orders

    def place(self, h, mask):
        return max(at for at, bit in enumerate(self.orders[h]) if mask & bit)

    def copy(self, h, mask):
        last = self.orders[h][self.place(h, mask)]
        block = flipped(self.me, mask - last)
        src = self.own(h) if mask == last else self.slot(h, block)
        return remote(
            src,
            self.slot(h, block),
            self.sems.at[0, h, mask],
            self.sems.at[1, h, mask],
            "expert",
            flipped(self.me, last),
        )

    def wait(self, h, mask):
        here = self.slot(h, flipped(self.me, mask))
        remote(
            here, here, self.sems.at[0, h, mask], self.sems.at[1, h, mask], "expert", flipped(self.me, 1)
        ).wait_recv()

    def start(self, some=None):
        for at in range(len(self.orders[0])):
            for h, order in enumerate(self.orders):
                if some is None or h in some:
                    self.copy(h, order[at]).start()

    def moves(self):
        found = [(h, mask) for h in range(len(self.orders)) for mask in range(1, self.size)]
        found.sort(key=lambda move: (move[1].bit_count(), self.place(*move), move[0]))
        return found

    def move(self, h, mask):
        self.wait(h, mask)
        for bit in self.orders[h][self.place(h, mask) + 1 :]:
            self.copy(h, mask | bit).start()

    def relay(self):
        for h, mask in self.moves():
            self.move(h, mask)

    def finish(self):
        for h in range(len(self.orders)):
            for mask in range(1, self.size):
                self.copy(h, mask).wait_send()


class PlaneReduce:
    def __init__(self, acc, inbox, sems, orders):
        self.size, self.me = lax.axis_size("expert"), lax.axis_index("expert")
        self.acc, self.inbox, self.sems, self.orders = acc, inbox, sems, orders

    def masks(self, h, at):
        later = self.orders[h][at + 1 :]
        found = [0]
        for bit in later:
            found = found + [mask | bit for mask in found]
        return sorted(found, key=lambda mask: (mask == 0, self.first(h, mask) if mask else 0))

    def first(self, h, mask):
        return min(at for at, bit in enumerate(self.orders[h]) if mask & bit)

    def number(self, h, at, mask):
        before = sum(self.size >> (step + 1) for step in range(at))
        return before + sorted(self.masks(h, at)).index(mask)

    def copy(self, h, at, mask):
        bit = self.orders[h][at]
        n = self.number(h, at, mask)
        return remote(
            self.acc(h, flipped(self.me, mask | bit)),
            self.inbox(h, n),
            self.sems.at[0, h, n],
            self.sems.at[1, h, n],
            "expert",
            flipped(self.me, bit),
        )

    def start(self, h):
        for mask in self.masks(h, 0):
            self.copy(h, 0, mask).start()

    def advance(self, h, at):
        for mask in self.masks(h, at):
            self.copy(h, at, mask).wait_recv()
            if mask:
                here = self.acc(h, flipped(self.me, mask))
                arrived = self.inbox(h, self.number(h, at, mask))
                here[...] = (
                    here[...].astype(jnp.float32) + arrived[...].astype(jnp.float32)
                ).astype(here.dtype)
                if self.first(h, mask) == at + 1:
                    self.copy(h, at + 1, mask - self.orders[h][at + 1]).start()

    def result(self, h, out):
        total = self.acc(h, self.me)[...].astype(jnp.float32)
        for at in range(len(self.orders[h])):
            total = total + self.inbox(h, self.number(h, at, 0))[...].astype(jnp.float32)
        out[...] = total

    def finish(self, h):
        for at in range(len(self.orders[h])):
            for mask in self.masks(h, at):
                self.copy(h, at, mask).wait_send()


def part_of(ref, item, rows, width):
    chunk, low, wide = item
    if wide == width:
        return ref.at[chunk, rows]
    return ref.at[chunk, rows, pl.ds(low, wide)]


def halved(chunks, width, at):
    items = []
    for c in range(chunks):
        if c == at and width >= 256:
            items += [(c, 0, width // 2), (c, width // 2, width // 2)]
        else:
            items.append((c, 0, width))
    return items


def vmem(shape, dtype):
    return pltpu.VMEM(shape, dtype)


def dma(*shape):
    return pltpu.SemaphoreType.DMA(shape)


def call(kernel, outs, scratch, number, *operands):
    whole = pl.BlockSpec(memory_space=pltpu.VMEM)
    return pl.pallas_call(
        kernel,
        out_shape=outs,
        in_specs=[whole] * len(operands),
        out_specs=jax.tree.map(lambda _: whole, outs),
        scratch_shapes=scratch,
        compiler_params=pltpu.CompilerParams(
            collective_id=number, has_side_effects=True, vmem_limit_bytes=VMEM_LIMIT
        ),
    )(*operands)


class PlaneExchange:
    def __init__(self, src, dst, sems):
        self.size, self.me = lax.axis_size("expert"), lax.axis_index("expert")
        self.src, self.dst, self.sems = src, dst, sems

    def copy(self, k, peer):
        return remote(
            self.src(k, peer),
            self.dst(k, self.me),
            self.sems.at[0, k, peer],
            self.sems.at[1, k, self.me],
            "expert",
            peer,
        )

    def peers(self):
        order = sorted(range(1, self.size), key=lambda mask: (mask == 1, -mask.bit_count()))
        return [flipped(self.me, mask) for mask in order]

    def start(self, k):
        for peer in self.peers():
            self.copy(k, peer).start()

    def keep(self, k):
        self.dst(k, self.me)[...] = self.src(k, self.me)[...]

    def wait(self, k):
        for peer in self.peers():
            here = self.dst(k, peer)
            remote(
                here, here, self.sems.at[0, k, peer], self.sems.at[1, k, peer], "expert", peer
            ).wait_recv()

    def finish(self, k):
        for peer in self.peers():
            self.copy(k, peer).wait_send()


def combine(values, select, slots, number):
    data, group = lax.axis_size("dp"), lax.axis_size("expert")
    chunks, entries, width = values.shape
    rows = select.shape[1] // data
    window = 1

    def kernel(v_ref, select, out_ref, turned, back, part, inbox, ls, es):
        greet()
        exchange = PlaneExchange(
            lambda k, p: v_ref.at[k, pl.ds(pl.multiple_of(p * slots, slots), slots)],
            lambda k, p: back.at[k, pl.ds(pl.multiple_of(p * slots, slots), slots)],
            es,
        )
        line = LineReduce(
            lambda k, j: part.at[k, pl.ds(pl.multiple_of(j * rows, rows), rows)],
            lambda way, k, j: inbox.at[k, j + 1 - way],
            ls,
        )
        for k in range(window):
            exchange.start(k)
        turned[...] = select[...].T
        for k in range(chunks):
            exchange.keep(k)
        for k in range(chunks):
            exchange.wait(k)
            if k + window < chunks:
                exchange.start(k + window)
            total = jnp.dot(
                turned[...], back[k], preferred_element_type=jnp.float32
            )
            part[k] = total.astype(jnp.bfloat16)
            line.begin(k)
            line.near(k)
            if k:
                line.far(k - 1)
        line.far(chunks - 1)
        for k in range(chunks):
            line.result(k, out_ref.at[:, pl.ds(k * width, width)])
            line.finish(k)
            exchange.finish(k)

    return call(
        kernel,
        jax.ShapeDtypeStruct((rows, chunks * width), jnp.float32),
        [
            vmem(select.shape[::-1], jnp.bfloat16),
            vmem(values.shape, jnp.bfloat16),
            vmem((chunks, data * rows, width), jnp.bfloat16),
            vmem((chunks, data + 1, rows, width), jnp.bfloat16),
            dma(4, chunks, data),
            dma(2, chunks, group),
        ],
        number,
        values,
        select,
    )


def expert_layer(
    second, pair, probs, hidden, out_grad, gain, w_router, select, grads_here,
    w_gate, w_up, w_down, cut, with_mix,
):
    data, group = lax.axis_size("dp"), lax.axis_size("expert")
    chunks, rows, width = second.shape
    model = chunks * width
    experts = w_router.shape[0]
    extra = pair.shape[1]
    entries = select.shape[0]
    slots = entries // group
    hidden_units = w_gate.shape[1]
    block = 2 * slots
    pieces = model // cut
    early = max(1, chunks // 2)
    came = halved(chunks, width, 0)
    sent = halved(chunks, width, chunks - 1)

    def kernel(
        sec_ref, pair_ref, prob_ref, hid_ref, g_ref, gain_ref, r_ref, select, gh_any, wg_any, wu_any, wd_any,
        x_any, s_any, h_any, v_any, grad_hidden, branch_any, norm_sum, router_sum, turned_any, mix_out,
        x_all, pair_all, picked_pair, pair_here, rows_out, pair_out, back, pair_back,
        inbox, pair_box, summed, pair_sum, turned, low, wg, wu, wd,
        x_here, g_stage, s_stage, v_stage, h_stage,
        mix_back, loads, g_load, stores, keeps, ls, es, ls2, es2, es3,
    ):
        place, plane = lax.axis_index("dp"), lax.axis_index("expert")
        own = place * group + plane
        pairs = group // 2
        fetches = [
            pltpu.make_async_copy(src, dst, loads.at[at])
            for at, (src, dst) in enumerate(((wg_any, wg), (wu_any, wu), (wd_any, wd)))
        ]

        def block_at(step):
            mask, at, bit = pairs - 1 - step, 0, 1
            while bit < pairs:
                at = at + bit * ((plane // (2 * bit) + mask // bit) % 2)
                bit *= 2
            return at

        def block_rows(step):
            at = block_at(step)
            return pl.ds(pl.multiple_of(at * block, block), block)

        def load_grads(step):
            slot = step % 2
            return pltpu.make_async_copy(
                gh_any.at[:, block_rows(step)], g_stage.at[slot], g_load.at[slot]
            )

        def store_block(step):
            slot, here = step % 2, block_rows(step)
            return [
                pltpu.make_async_copy(s_stage.at[slot], s_any.at[:, here], stores.at[slot, 0]),
                pltpu.make_async_copy(v_stage.at[slot], v_any.at[:, here], stores.at[slot, 1]),
                pltpu.make_async_copy(h_stage.at[slot], h_any.at[:, here], stores.at[slot, 2]),
            ]

        load_grads(0).start()
        for fetch in fetches:
            fetch.start()
        mine = pl.ds(pl.multiple_of(place * rows, rows), rows)
        for c in range(chunks):
            x_all[c, mine] = sec_ref[c]
        pair_all[mine] = pair_ref[...]
        greet()

        def slot_rows(p):
            return pl.ds(pl.multiple_of(p * slots, slots), slots)

        def token_rows(j):
            return pl.ds(pl.multiple_of(j * rows, rows), rows)

        def pick(items, full, wide):
            return lambda k, p: (
                part_of(full, items[k], slot_rows(p), width)
                if k < len(items)
                else wide.at[slot_rows(p)]
            )

        exchange = PlaneExchange(
            pick(came, rows_out, picked_pair), pick(came, x_here, pair_here), es
        )

        def done(k):
            if k == 0:
                picked_pair[...] = jnp.dot(
                    select[...], pair_all[...], preferred_element_type=jnp.float32
                ).astype(jnp.bfloat16)
                exchange.start(len(came))
                exchange.keep(len(came))
            else:
                c, at, wide = came[k - 1]
                rows_out[c, :, at : at + wide] = jnp.dot(
                    select[...], x_all[c, :, at : at + wide], preferred_element_type=jnp.float32
                ).astype(jnp.bfloat16)
                exchange.start(k - 1)
                exchange.keep(k - 1)

        line = LineGather(
            lambda k: (
                pair_ref if k == 0 else part_of(sec_ref, came[k - 1], pl.ds(0, rows), width)
            ),
            lambda k, j: (
                pair_all.at[token_rows(j)]
                if k == 0
                else part_of(x_all, came[k - 1], token_rows(j), width)
            ),
            ls,
        )
        line.run(len(came) + 1, 3, done)
        turned[...] = select[...].T
        keep_turned = pltpu.make_async_copy(turned, turned_any, keeps.at[2])
        keep_turned.start()
        for fetch in fetches:
            fetch.wait()
        for k in range(len(came) + 1):
            exchange.wait(k)
        for k in range(len(came) + 1):
            exchange.finish(k)
        keep_rows = pltpu.make_async_copy(x_here, x_any, keeps.at[0])
        keep_rows.start()

        give_back = PlaneExchange(
            pick(sent, rows_out, pair_out), pick(sent, back, pair_back), es2
        )
        lane = lax.broadcasted_iota(jnp.int32, (block, extra), 1)

        def run_block(step, carry):
            at = block_at(step)
            here = block_rows(step)
            slot = step % 2
            load_grads(step).wait()

            @pl.when(step + 1 < pairs)
            def _():
                load_grads(step + 1).start()

            @pl.when(step >= 2)
            def _():
                for store in store_block(step - 2):
                    store.wait()

            chosen = (lane == own) | (lane == own + experts)
            prob = jnp.sum(
                jnp.where(chosen, pair_here[here].astype(jnp.float32), 0.0), axis=-1, keepdims=True
            )
            gate_h = jnp.zeros((block, hidden_units), jnp.float32)
            up_h = jnp.zeros((block, hidden_units), jnp.float32)
            for c in range(chunks):
                x = x_here[c, here]
                part = pl.ds(c * width, width)
                gate_h += jnp.dot(x, wg[part], preferred_element_type=jnp.float32)
                up_h += jnp.dot(x, wu[part], preferred_element_type=jnp.float32)
            sigmoid = jax.nn.sigmoid(gate_h)
            silu = gate_h * sigmoid
            active = (silu * up_h).astype(jnp.bfloat16)
            h_stage[slot, 0] = active
            grad_active = jnp.zeros((block, hidden_units), jnp.float32)
            slot_gate = jnp.zeros((block, 1), jnp.float32)
            for c in range(chunks):
                part = pl.ds(c * width, width)
                out = jnp.dot(active, wd[:, part], preferred_element_type=jnp.float32)
                out = out.astype(jnp.bfloat16).astype(jnp.float32)
                grad = g_stage[slot, c].astype(jnp.float32)
                slot_gate += jnp.sum(out * grad, axis=-1, keepdims=True)
                v_stage[slot, c] = (prob * out).astype(jnp.bfloat16)
                grad_slot = (prob * grad).astype(jnp.bfloat16)
                s_stage[slot, c] = grad_slot
                grad_active += nt_dot(grad_slot, wd[:, part])
            grad_gate_h = grad_active * up_h * sigmoid * (1.0 + gate_h * (1.0 - sigmoid))
            grad_gate_h = grad_gate_h.astype(jnp.bfloat16)
            grad_up_h = (grad_active * silu).astype(jnp.bfloat16)
            h_stage[slot, 1] = grad_gate_h
            h_stage[slot, 2] = grad_up_h
            for store in store_block(step):
                store.start()
            top = slot_gate.astype(jnp.bfloat16).astype(jnp.float32)
            pair_out[here] = (
                jnp.where(lane == own, top, 0.0)
                + jnp.where(lane == own + experts, slot_gate - top, 0.0)
            ).astype(jnp.bfloat16)
            for c in range(chunks):
                part = pl.ds(c * width, width)
                rows_out[c, here] = (
                    nt_dot(grad_gate_h, wg[part]) + nt_dot(grad_up_h, wu[part])
                ).astype(jnp.bfloat16)
            for member in range(2):
                peer = 2 * at + member

                @pl.when(peer != plane)
                def _():
                    for k in [len(sent)] + list(range(early)):
                        give_back.copy(k, peer).start()

            return carry

        lax.fori_loop(0, pairs, run_block, 0)
        keep_rows.wait()
        for step in range(max(0, pairs - 2), pairs):
            for store in store_block(step):
                store.wait()
        mix = PlaneExchange(
            lambda k, p: v_any.at[0, slot_rows(p)], lambda k, p: mix_back.at[slot_rows(p)], es3
        )
        own_mix = pltpu.make_async_copy(
            v_any.at[0, slot_rows(plane)], mix_back.at[slot_rows(plane)], keeps.at[3]
        ) if with_mix else None
        give_back.start(early)
        for k in range(len(sent) + 1):
            give_back.keep(k)
        sums = LineReduce(
            lambda k, j: (
                part_of(x_all, sent[k], token_rows(j), width)
                if k < len(sent)
                else pair_all.at[token_rows(j)]
            ),
            lambda way, k, j: (
                inbox.at[
                    sent[k][0], j + 1 - way, :, pl.ds(sent[k][1], sent[k][2])
                ]
                if k < len(sent)
                else pair_box.at[j + 1 - way]
            ),
            ls2,
        )
        order = [len(sent)] + list(range(len(sent)))
        for at, k in enumerate(order):
            give_back.wait(k)
            if k < len(sent):
                c, low_col, wide = sent[k]
                x_all[c, :, low_col : low_col + wide] = jnp.dot(
                    turned[...],
                    back[c, :, low_col : low_col + wide],
                    preferred_element_type=jnp.float32,
                ).astype(jnp.bfloat16)
            else:
                pair_all[...] = jnp.dot(
                    turned[...], pair_back[...], preferred_element_type=jnp.float32
                ).astype(jnp.bfloat16)
            sums.begin(k)
            if k < len(sent) and early + 1 + k < len(sent):
                give_back.start(early + 1 + k)
            if at >= 1:
                sums.near(order[at - 1])
            if at >= 2:
                sums.far(order[at - 2])
        if with_mix:
            mix.start(0)
            own_mix.start()
        sums.near(order[-1])
        for k in order[-2:]:
            sums.far(k)
        for k, (c, low_col, wide) in enumerate(sent):
            sums.result(k, summed.at[:, pl.ds(c * width + low_col, wide)])
        sums.result(len(sent), pair_sum)

        gate = prob_ref[...]
        grad_gate = pair_sum[:, 0:experts] + pair_sum[:, experts : 2 * experts]
        inner = jnp.sum(gate * grad_gate, axis=-1, keepdims=True)
        grad_logits = (gate * (grad_gate - inner)).astype(jnp.bfloat16)
        for c in range(chunks):
            part = pl.ds(c * width, width)
            router_sum[:, part] = lax.dot_general(
                grad_logits,
                sec_ref[c],
                (((0,), (0,)), ((), ())),
                preferred_element_type=jnp.float32,
            )
        grad_second = summed[...] + jnp.dot(
            grad_logits, r_ref[...], preferred_element_type=jnp.float32
        )
        state = hid_ref[...]
        scale = row_scale(state)
        norm_sum[...] = jnp.sum(grad_second * state * scale, axis=0, keepdims=True)
        scaled = grad_second * gain_ref[...]
        inner = jnp.mean(scaled * state, axis=-1, keepdims=True)
        total = scale * scaled - state * (scale * scale * scale * inner)
        total = total + g_ref[...].astype(jnp.float32)
        grad_hidden[...] = total
        total = total.astype(jnp.bfloat16)
        for piece in range(pieces):
            low[piece] = total[:, piece * cut : (piece + 1) * cut]
        keep_low = pltpu.make_async_copy(low, branch_any, keeps.at[1])
        keep_low.start()
        if with_mix:
            own_mix.wait()
            mix.wait(0)
            mix_out[...] = jnp.dot(
                turned[...], mix_back[...], preferred_element_type=jnp.float32
            ).astype(jnp.bfloat16)
            mix.finish(0)
        keep_turned.wait()
        keep_low.wait()
        for k in range(len(sent) + 1):
            sums.finish(k)
            give_back.finish(k)

    bf, fl = jnp.bfloat16, jnp.float32
    whole = pl.BlockSpec(memory_space=pltpu.VMEM)
    anywhere = pl.BlockSpec(memory_space=pl.ANY)
    outs = [
        jax.ShapeDtypeStruct((chunks, entries, width), bf),
        jax.ShapeDtypeStruct((chunks, entries, width), bf),
        jax.ShapeDtypeStruct((3, entries, hidden_units), bf),
        jax.ShapeDtypeStruct((chunks, entries, width), bf),
        jax.ShapeDtypeStruct((rows, model), fl),
        jax.ShapeDtypeStruct((pieces, rows, cut), bf),
        jax.ShapeDtypeStruct((1, model), fl),
        jax.ShapeDtypeStruct((experts, model), fl),
        jax.ShapeDtypeStruct(select.shape[::-1], bf),
        jax.ShapeDtypeStruct((data * rows if with_mix else 16, width), bf),
    ]
    results = list(pl.pallas_call(
        kernel,
        out_shape=outs,
        in_specs=[whole] * 8 + [anywhere] * 4,
        out_specs=[anywhere] * 4 + [whole, anywhere, whole, whole, anywhere, whole],
        scratch_shapes=[
            vmem((chunks, data * rows, width), bf),
            vmem((data * rows, extra), bf),
            vmem((entries, extra), bf),
            vmem((entries, extra), bf),
            vmem((chunks, entries, width), bf),
            vmem((entries, extra), bf),
            vmem((chunks, entries, width), bf),
            vmem((entries, extra), bf),
            vmem((chunks, data + 1, rows, width), bf),
            vmem((data + 1, rows, extra), bf),
            vmem((rows, model), fl),
            vmem((rows, extra), fl),
            vmem(select.shape[::-1], bf),
            vmem((pieces, rows, cut), bf),
            vmem((model, hidden_units), bf),
            vmem((model, hidden_units), bf),
            vmem((hidden_units, model), bf),
            vmem((chunks, entries, width), bf),
            vmem((2, chunks, block, width), bf),
            vmem((2, chunks, block, width), bf),
            vmem((2, chunks, block, width), bf),
            vmem((2, 3, block, hidden_units), bf),
            vmem((entries if with_mix else 16, width), bf),
            dma(3),
            dma(2),
            dma(2, 3),
            dma(4),
            dma(4, len(came) + 1, data - 1),
            dma(2, len(came) + 1, group),
            dma(4, len(sent) + 1, data),
            dma(2, len(sent) + 1, group),
            dma(2, 1, group),
        ],
        compiler_params=pltpu.CompilerParams(
            collective_id=3, has_side_effects=True, vmem_limit_bytes=VMEM_LIMIT
        ),
    )(
        second, pair, probs, hidden, out_grad, gain, w_router, select, grads_here,
        w_gate, w_up, w_down,
    ))
    return results


def expert_weight_grads(arrived, grad_arrived, low_rows, others, kv):
    chunks, entries, width = arrived.shape
    hidden_units = low_rows.shape[2]
    part = kv.shape[0] // 2
    passed = len(others) + 2

    def kernel(x_ref, s_ref, low_ref, *refs):
        sources = refs[:passed]
        gate_out, up_out, down_out = refs[passed : passed + 3]
        targets = refs[passed + 3 : 2 * passed + 3]
        turned = refs[2 * passed + 3]

        @pl.when(pl.program_id(0) == 0)
        def _():
            turned[...] = low_ref[0].T

        for source, target in zip(sources, targets):
            target[...] = source[...]
        x = x_ref[0].T
        gate_out[0] = jnp.dot(x, low_ref[1], preferred_element_type=jnp.float32)
        up_out[0] = jnp.dot(x, low_ref[2], preferred_element_type=jnp.float32)
        down_out[0] = jnp.dot(turned[...], s_ref[0], preferred_element_type=jnp.float32)

    rows = pl.BlockSpec((1, entries, width), lambda c: (c, 0, 0))
    tall = pl.BlockSpec((1, width, hidden_units), lambda c: (0, c, 0))

    def slab(lines, item, first=0):
        return pl.BlockSpec((lines // chunks, item.shape[1]), lambda c: (c + first, 0))

    slabs = [slab(item.shape[0], item) for item in others]
    half = slab(part, kv)
    return pl.pallas_call(
        kernel,
        grid=(chunks,),
        out_shape=[
            jax.ShapeDtypeStruct((1, chunks * width, hidden_units), jnp.float32),
            jax.ShapeDtypeStruct((1, chunks * width, hidden_units), jnp.float32),
            jax.ShapeDtypeStruct((1, hidden_units, chunks * width), jnp.float32),
        ]
        + [jax.ShapeDtypeStruct(item.shape, item.dtype) for item in others]
        + [jax.ShapeDtypeStruct((part, kv.shape[1]), kv.dtype)] * 2,
        in_specs=[rows, rows, pl.BlockSpec((3, entries, hidden_units), lambda c: (0, 0, 0))]
        + slabs
        + [half, slab(part, kv, chunks)],
        out_specs=[tall, tall, pl.BlockSpec((1, hidden_units, width), lambda c: (0, 0, c))]
        + slabs
        + [half, half],
        scratch_shapes=[vmem((hidden_units, entries), jnp.bfloat16)],
        compiler_params=pltpu.CompilerParams(vmem_limit_bytes=VMEM_LIMIT),
    )(arrived, grad_arrived, low_rows, *others, kv, kv)


def attention_backward(
    grad_branch, out_blocks, x, w_q, w_kv, q_raw, q_low, k_raw, k_low, v_low, lse, att,
    cos, sin, gain_q, gain_k, mixed, turned, tokens, gain, grad_hidden, hidden, norm2_sum, router_sum, first_mix,
    seq_len, with_mix,
):
    data, group = lax.axis_size("dp"), lax.axis_size("expert")
    pieces, rows, cut = grad_branch.shape
    chunks, total, width = x.shape
    model = chunks * width
    depth = model // data
    wide = w_q.shape[1]
    sharing, _, both, _ = w_kv.shape
    part = both // 2
    head = sharing * part
    heads = wide // head
    block = min(256, seq_len)
    scale = head ** (-0.5)
    entries = turned.shape[1]
    slots = entries // group
    orders = [order[::-1] for order in bit_orders(group)]
    orders = [orders[at % 2] for at in range(chunks)]
    steps = len(orders[0])

    def kernel(
        gb_ref, wo_any, x_any, wq_any, wkv_any, qr_any, ql_any, kr_any, kl_any, vl_any, lse_any, att_ref,
        cos_ref, sin_ref, gq_ref, gk_ref, mix_any, turned_any, tok_ref, gain_ref, gh_any, hid_ref, n2_ref, rt_any, fm_ref,
        tok_out, wo_out, wq_out, wkv_out, gq_out, gk_out, n1_out, n2_out, rt_out, layer_out,
        wo_ref, x_ref, wq_ref, wkv_ref, ql_ref, kr_ref, kl_ref, vl_ref, lse_ref, turned,
        big, row_terms, log_rows, dq_low, dk, dv, dkv_low, kv_box, raw_buf,
        wo_part, wo_box, w_part, w_box, kv_part, kv_inbox, dx_box, back,
        mix_part, mix_box, summed, dx_sum, vec, vec_plane, vec_half, vec_line, rt_acc, rt_box, rt_half, rt_line, gq_sum, gk_sum,
        loads, raw_load, keep_s, wo_s, w_s, kv_s, sib_s, dx_s, ex_s, mix_s, vp_s, vl_s, rp_s, rl_s, rg_s, gb_s,
    ):
        place, plane = lax.axis_index("dp"), lax.axis_index("expert")
        member = plane % sharing

        def branch(j):
            first = j * cut
            return big.at[first // width, :, pl.ds(first % width, cut)]

        fetches = [
            pltpu.make_async_copy(src, dst, loads.at[at])
            for at, (src, dst) in enumerate(
                (
                    (rt_any, rt_acc),
                    (wo_any, wo_ref),
                    (ql_any, ql_ref),
                    (kl_any, kl_ref),
                    (vl_any, vl_ref),
                    (lse_any, lse_ref),
                    (x_any, x_ref),
                    (kr_any, kr_ref),
                    (wq_any, wq_ref),
                    (wkv_any, wkv_ref),
                    (gh_any, tok_out),
                )
            )
        ]
        for fetch in fetches:
            fetch.start()
        if with_mix:
            turned_load = pltpu.make_async_copy(turned_any, turned, loads.at[len(fetches)])
            turned_load.start()

        def load_raw(h):
            mine = pl.ds(pl.multiple_of(h * head, head), head)
            return pltpu.make_async_copy(qr_any.at[:, mine], raw_buf.at[h % 2], raw_load.at[h % 2])

        load_raw(0).start()

        def slot_rows(p):
            return pl.ds(pl.multiple_of(p * slots, slots), slots)

        def token_rows(j):
            return pl.ds(pl.multiple_of(j * rows, rows), rows)

        exchange = PlaneExchange(
            lambda k, p: mix_any.at[k, slot_rows(p)], lambda k, p: back.at[k, slot_rows(p)], ex_s
        )
        wo_sum = LineReduce(
            lambda k, j: wo_part.at[j, pl.ds(k * (wide // 2), wide // 2)],
            lambda way, k, j: wo_box.at[j + 1 - way, pl.ds(k * (wide // 2), wide // 2)],
            wo_s,
        )
        w_sum = LineReduce(
            lambda k, j: w_part.at[k, j], lambda way, k, j: w_box.at[k, j + 1 - way], w_s
        )
        kv_sum = LineReduce(
            lambda k, j: kv_part.at[j], lambda way, k, j: kv_inbox.at[j + 1 - way], kv_s
        )
        reduce = PlaneReduce(
            lambda h, j: big.at[h, token_rows(j)], lambda h, n: dx_box.at[h, n], dx_s, orders
        )

        mix_sum = LineReduce(
            lambda k, j: mix_part.at[k, token_rows(j)],
            lambda way, k, j: mix_box.at[k, j + 1 - way],
            mix_s,
        )
        share = model // group

        def share_cols(j):
            return pl.ds(pl.multiple_of(j * share, share), share)

        router = PlaneReduce(
            lambda h, j: rt_acc.at[:, share_cols(j)], lambda h, n: rt_box.at[n], rp_s, orders[:1]
        )
        router_back = PlaneGather(
            lambda h: rt_half.at[1],
            lambda h, j: rt_out.at[:, share_cols(j)],
            rg_s,
            bit_orders(group)[:1],
        )

        def router_line(step):
            return remote(
                rt_half.at[0], rt_line.at[step], rl_s.at[0, step], rl_s.at[1, step],
                "dp", (place + step) % data,
            )

        def router_stage(at):
            if at < steps:
                router.advance(0, at)
            elif at == steps:
                router.result(0, rt_half.at[0])
                for step in range(1, data):
                    router_line(step).start()
            elif at == steps + 1:
                total = rt_half[0]
                for step in range(1, data):
                    router_line(step).wait_recv()
                    total = total + rt_line[step]
                rt_half[1] = total
                rt_out[:, share_cols(plane)] = total
                router_back.start()
            else:
                router_back.relay()

        def vec_across(mask):
            return remote(
                vec, vec_plane.at[mask], vp_s.at[0, mask], vp_s.at[1, mask],
                "expert", flipped(plane, mask),
            )

        def vec_along(step):
            return remote(
                vec_half, vec_line.at[step], vl_s.at[0, step], vl_s.at[1, step],
                "dp", (place + step) % data,
            )

        def x_block(j):
            first = j * depth
            inner = first % width
            return x_ref[first // width, :, inner : inner + depth]

        own_rows = token_rows(plane)
        for h in range(pieces):
            branch(h)[own_rows] = gb_ref[h]
        if with_mix:
            mix_part[0] = fm_ref[...]
        greet(far=True)
        if with_mix:
            mix_sum.begin(0)
        gather = PlaneGather(
            lambda h: gb_ref.at[h],
            lambda h, j: big.at[
                (h * cut) // width, token_rows(j), pl.ds((h * cut) % width, cut)
            ],
            gb_s,
            [bit_orders(group)[at % 2] for at in range(pieces)],
        )
        pairs = [range(h, min(h + 2, pieces)) for h in range(0, pieces, 2)]
        gather.start(pairs[0])
        fetches[0].wait()
        att_turned = att_ref[...].T

        def wo_piece(j):
            wo_part[j] = jnp.dot(
                att_turned, branch(j)[...], preferred_element_type=jnp.float32
            ).astype(jnp.bfloat16)
            for k in range(2):
                wo_sum.begin_block(k, j)

        for at, pair in enumerate(pairs):
            moves = [move for move in gather.moves() if move[0] in pair]
            first = [move for move in moves if move[1].bit_count() == 1]
            for move in first:
                gather.move(*move)
            if at + 1 < len(pairs):
                gather.start(pairs[at + 1])
            for move in moves[len(first) :]:
                gather.move(*move)
            for h in pair:
                wo_piece(h)
        router.start(0)
        if with_mix:
            if chunks > 1:
                exchange.start(1)
            mix_sum.near(0)
        fetches[1].wait()

        lane = lax.broadcasted_iota(jnp.int32, (block, head), 1)

        def attended_grad(at, carry):
            here = pl.ds(pl.multiple_of(at * block, block), block)
            value = jnp.zeros((block, wide), jnp.float32)
            for j in range(pieces):
                value += nt_dot(branch(j)[here], wo_ref[j])
            low = value.astype(jnp.bfloat16)
            dq_low[here] = low
            both_rows = low.astype(jnp.float32) * att_ref[here].astype(jnp.float32)
            terms = jnp.zeros((block, head), jnp.float32)
            for h in range(heads):
                term = jnp.sum(both_rows[:, h * head : (h + 1) * head], axis=-1, keepdims=True)
                terms = jnp.where(lane == h, term, terms)
            dk[here] = terms
            return carry

        lax.fori_loop(0, total // block, attended_grad, 0)
        for at in range(2, 7):
            fetches[at].wait()
        row_terms[...] = dk[...].T
        log_rows[...] = lse_ref[...].T * LOG2_E
        dk[...] = jnp.zeros_like(dk)
        dv[...] = jnp.zeros_like(dv)
        above = lax.broadcasted_iota(
            jnp.int32, (block, block), 0
        ) <= lax.broadcasted_iota(jnp.int32, (block, block), 1)

        def turned_dot(left, right):
            return lax.dot_general(
                left, right, (((0,), (0,)), ((), ())), preferred_element_type=jnp.float32
            )

        def unrotate(value, table):
            return value * cos_ref[table] - half_turn(value) * sin_ref[table]

        def norm_back(turned_grad, raw, gain):
            factor = row_scale(raw)
            gain_term = jnp.sum(turned_grad * raw * factor, axis=0, keepdims=True)
            scaled = turned_grad * gain
            inner = jnp.mean(scaled * raw, axis=-1, keepdims=True)
            return factor * scaled - raw * (factor * factor * factor * inner), gain_term

        gq_sum[...] = jnp.zeros_like(gq_sum)
        gk_sum[...] = jnp.zeros_like(gk_sum)

        def own_mix(k):
            return pltpu.make_async_copy(
                mix_any.at[k, slot_rows(plane)], back.at[k, slot_rows(plane)], keep_s.at[k]
            )

        def gather_mix(k):
            own_mix(k).wait()
            exchange.wait(k)
            mix_part[k] = jnp.dot(
                turned[...], back[k], preferred_element_type=jnp.float32
            ).astype(jnp.bfloat16)
            mix_sum.begin(k)

        if with_mix:
            for k in range(1, chunks):
                own_mix(k).start()
            turned_load.wait()
            mix_sum.far(0)

        def head_back(h, carry):
            mine = pl.ds(pl.multiple_of(h * head, head), head)
            load_raw(h).wait()

            @pl.when(h + 1 < heads)
            def _():
                load_raw(h + 1).start()

            for seq in range(total // seq_len):
                base = seq * seq_len
                for at in range(seq_len // block):
                    here = pl.ds(base + at * block, block)
                    query = ql_ref[here, mine]
                    grad = dq_low[here, mine]
                    log_sum = log_rows[pl.ds(h, 1), here]
                    row_term = row_terms[pl.ds(h, 1), here]
                    grad_query = jnp.zeros((block, head), jnp.float32)
                    for other in range(at + 1):
                        behind = pl.ds(base + other * block, block)
                        key = kl_ref[behind]
                        probs = jnp.exp2(nt_dot(key, query) * (scale * LOG2_E) - log_sum)
                        if other == at:
                            probs = jnp.where(above, probs, 0.0)
                        grad_probs = nt_dot(vl_ref[behind], grad)
                        grad_scores = (probs * (grad_probs - row_term)).astype(jnp.bfloat16)
                        dv[behind] += jnp.dot(
                            probs.astype(jnp.bfloat16), grad, preferred_element_type=jnp.float32
                        )
                        dk[behind] += jnp.dot(
                            grad_scores, query, preferred_element_type=jnp.float32
                        )
                        grad_query += turned_dot(grad_scores, key)
                    grad_query = grad_query * scale
                    table = pl.ds(at * block, block)
                    raw_grad, gain_term = norm_back(
                        unrotate(grad_query, table), raw_buf[h % 2, here], gq_ref[...]
                    )
                    gq_sum[...] += gain_term
                    dq_low[here, mine] = raw_grad.astype(jnp.bfloat16)
            low_turned = dq_low[:, mine].T
            for j in range(data):
                w_part[h, j] = jnp.dot(
                    low_turned, x_block(j), preferred_element_type=jnp.float32
                ).astype(jnp.bfloat16)
            w_sum.begin(h)

            if with_mix:

                @pl.when(h + 2 < chunks)
                def _():
                    exchange.start(h + 2)

            if with_mix and heads > 2:

                @pl.when((h >= 2) & (h - 1 < chunks))
                def _():
                    gather_mix(h - 1)

            @pl.when(h == heads - 2)
            def _():
                wo_sum.near(0)

            @pl.when(h == heads - 1)
            def _():
                wo_sum.near(1)
                wo_sum.far(0)

            return carry

        lax.fori_loop(0, heads, head_back, 0)
        if with_mix:
            for k in range(heads + 2, chunks):
                exchange.start(k)
        for at in range(7, len(fetches)):
            fetches[at].wait()
        for at in range(total // block):
            here = pl.ds(at * block, block)
            table = pl.ds((at * block) % seq_len, block)
            raw_grad, gain_term = norm_back(
                unrotate(dk[here] * scale, table), kr_ref[here], gk_ref[...]
            )
            gk_sum[...] += gain_term
            value_grad = dv[here]
            for m in range(sharing):
                cols = slice(m * part, (m + 1) * part)
                dkv_low[m, here] = jnp.concatenate(
                    [raw_grad[:, cols], value_grad[:, cols]], axis=1
                ).astype(jnp.bfloat16)

        def swap(mask):
            other = flipped(plane, mask)
            return remote(
                dkv_low.at[other % sharing],
                kv_box.at[member],
                sib_s.at[0, mask],
                sib_s.at[1, mask],
                "expert",
                other,
            )

        for mask in range(1, sharing):
            swap(mask).start()
        gather.finish()
        for j in range(data):
            first = j * depth
            c, inner = first // width, first % width

            def input_grad(at, carry):
                here = pl.ds(pl.multiple_of(at * block, block), block)
                value = nt_dot(dq_low[here], wq_ref[pl.ds(first, depth)])
                for m in range(sharing):
                    value += jnp.dot(
                        dkv_low[m, here], wkv_ref[m, j], preferred_element_type=jnp.float32
                    )
                big[c, here, inner : inner + depth] = value.astype(jnp.bfloat16)
                return carry

            lax.fori_loop(0, total // block, input_grad, 0)
            if inner + depth == width:
                reduce.start(c)
        kv_box[member] = dkv_low[member]
        for mask in range(1, sharing):
            other = kv_box.at[flipped(plane, mask) % sharing]
            remote(
                other, other, sib_s.at[0, mask], sib_s.at[1, mask], "expert", flipped(plane, mask)
            ).wait_recv()
        kv_turned = [kv_box[m].T for m in range(sharing)]
        for j in range(data):
            block_x = x_block(j)
            value = sum(
                jnp.dot(item, block_x, preferred_element_type=jnp.float32) for item in kv_turned
            )
            kv_part[j] = value.astype(jnp.bfloat16)
        kv_sum.begin(0)
        mixed_at = min(chunks, max(1, heads - 1)) if with_mix else chunks
        for k in range(mixed_at, chunks - 1):
            gather_mix(k)
        for c in range(chunks):
            reduce.advance(c, 0)
        if with_mix and mixed_at < chunks:
            gather_mix(chunks - 1)
        wo_sum.far(1)
        w_sum.near(0)
        for at in range(1, steps):
            for c in range(chunks):
                reduce.advance(c, at)
        router_stage(0)
        for c in range(chunks):
            reduce.result(c, dx_sum.at[:, pl.ds(c * width, width)])
        state = tok_ref[...].astype(jnp.float32)
        grad_normed = dx_sum[...]
        raw_grad, gain_term = norm_back(grad_normed, state, gain_ref[...])
        tok_out[...] += raw_grad
        vec[...] = jnp.zeros_like(vec)
        for c in range(chunks):
            cols = slice(c * width, (c + 1) * width)
            vec[c : c + 1, 0:width] = gain_term[:, cols]
            vec[chunks + c : chunks + c + 1, 0:width] = n2_ref[:, cols]
        vec[0:1, width : width + head] = gq_sum[...]
        vec[1:2, width : width + head] = gk_sum[...]
        for mask in range(1, group):
            vec_across(mask).start()
        sweeps = [(w_sum, h) for h in range(heads)] + [(kv_sum, 0)]
        if with_mix:
            for k in range(1, chunks):
                place_at = heads - mixed_at + 2 * k
                sweeps.insert(place_at if k < mixed_at else len(sweeps), (mix_sum, k))
        for at, (line, k) in enumerate(sweeps):
            if at:
                line.near(k)
                sweeps[at - 1][0].far(sweeps[at - 1][1])
                if at < steps + 3:
                    router_stage(at)
        sweeps[-1][0].far(sweeps[-1][1])
        for stage in range(max(1, min(len(sweeps), steps + 3)), steps + 3):
            router_stage(stage)
        all_sum = vec[...]
        for mask in range(1, group):
            vec_across(mask).wait_recv()
            all_sum = all_sum + vec_plane[mask]
        vec_half[...] = all_sum
        for step in range(1, data):
            vec_along(step).start()
        for k in range(2):
            wo_sum.result(k, wo_out.at[pl.ds(k * (wide // 2), wide // 2)])
        for h in range(heads):
            w_sum.result(h, summed)
            wq_out[:, h * head : (h + 1) * head] = summed[...].T
        kv_sum.result(0, wkv_out)
        if with_mix:
            for k in range(chunks):
                mix_sum.result(k, dx_sum.at[:, pl.ds(k * width, width)])
            layer_out[...] = (hid_ref[...] + dx_sum[...]).astype(jnp.bfloat16)
        for step in range(1, data):
            vec_along(step).wait_recv()
            all_sum = all_sum + vec_line[step]
        for c in range(chunks):
            cols = pl.ds(c * width, width)
            n1_out[:, cols] = all_sum[c : c + 1, 0:width]
            n2_out[:, cols] = all_sum[chunks + c : chunks + c + 1, 0:width]
        gq_out[...] = all_sum[0:1, width : width + head]
        gk_out[...] = all_sum[1:2, width : width + head]
        for mask in range(1, group):
            vec_across(mask).wait_send()
        for step in range(1, data):
            vec_along(step).wait_send()
            router_line(step).wait_send()
        router.finish(0)
        router_back.finish()
        for k in range(2):
            wo_sum.finish(k)
        for h in range(heads):
            w_sum.finish(h)
        kv_sum.finish(0)
        for mask in range(1, sharing):
            swap(mask).wait_send()
        for c in range(chunks):
            reduce.finish(c)
        if with_mix:
            for k in range(chunks):
                mix_sum.finish(k)
                if k:
                    exchange.finish(k)

    bf, fl = jnp.bfloat16, jnp.float32
    whole = pl.BlockSpec(memory_space=pltpu.VMEM)
    anywhere = pl.BlockSpec(memory_space=pl.ANY)
    mix_entries = entries if with_mix else 16
    mix_rows = rows if with_mix else 16
    mix_all = data * rows if with_mix else 16
    experts = router_sum.shape[0]
    share = model // group
    lines = whole_up(2 * chunks, 8)
    outs = [
        jax.ShapeDtypeStruct((rows, model), fl),
        jax.ShapeDtypeStruct((wide, cut), fl),
        jax.ShapeDtypeStruct((depth, wide), fl),
        jax.ShapeDtypeStruct((both, depth), fl),
        jax.ShapeDtypeStruct((1, head), fl),
        jax.ShapeDtypeStruct((1, head), fl),
        jax.ShapeDtypeStruct((1, model), fl),
        jax.ShapeDtypeStruct((1, model), fl),
        jax.ShapeDtypeStruct((experts, model), fl),
        jax.ShapeDtypeStruct((mix_rows, model), bf),
    ]
    return pl.pallas_call(
        kernel,
        out_shape=outs,
        in_specs=[whole]
        + [anywhere] * 10
        + [whole] * 5
        + [anywhere] * 2
        + [whole] * 2
        + [anywhere, whole if with_mix else anywhere, whole, anywhere]
        + [whole if with_mix else anywhere],
        out_specs=[whole] * len(outs),
        scratch_shapes=[
            vmem(out_blocks.shape, bf),
            vmem(x.shape, bf),
            vmem(w_q.shape, bf),
            vmem(w_kv.shape, bf),
            vmem(q_low.shape, bf),
            vmem(k_raw.shape, fl),
            vmem(k_low.shape, bf),
            vmem(v_low.shape, bf),
            vmem(lse.shape, fl),
            vmem(turned.shape if with_mix else (16, 128), bf),
            vmem((chunks, total, width), bf),
            vmem((head, total), fl),
            vmem((head, total), fl),
            vmem((total, wide), bf),
            vmem((total, head), fl),
            vmem((total, head), fl),
            vmem((sharing, total, both), bf),
            vmem((sharing, total, both), bf),
            vmem((2, total, head), fl),
            vmem((data, wide, cut), bf),
            vmem((data + 1, wide, cut), bf),
            vmem((heads, data, head, depth), bf),
            vmem((heads, data + 1, head, depth), bf),
            vmem((data, both, depth), bf),
            vmem((data + 1, both, depth), bf),
            vmem((chunks, group - 1, rows, width), bf),
            vmem((chunks, mix_entries, width), bf),
            vmem((chunks, mix_all, width), bf),
            vmem((chunks, data + 1, mix_rows, width), bf),
            vmem((head, depth), fl),
            vmem((rows, model), fl),
            vmem((lines, width + head), fl),
            vmem((group, lines, width + head), fl),
            vmem((lines, width + head), fl),
            vmem((data, lines, width + head), fl),
            vmem((experts, model), fl),
            vmem((group - 1, experts, share), fl),
            vmem((2, experts, share), fl),
            vmem((data, experts, share), fl),
            vmem((1, head), fl),
            vmem((1, head), fl),
            dma(12),
            dma(2),
            dma(chunks),
            dma(4, 2, data),
            dma(4, heads, data),
            dma(4, 1, data),
            dma(2, sharing),
            dma(2, chunks, group - 1),
            dma(2, chunks, group),
            dma(4, chunks, data),
            dma(2, group),
            dma(2, data),
            dma(2, 1, group - 1),
            dma(2, data),
            dma(2, 1, group),
            dma(2, pieces, group),
        ],
        compiler_params=pltpu.CompilerParams(
            collective_id=7, has_side_effects=True, vmem_limit_bytes=VMEM_LIMIT
        ),
    )(
        grad_branch, out_blocks, x, w_q, w_kv, q_raw, q_low, k_raw, k_low, v_low, lse, att,
        cos, sin, gain_q, gain_k, mixed, turned, tokens, gain, grad_hidden, hidden, norm2_sum, router_sum, first_mix,
    )


def rope_arrays(seq_len, head_dim):
    half = head_dim // 2
    frequency = ROPE_THETA ** (-(np.arange(half) * 2.0) / head_dim)
    angles = np.arange(seq_len)[:, None] * frequency[None, :]
    cos = np.concatenate([np.cos(angles), np.cos(angles)], axis=1).astype(np.float32)
    sin = np.concatenate([-np.sin(angles), np.sin(angles)], axis=1).astype(np.float32)
    return cos, sin


def row_scale(value):
    return lax.rsqrt(jnp.mean(value * value, axis=-1, keepdims=True) + NORM_EPS)


def half_turn(value):
    return pltpu.roll(value, value.shape[-1] // 2, value.ndim - 1)


def nt_dot(left, right):
    return lax.dot_general(
        left, right, (((1,), (1,)), ((), ())), preferred_element_type=jnp.float32
    )


def causal(start, rows, keys):
    at_row = lax.broadcasted_iota(jnp.int32, (rows, keys), 0) + start
    return lax.broadcasted_iota(jnp.int32, (rows, keys), 1) <= at_row


class Always:
    def __init__(self, order):
        self.order = order

    def __getitem__(self, at):
        return self.order


def front(
    tokens, gain, w_q, w_k, w_v, w_out, out_grad, slot_rows, cos, sin, gain_q, gain_k,
    gain2, router, hot, capacity, slots, seq_len,
):
    data, group = lax.axis_size("dp"), lax.axis_size("expert")
    rows, model = tokens.shape
    width = min(512, model)
    chunks = model // width
    depth, wide = w_q.shape
    cut = w_out.shape[1]
    part = w_k.shape[0]
    both = 2 * part
    head = gain_q.shape[1]
    sharing = head // part
    heads = wide // head
    total = group * rows
    block = min(256, seq_len)
    scale = head ** (-0.5)
    experts = router.shape[0]
    extra = whole_up(2 * experts, 128)
    entries = group * slots
    x_orders = bit_orders(group)
    x_orders = [x_orders[at % 2] for at in range(chunks)]
    b_orders = [Always(order[::-1]) for order in bit_orders(group)]
    steps = len(b_orders[0][0])
    halves = 2
    deep = depth // halves
    first_grad = 2 + halves
    first_out = first_grad + chunks - 1
    first_last = first_out + 1
    last = [item for item in halved(chunks, width, chunks - 1) if item[0] == chunks - 1]
    items = first_last + len(last)

    def kernel(
        tok_ref, gain_ref, wq_ref, wk_ref, wv_ref, wo_ref, og_ref, s_ref, cos_ref, sin_ref, gq_ref, gk_ref,
        gain2_ref, r_ref, hot_ref,
        x_any, wq_any, wkv_any, wo_any, g_any, sel_any, qr_any, ql_any, kr_any, kl_any, vl_any, lse_any,
        att_any, hidden, second, pair, probs,
        x_own, g_own, kv_own, x_all, wq_all, wkv_all, wo_all, g_all, s_all, picked, g_here, select,
        q_raw, q_low, k_raw, k_low, v_low, lse, att, acc, inbox,
        ps, ls, es, ks, bs, outs,
    ):
        place, plane = lax.axis_index("dp"), lax.axis_index("expert")
        member = plane % sharing
        state = tok_ref[...].astype(jnp.float32)
        normed = (state * row_scale(state) * gain_ref[...]).astype(jnp.bfloat16)
        mine = pl.ds(pl.multiple_of(place * rows, rows), rows)
        own_rows = pl.ds(pl.multiple_of(plane * rows, rows), rows)
        for c in range(chunks):
            x_own[c] = normed[:, c * width : (c + 1) * width]
            x_all[c, own_rows] = x_own[c]
            g_own[c] = og_ref[:, c * width : (c + 1) * width]
            g_all[c, mine] = g_own[c]
        kv_own[0:part] = wk_ref[...]
        kv_own[part:both] = wv_ref[...]
        wq_all[place] = wq_ref[...]
        wkv_all[member, place] = kv_own[...]
        wo_all[place] = wo_ref[...]
        s_all[place] = s_ref[...]
        greet()

        def token_rows(j):
            return pl.ds(pl.multiple_of(j * rows, rows), rows)

        def slot_rows_of(p):
            return pl.ds(pl.multiple_of(p * slots, slots), slots)

        gather = PlaneGather(
            lambda h: x_own.at[h], lambda h, j: x_all.at[h, token_rows(j)], ps, x_orders
        )

        def is_grad(k):
            return not isinstance(k, int) or first_grad <= k < first_out

        def own(k):
            if is_grad(k):
                return g_own.at[k - first_grad]
            if k == 0:
                return s_ref
            if k == 1:
                return kv_own
            if k < first_grad:
                return wq_ref.at[pl.ds((k - 2) * deep, deep)]
            if k >= first_last:
                return part_of(g_own, last[k - first_last], pl.ds(0, rows), width)
            return wo_ref

        def slot(k, j):
            if is_grad(k):
                return g_all.at[k - first_grad, token_rows(j)]
            if k == 0:
                return s_all.at[j]
            if k == 1:
                return wkv_all.at[member, j]
            if k < first_grad:
                return wq_all.at[j, pl.ds((k - 2) * deep, deep)]
            if k >= first_last:
                return part_of(g_all, last[k - first_last], token_rows(j), width)
            return wo_all.at[j]

        line = LineGather(own, slot, ls)
        def exchanged(ref):
            return lambda k, p: (
                part_of(ref, last[k - chunks + 1], slot_rows_of(p), width)
                if isinstance(k, int) and k >= chunks - 1
                else ref.at[k, slot_rows_of(p)]
            )

        exchange = PlaneExchange(exchanged(picked), exchanged(g_here), es)
        turns_of_grads = chunks - 1 + len(last)
        reduces = [
            PlaneReduce(lambda h, j: acc.at[h, j], lambda h, n: inbox.at[h, n], bs, order)
            for order in b_orders
        ]
        keeps = {}

        def keep(name, src, dst):
            keeps[name] = pltpu.make_async_copy(src, dst, outs.at[len(keeps)])
            keeps[name].start()

        def share(mask):
            return remote(
                wkv_all.at[member], wkv_all.at[member], ks.at[0, mask], ks.at[1, mask],
                "expert", flipped(plane, mask),
            )

        gather.start()
        for k in range(first_grad):
            line.start(k)
        moves = gather.moves()
        for s in range(1, data):
            line.step(0, s)
        wanted = lax.broadcasted_iota(jnp.int32, (slots, rows), 0).astype(jnp.float32)
        for j in range(data):
            for peer in range(group):
                row = s_all[j, pl.ds(pl.multiple_of(place * group, 8), group)][peer : peer + 1]
                row = jnp.where(row >= 0, row + j * capacity, -1.0)
                select[pl.ds(peer * slots, slots), pl.ds(j * rows, rows)] = jnp.where(
                    wanted == row, 1.0, 0.0
                ).astype(jnp.bfloat16)
        for k in range(first_grad, min(first_grad + 2, first_out)):
            line.start(k)
        taken = 0
        turns = [(k, s) for k in range(1, first_grad) for s in range(1, data)]
        for at, (k, s) in enumerate(turns):
            until = len(moves) * (at + 1) // len(turns)
            for move in moves[taken:until]:
                gather.move(*move)
            taken = until
            line.step(k, s)
            if k == 1 and s == data - 1:
                for mask in range(1, sharing):
                    share(mask).start()
        for k in range(first_grad + 2, first_out):
            line.start(k)
        for mask in range(1, sharing):
            other = wkv_all.at[flipped(plane, mask) % sharing]
            remote(
                other, other, ks.at[0, mask], ks.at[1, mask], "expert", flipped(plane, mask)
            ).wait_recv()
        keep("select", select, sel_any)
        keep("x", x_all, x_any)
        keep("wq", wq_all, wq_any)
        keep("wkv", wkv_all, wkv_any)

        def x_block(rows_here, j):
            first = j * depth
            inner = first % width
            return x_all[first // width, rows_here, inner : inner + depth]

        def project(at, carry):
            here = pl.ds(pl.multiple_of(at * block, block), block)
            table = pl.ds(pl.multiple_of((at * block) % seq_len, block), block)
            cos_here, sin_here = cos_ref[table], sin_ref[table]
            blocks = [x_block(here, j) for j in range(data)]
            raw = sum(
                jnp.dot(blocks[j], wq_all[j], preferred_element_type=jnp.float32)
                for j in range(data)
            )
            q_raw[here] = raw
            for h in range(heads):
                one = raw[:, h * head : (h + 1) * head]
                one = one * row_scale(one) * gq_ref[...]
                turned = one * cos_here + half_turn(one) * sin_here
                q_low[here, h * head : (h + 1) * head] = turned.astype(jnp.bfloat16)
            kv = [sum(nt_dot(blocks[j], wkv_all[m, j]) for j in range(data)) for m in range(sharing)]
            raw = jnp.concatenate([item[:, :part] for item in kv], axis=1)
            k_raw[here] = raw
            one = raw * row_scale(raw) * gk_ref[...]
            k_low[here] = (one * cos_here + half_turn(one) * sin_here).astype(jnp.bfloat16)
            v_low[here] = jnp.concatenate([item[:, part:] for item in kv], axis=1).astype(
                jnp.bfloat16
            )
            return carry

        lax.fori_loop(0, total // block, project, 0)
        keep("q_raw", q_raw, qr_any)
        keep("q_low", q_low, ql_any)
        keep("k_raw", k_raw, kr_any)
        keep("k_low", k_low, kl_any)
        keep("v_low", v_low, vl_any)
        lane = lax.broadcasted_iota(jnp.int32, (block, head), 1)
        below = causal(0, block, block)
        lse[...] = jnp.zeros_like(lse)

        def send_grads(c):
            picked[c] = jnp.dot(
                select[...], g_all[c], preferred_element_type=jnp.float32
            ).astype(jnp.bfloat16)
            exchange.start(c)
            exchange.keep(c)

        def attend(h, carry):
            cols = pl.ds(pl.multiple_of(h * head, head), head)
            count = 0
            for seq in range(total // seq_len):
                base = seq * seq_len
                for at in range(seq_len // block):
                    here = pl.ds(base + at * block, block)
                    query = q_low[here, cols]
                    tiles = []
                    if at:
                        tiles.append(pl.ds(base, at * block))
                    tiles.append(here)
                    scores = [nt_dot(query, k_low[tile]) for tile in tiles]
                    scores[-1] = jnp.where(below, scores[-1], -jnp.inf)
                    top = jnp.max(scores[-1], axis=-1, keepdims=True)
                    if at:
                        top = jnp.maximum(top, jnp.max(scores[0], axis=-1, keepdims=True))
                    raised = [jnp.exp2((score - top) * (scale * LOG2_E)) for score in scores]
                    norm = sum(jnp.sum(item, axis=-1, keepdims=True) for item in raised)
                    inverse = 1.0 / norm
                    att[here, cols] = sum(
                        jnp.dot(
                            (item * inverse).astype(jnp.bfloat16),
                            v_low[tile],
                            preferred_element_type=jnp.float32,
                        )
                        for item, tile in zip(raised, tiles)
                    ).astype(jnp.bfloat16)
                    lse[here] = jnp.where(lane == h, top * scale + jnp.log(norm), lse[here])
                    count += 1
                    if count < data:

                        @pl.when(h < chunks - 1)
                        def _():
                            line.step(first_grad + h, count)

            @pl.when(h < chunks - 1)
            def _():
                for s in range(count + 1, data):
                    line.step(first_grad + h, s)
                send_grads(h)

            @pl.when(h == 0)
            def _():
                line.start(first_out)

            return carry

        lax.fori_loop(0, heads, attend, 0)
        keep("lse", lse, lse_any)
        keep("att", att, att_any)
        for c in range(heads, chunks - 1):
            for s in range(1, data):
                line.step(first_grad + c, s)
            send_grads(c)
        for k in range(first_last, items):
            line.start(k)

        def send_last(n):
            c, at, wide = last[n]
            picked[c, :, at : at + wide] = jnp.dot(
                select[...], g_all[c, :, at : at + wide], preferred_element_type=jnp.float32
            ).astype(jnp.bfloat16)
            exchange.start(chunks - 1 + n)
            exchange.keep(chunks - 1 + n)

        tail = []
        for n in range(len(last)):
            tail += [(n, s) for s in range(1, data)]

        def arrivals(s):
            if s == 0:
                return [(place, place >= 0, reduces[0])]
            return [
                (place - s, place >= s, reduces[(s + 1) % 2]),
                (place + s, place + s < data, reduces[s % 2]),
            ]

        def each(s, act):
            for j, present, reduce in arrivals(s):

                @pl.when(present)
                def _():
                    act(j, reduce)

        def project_out(j, reduce):
            acc[j] = (
                jnp.dot(att[...], wo_all[j], preferred_element_type=jnp.float32)
                .astype(jnp.bfloat16)
                .reshape(group, rows, cut)
            )
            reduce.start(j)

        for turn in range(data + steps):
            if turn < data:
                if turn:
                    line.step(first_out, turn)
                each(turn, project_out)
            for at in range(steps):
                if 0 <= turn - 1 - at < data:
                    each(turn - 1 - at, lambda j, reduce: reduce.advance(j, at))
            if turn >= data - 1:
                count = -(-len(tail) // (data + steps - turn))
                for n, s in tail[:count]:
                    line.step(first_last + n, s)
                    if s == data - 1:
                        send_last(n)
                tail = tail[count:]
        keep("wo", wo_all, wo_any)

        def branch_piece(j, reduce):
            reduce.result(j, hidden.at[:, pl.ds(pl.multiple_of(j * cut, cut), cut)])

        for s in range(data):
            each(s, branch_piece)
        summed = hidden[...] + tok_ref[...].astype(jnp.float32)
        hidden[...] = summed
        low = (summed * row_scale(summed) * gain2_ref[...]).astype(jnp.bfloat16)
        for c in range(chunks):
            second[c] = low[:, c * width : (c + 1) * width]
        logits = nt_dot(low, r_ref[...])
        masked = jnp.where(hot_ref[...] > 0, logits, -jnp.inf)
        raised = jnp.exp(masked - jnp.max(masked, axis=-1, keepdims=True))
        gate = raised / jnp.sum(raised, axis=-1, keepdims=True)
        probs[...] = gate
        top = gate.astype(jnp.bfloat16).astype(jnp.float32)
        parts = [top, gate - top]
        if extra > 2 * experts:
            parts.append(jnp.zeros((rows, extra - 2 * experts), jnp.float32))
        pair[...] = jnp.concatenate(parts, axis=1).astype(jnp.bfloat16)
        for k in range(turns_of_grads):
            exchange.wait(k)
        keep("g", g_here, g_any)
        for k in range(items):
            line.finish(k)
        gather.finish()
        for mask in range(1, sharing):
            share(mask).wait_send()
        for k in range(turns_of_grads):
            exchange.finish(k)
        for s in range(data):
            each(s, lambda j, reduce: reduce.finish(j))
        for copy in keeps.values():
            copy.wait()

    bf, fl = jnp.bfloat16, jnp.float32
    whole = pl.BlockSpec(memory_space=pltpu.VMEM)
    anywhere = pl.BlockSpec(memory_space=pl.ANY)

    def shape(*dims, dtype=bf):
        return jax.ShapeDtypeStruct(dims, dtype)

    kept = [
        shape(chunks, total, width),
        shape(data, depth, wide),
        shape(sharing, data, both, depth),
        shape(data, wide, cut),
        shape(chunks, entries, width),
        shape(entries, data * rows),
        shape(total, wide, dtype=fl),
        shape(total, wide),
        shape(total, head, dtype=fl),
        shape(total, head),
        shape(total, head),
        shape(total, head, dtype=fl),
        shape(total, wide),
    ]
    small = [
        shape(rows, model, dtype=fl),
        shape(chunks, rows, width),
        shape(rows, extra),
        shape(rows, experts, dtype=fl),
    ]
    return pl.pallas_call(
        kernel,
        out_shape=kept + small,
        in_specs=[whole] * 15,
        out_specs=[anywhere] * len(kept) + [whole] * len(small),
        scratch_shapes=[
            vmem((chunks, rows, width), bf),
            vmem((chunks, rows, width), bf),
            vmem((both, depth), bf),
            vmem((chunks, total, width), bf),
            vmem((data, depth, wide), bf),
            vmem((sharing, data, both, depth), bf),
            vmem((data, wide, cut), bf),
            vmem((chunks, data * rows, width), bf),
            vmem((data, experts, rows), fl),
            vmem((chunks, entries, width), bf),
            vmem((chunks, entries, width), bf),
            vmem((entries, data * rows), bf),
            vmem((total, wide), fl),
            vmem((total, wide), bf),
            vmem((total, head), fl),
            vmem((total, head), bf),
            vmem((total, head), bf),
            vmem((total, head), fl),
            vmem((total, wide), bf),
            vmem((data, group, rows, cut), bf),
            vmem((data, group - 1, rows, cut), bf),
            dma(2, chunks, group),
            dma(4, items, data - 1),
            dma(2, chunks - 1 + len(last), group),
            dma(2, sharing),
            dma(2, data, group - 1),
            dma(len(kept)),
        ],
        compiler_params=pltpu.CompilerParams(
            collective_id=1, has_side_effects=True, vmem_limit_bytes=VMEM_LIMIT
        ),
    )(
        tokens, gain, w_q, w_k, w_v, w_out, out_grad, slot_rows, cos, sin, gain_q, gain_k,
        gain2, router, hot,
    )


def local(
    tokens,
    norm1_gain,
    w_query,
    key_weight,
    value_weight,
    w_out,
    query_gain,
    key_gain,
    norm2_gain,
    w_router,
    w_gate,
    w_up,
    w_down,
    routes,
    out_grad,
):
    data_count = lax.axis_size("dp")
    group_count = lax.axis_size("expert")
    group_index = lax.axis_index("expert")
    local_rows = tokens.shape[0]
    model_width = tokens.shape[1]
    head_dim = query_gain.shape[0]
    heads_here = w_query.shape[1] // head_dim
    top_count = routes.shape[1]
    expert_total = data_count * group_count
    capacity = max(2, (local_rows * top_count * 9 + 8 * expert_total - 1) // (8 * expert_total))
    data_index = lax.axis_index("dp")
    own_expert = data_index * group_count + group_index
    expert_ids = jnp.arange(expert_total)
    hot = jnp.any(routes[:, :, None] == expert_ids[None, None, :], axis=1)
    earlier = (jnp.arange(local_rows)[:, None] > jnp.arange(local_rows)[None, :]).astype(jnp.bfloat16)
    rank = jnp.dot(earlier, hot.astype(jnp.bfloat16), preferred_element_type=jnp.float32)
    slot_rows = jnp.where(hot, rank, -1.0).T
    slots = whole_up(data_count * capacity, 16)
    width_k = key_weight.shape[1]
    all_rows = group_count * local_rows
    seq_len = min(SEQ_LEN, all_rows)
    router = w_router.T
    cos_rows, sine_rows = [jnp.asarray(table) for table in rope_arrays(seq_len, head_dim)]
    (
        gathered, q_blocks, kv_blocks, out_blocks, grads_here, select, query_raw, queries, key_raw,
        keys_low, values_low, log_sum, attended, hidden, second, pair, gate_probs,
    ) = front(
        tokens, norm1_gain[None], w_query, key_weight.T, value_weight.T, w_out, out_grad, slot_rows,
        cos_rows, sine_rows, query_gain[None], key_gain[None], norm2_gain[None], router,
        hot.astype(jnp.float32), capacity, slots, seq_len,
    )
    q_cols = q_blocks.reshape(model_width, -1)
    with_mix = all_rows <= group_count * slots
    (
        arrived, grad_arrived, low_rows, mixed, grad_hidden, grad_branch, grad_norm2, grad_router,
        turned, first_mix,
    ) = expert_layer(
        second, pair, gate_probs, hidden, out_grad, norm2_gain[None], router, select, grads_here,
        w_gate[0], w_up[0], w_down[0], out_blocks.shape[2], with_mix,
    )
    (
        grad_tokens, grad_wo, grad_wq, grad_wkv, grad_query_gain, grad_key_gain, grad_norm1,
        grad_norm2, grad_router, output,
    ) = attention_backward(
        grad_branch, out_blocks, gathered, q_cols, kv_blocks, query_raw, queries, key_raw, keys_low,
        values_low, log_sum, attended, cos_rows, sine_rows, query_gain[None], key_gain[None],
        mixed, turned, tokens, norm1_gain[None], grad_hidden, hidden, grad_norm2, grad_router, first_mix,
        seq_len, with_mix,
    )
    if not with_mix:
        output = (hidden + combine(mixed, select, slots, 5)).astype(jnp.bfloat16)
    (
        grad_gate_w, grad_up_w, grad_down, output, grad_tokens, grad_wq, grad_wo, grad_router,
        grad_wk, grad_wv,
    ) = expert_weight_grads(
        arrived, grad_arrived, low_rows, [output, grad_tokens, grad_wq, grad_wo, grad_router],
        grad_wkv,
    )
    return (
        output,
        grad_tokens,
        grad_norm1[0],
        grad_wq,
        grad_wk.T,
        grad_wv.T,
        grad_wo,
        grad_query_gain[0],
        grad_key_gain[0],
        grad_norm2[0],
        grad_router.T,
        grad_gate_w,
        grad_up_w,
        grad_down,
    )


def solution(mesh):
    placed = (
        P(("dp", "expert"), None),
        P(),
        P("dp", "expert"),
        P("dp", "expert"),
        P("dp", "expert"),
        P("expert", "dp"),
        P(),
        P(),
        P(),
        P(),
        P(("dp", "expert"), None, None),
        P(("dp", "expert"), None, None),
        P(("dp", "expert"), None, None),
        P(("dp", "expert"), None),
        P(("dp", "expert"), None),
    )
    return jax.shard_map(
        local,
        mesh=mesh,
        in_specs=placed,
        out_specs=(
            P(("dp", "expert"), None),
            P(("dp", "expert"), None),
            P(),
            P("dp", "expert"),
            P("dp", "expert"),
            P("dp", "expert"),
            P("expert", "dp"),
            P(),
            P(),
            P(),
            P(),
            P(("dp", "expert"), None, None),
            P(("dp", "expert"), None, None),
            P(("dp", "expert"), None, None),
        ),
        check_vma=False,
    )
```

```python
import jax
import jax.numpy as jnp
import numpy as np
from jax import lax
from jax.experimental import pallas as pl
from jax.experimental.pallas import tpu as pltpu
from jax.sharding import PartitionSpec as P

SEQ_LEN = 1024


NORM_EPS = 1e-06
ROPE_THETA = 1000000.0
LOG2_E = 1.4426950408889634


def whole_up(value, unit):
    return -(-value // unit) * unit


def whole_up(value, unit):
    return -(-value // unit) * unit


VMEM_LIMIT = 61 * 1024 * 1024


def flipped(index, mask):
    moved = index
    bit = 1
    while bit <= mask:
        if mask & bit:
            moved = moved + bit * (1 - 2 * ((index // bit) % 2))
        bit *= 2
    return moved


def remote(src, dst, send_sem, recv_sem, axis, target):
    return pltpu.make_async_remote_copy(
        src_ref=src,
        dst_ref=dst,
        send_sem=send_sem,
        recv_sem=recv_sem,
        device_id={axis: target},
        device_id_type=pl.DeviceIdType.MESH,
    )


def greet(line=True, plane=True, far=False):
    barrier = pltpu.get_barrier_semaphore()
    count = 0
    if line:
        size, me = lax.axis_size("dp"), lax.axis_index("dp")
        for step in range(1, size) if far else (1, size - 1):
            pl.semaphore_signal(
                barrier,
                inc=1,
                device_id={"dp": (me + step) % size},
                device_id_type=pl.DeviceIdType.MESH,
            )
            count += 1
    if plane:
        size, me = lax.axis_size("expert"), lax.axis_index("expert")
        for mask in range(1, size):
            pl.semaphore_signal(
                barrier,
                inc=1,
                device_id={"expert": flipped(me, mask)},
                device_id_type=pl.DeviceIdType.MESH,
            )
            count += 1
    pl.semaphore_wait(barrier, count)


class LineGather:
    def __init__(self, own, slot, sems):
        self.size, self.me = lax.axis_size("dp"), lax.axis_index("dp")
        self.own, self.slot, self.sems = own, slot, sems

    def copy(self, way, k, s, src, block):
        target = self.me + 1 if way == 0 else self.me - 1
        dst = self.slot(k, block)
        return remote(src, dst, self.sems.at[way, k, s], self.sems.at[2 + way, k, s], "dp", target)

    def can_send(self, way, s):
        if way == 0:
            return (self.me < self.size - 1) & (self.me - s >= 0)
        return (self.me > 0) & (self.me + s < self.size)

    def start(self, k):
        for way in range(2):

            @pl.when(self.can_send(way, 0))
            def _():
                self.copy(way, k, 0, self.own(k), self.me).start()

    def step(self, k, s):
        for way in range(2):
            block = self.me - s if way == 0 else self.me + s
            present = block >= 0 if way == 0 else block < self.size

            @pl.when(present)
            def _():
                self.copy(way, k, s - 1, self.slot(k, block), block).wait_recv()

            if s < self.size - 1:

                @pl.when(self.can_send(way, s))
                def _():
                    self.copy(way, k, s, self.slot(k, block), block).start()

    def finish(self, k):
        for s in range(self.size - 1):
            for way in range(2):

                @pl.when(self.can_send(way, s))
                def _():
                    self.copy(way, k, s, self.own(k), self.me).wait_send()

    def run(self, count, window, done):
        for k in range(min(window, count)):
            self.start(k)
        for k in range(count):
            for s in range(1, self.size):
                self.step(k, s)
            if k + window < count:
                self.start(k + window)
            done(k)
        for k in range(count):
            self.finish(k)


class LineReduce:
    def __init__(self, part, inbox, sems):
        self.size, self.me = lax.axis_size("dp"), lax.axis_index("dp")
        self.part, self.inbox, self.sems = part, inbox, sems

    def copy(self, way, k, j):
        target = self.me + 1 if way == 0 else self.me - 1
        return remote(
            self.part(k, j),
            self.inbox(way, k, j),
            self.sems.at[way, k, j],
            self.sems.at[2 + way, k, j],
            "dp",
            target,
        )

    def begin(self, k):
        last = self.size - 1
        for turn in range(last):
            for way, j, end in ((0, last - turn, 0), (1, turn, last)):

                @pl.when(self.me == end)
                def _():
                    self.copy(way, k, j).start()

    def begin_block(self, k, j):
        for way, end in ((0, 0), (1, self.size - 1)):
            if j != end:

                @pl.when(self.me == end)
                def _():
                    self.copy(way, k, j).start()

    def sweep(self, k, way):
        last = self.size - 1
        for turn in range(last):
            j = last - turn if way == 0 else turn
            inner = (self.me > 0) if way == 0 else (self.me < last)
            passing = (j > self.me) if way == 0 else (j < self.me)

            @pl.when(inner & (passing | (self.me == j)))
            def _():
                self.copy(way, k, j).wait_recv()

            @pl.when(inner & passing)
            def _():
                total = self.part(k, j)[...].astype(jnp.float32) + self.inbox(way, k, j)[
                    ...
                ].astype(jnp.float32)
                self.part(k, j)[...] = total.astype(self.part(k, j).dtype)
                self.copy(way, k, j).start()

    def near(self, k):
        @pl.when(self.me < self.size // 2)
        def _():
            self.sweep(k, 0)

        @pl.when(self.me >= self.size // 2)
        def _():
            self.sweep(k, 1)

    def far(self, k):
        @pl.when(self.me < self.size // 2)
        def _():
            self.sweep(k, 1)

        @pl.when(self.me >= self.size // 2)
        def _():
            self.sweep(k, 0)

    def result(self, k, out):
        last = self.size - 1
        out[...] = self.part(k, self.me)[...].astype(jnp.float32)

        @pl.when(self.me > 0)
        def _():
            out[...] += self.inbox(0, k, self.me)[...].astype(jnp.float32)

        @pl.when(self.me < last)
        def _():
            out[...] += self.inbox(1, k, self.me)[...].astype(jnp.float32)

    def finish(self, k):
        last = self.size - 1
        for j in range(self.size):
            for way in range(2):
                sent = (j > self.me) if way == 0 else (j < self.me)

                @pl.when(sent)
                def _():
                    self.copy(way, k, j).wait_send()


def bit_orders(size):
    bits = [1 << i for i in range(size.bit_length() - 1)]
    bits.reverse()
    half = max(1, len(bits) // 2)
    if len(bits) == 3:
        return [bits, [bits[1], bits[0], bits[2]]]
    return [bits, bits[half:] + bits[:half]]


class PlaneGather:
    def __init__(self, own, slot, sems, orders):
        self.size, self.me = lax.axis_size("expert"), lax.axis_index("expert")
        self.own, self.slot, self.sems, self.orders = own, slot, sems, orders

    def place(self, h, mask):
        return max(at for at, bit in enumerate(self.orders[h]) if mask & bit)

    def copy(self, h, mask):
        last = self.orders[h][self.place(h, mask)]
        block = flipped(self.me, mask - last)
        src = self.own(h) if mask == last else self.slot(h, block)
        return remote(
            src,
            self.slot(h, block),
            self.sems.at[0, h, mask],
            self.sems.at[1, h, mask],
            "expert",
            flipped(self.me, last),
        )

    def wait(self, h, mask):
        here = self.slot(h, flipped(self.me, mask))
        remote(
            here, here, self.sems.at[0, h, mask], self.sems.at[1, h, mask], "expert", flipped(self.me, 1)
        ).wait_recv()

    def start(self, some=None):
        for at in range(len(self.orders[0])):
            for h, order in enumerate(self.orders):
                if some is None or h in some:
                    self.copy(h, order[at]).start()

    def moves(self):
        found = [(h, mask) for h in range(len(self.orders)) for mask in range(1, self.size)]
        found.sort(key=lambda move: (move[1].bit_count(), self.place(*move), move[0]))
        return found

    def move(self, h, mask):
        self.wait(h, mask)
        for bit in self.orders[h][self.place(h, mask) + 1 :]:
            self.copy(h, mask | bit).start()

    def relay(self):
        for h, mask in self.moves():
            self.move(h, mask)

    def finish(self):
        for h in range(len(self.orders)):
            for mask in range(1, self.size):
                self.copy(h, mask).wait_send()


class PlaneReduce:
    def __init__(self, acc, inbox, sems, orders):
        self.size, self.me = lax.axis_size("expert"), lax.axis_index("expert")
        self.acc, self.inbox, self.sems, self.orders = acc, inbox, sems, orders

    def masks(self, h, at):
        later = self.orders[h][at + 1 :]
        found = [0]
        for bit in later:
            found = found + [mask | bit for mask in found]
        return sorted(found, key=lambda mask: (mask == 0, self.first(h, mask) if mask else 0))

    def first(self, h, mask):
        return min(at for at, bit in enumerate(self.orders[h]) if mask & bit)

    def number(self, h, at, mask):
        before = sum(self.size >> (step + 1) for step in range(at))
        return before + sorted(self.masks(h, at)).index(mask)

    def copy(self, h, at, mask):
        bit = self.orders[h][at]
        n = self.number(h, at, mask)
        return remote(
            self.acc(h, flipped(self.me, mask | bit)),
            self.inbox(h, n),
            self.sems.at[0, h, n],
            self.sems.at[1, h, n],
            "expert",
            flipped(self.me, bit),
        )

    def start(self, h):
        for mask in self.masks(h, 0):
            self.copy(h, 0, mask).start()

    def advance(self, h, at):
        for mask in self.masks(h, at):
            self.copy(h, at, mask).wait_recv()
            if mask:
                here = self.acc(h, flipped(self.me, mask))
                arrived = self.inbox(h, self.number(h, at, mask))
                here[...] = (
                    here[...].astype(jnp.float32) + arrived[...].astype(jnp.float32)
                ).astype(here.dtype)
                if self.first(h, mask) == at + 1:
                    self.copy(h, at + 1, mask - self.orders[h][at + 1]).start()

    def result(self, h, out):
        total = self.acc(h, self.me)[...].astype(jnp.float32)
        for at in range(len(self.orders[h])):
            total = total + self.inbox(h, self.number(h, at, 0))[...].astype(jnp.float32)
        out[...] = total

    def finish(self, h):
        for at in range(len(self.orders[h])):
            for mask in self.masks(h, at):
                self.copy(h, at, mask).wait_send()


def part_of(ref, item, rows, width):
    chunk, low, wide = item
    if wide == width:
        return ref.at[chunk, rows]
    return ref.at[chunk, rows, pl.ds(low, wide)]


def halved(chunks, width, at):
    items = []
    for c in range(chunks):
        if c == at and width >= 256:
            items += [(c, 0, width // 2), (c, width // 2, width // 2)]
        else:
            items.append((c, 0, width))
    return items


def vmem(shape, dtype):
    return pltpu.VMEM(shape, dtype)


def dma(*shape):
    return pltpu.SemaphoreType.DMA(shape)


def call(kernel, outs, scratch, number, *operands):
    whole = pl.BlockSpec(memory_space=pltpu.VMEM)
    return pl.pallas_call(
        kernel,
        out_shape=outs,
        in_specs=[whole] * len(operands),
        out_specs=jax.tree.map(lambda _: whole, outs),
        scratch_shapes=scratch,
        compiler_params=pltpu.CompilerParams(
            collective_id=number, has_side_effects=True, vmem_limit_bytes=VMEM_LIMIT
        ),
    )(*operands)


class PlaneExchange:
    def __init__(self, src, dst, sems):
        self.size, self.me = lax.axis_size("expert"), lax.axis_index("expert")
        self.src, self.dst, self.sems = src, dst, sems

    def copy(self, k, peer):
        return remote(
            self.src(k, peer),
            self.dst(k, self.me),
            self.sems.at[0, k, peer],
            self.sems.at[1, k, self.me],
            "expert",
            peer,
        )

    def peers(self):
        order = sorted(range(1, self.size), key=lambda mask: (mask == 1, -mask.bit_count()))
        return [flipped(self.me, mask) for mask in order]

    def start(self, k):
        for peer in self.peers():
            self.copy(k, peer).start()

    def keep(self, k):
        self.dst(k, self.me)[...] = self.src(k, self.me)[...]

    def wait(self, k):
        for peer in self.peers():
            here = self.dst(k, peer)
            remote(
                here, here, self.sems.at[0, k, peer], self.sems.at[1, k, peer], "expert", peer
            ).wait_recv()

    def finish(self, k):
        for peer in self.peers():
            self.copy(k, peer).wait_send()


def combine(values, select, slots, number):
    data, group = lax.axis_size("dp"), lax.axis_size("expert")
    chunks, entries, width = values.shape
    rows = select.shape[1] // data
    window = 1

    def kernel(v_ref, select, out_ref, turned, back, part, inbox, ls, es):
        greet()
        exchange = PlaneExchange(
            lambda k, p: v_ref.at[k, pl.ds(pl.multiple_of(p * slots, slots), slots)],
            lambda k, p: back.at[k, pl.ds(pl.multiple_of(p * slots, slots), slots)],
            es,
        )
        line = LineReduce(
            lambda k, j: part.at[k, pl.ds(pl.multiple_of(j * rows, rows), rows)],
            lambda way, k, j: inbox.at[k, j + 1 - way],
            ls,
        )
        for k in range(window):
            exchange.start(k)
        turned[...] = select[...].T
        for k in range(chunks):
            exchange.keep(k)
        for k in range(chunks):
            exchange.wait(k)
            if k + window < chunks:
                exchange.start(k + window)
            total = jnp.dot(
                turned[...], back[k], preferred_element_type=jnp.float32
            )
            part[k] = total.astype(jnp.bfloat16)
            line.begin(k)
            line.near(k)
            if k:
                line.far(k - 1)
        line.far(chunks - 1)
        for k in range(chunks):
            line.result(k, out_ref.at[:, pl.ds(k * width, width)])
            line.finish(k)
            exchange.finish(k)

    return call(
        kernel,
        jax.ShapeDtypeStruct((rows, chunks * width), jnp.float32),
        [
            vmem(select.shape[::-1], jnp.bfloat16),
            vmem(values.shape, jnp.bfloat16),
            vmem((chunks, data * rows, width), jnp.bfloat16),
            vmem((chunks, data + 1, rows, width), jnp.bfloat16),
            dma(4, chunks, data),
            dma(2, chunks, group),
        ],
        number,
        values,
        select,
    )


def expert_layer(
    second, pair, probs, hidden, out_grad, gain, w_router, select, grads_here,
    w_gate, w_up, w_down, cut, with_mix,
):
    data, group = lax.axis_size("dp"), lax.axis_size("expert")
    chunks, rows, width = second.shape
    model = chunks * width
    experts = w_router.shape[0]
    extra = pair.shape[1]
    entries = select.shape[0]
    slots = entries // group
    hidden_units = w_gate.shape[1]
    block = 2 * slots
    pieces = model // cut
    early = max(1, chunks // 2)
    came = halved(chunks, width, 0)
    sent = halved(chunks, width, chunks - 1)

    def kernel(
        sec_ref, pair_ref, prob_ref, hid_ref, g_ref, gain_ref, r_ref, select, gh_any, wg_any, wu_any, wd_any,
        d_any, s_any, a_any, v_any, grad_hidden, branch_any, norm_sum, router_sum, turned_any, mix_out,
        x_all, pair_all, picked_pair, pair_here, rows_out, pair_out, back, pair_back,
        inbox, pair_box, summed, pair_sum, turned, low, wg, wu, wd,
        x_here, g_stage, s_stage, v_stage, a_stage, grad_h, d_stage,
        mix_back, loads, g_load, stores, keeps, d_s, ls, es, ls2, es2, es3,
    ):
        place, plane = lax.axis_index("dp"), lax.axis_index("expert")
        own = place * group + plane
        pairs = group // 2
        fetches = [
            pltpu.make_async_copy(src, dst, loads.at[at])
            for at, (src, dst) in enumerate(((wg_any, wg), (wu_any, wu), (wd_any, wd)))
        ]

        def block_at(step):
            mask, at, bit = pairs - 1 - step, 0, 1
            while bit < pairs:
                at = at + bit * ((plane // (2 * bit) + mask // bit) % 2)
                bit *= 2
            return at

        def block_rows(step):
            at = block_at(step)
            return pl.ds(pl.multiple_of(at * block, block), block)

        def load_grads(step):
            slot = step % 2
            return pltpu.make_async_copy(
                gh_any.at[:, block_rows(step)], g_stage.at[slot], g_load.at[slot]
            )

        def store_block(step):
            slot, here = step % 2, block_rows(step)
            return [
                pltpu.make_async_copy(s_stage.at[slot], s_any.at[:, here], stores.at[slot, 0]),
                pltpu.make_async_copy(v_stage.at[slot], v_any.at[:, here], stores.at[slot, 1]),
                pltpu.make_async_copy(a_stage.at[slot], a_any.at[here], stores.at[slot, 2]),
            ]

        load_grads(0).start()
        for fetch in fetches:
            fetch.start()
        mine = pl.ds(pl.multiple_of(place * rows, rows), rows)
        for c in range(chunks):
            x_all[c, mine] = sec_ref[c]
        pair_all[mine] = pair_ref[...]
        greet()

        def slot_rows(p):
            return pl.ds(pl.multiple_of(p * slots, slots), slots)

        def token_rows(j):
            return pl.ds(pl.multiple_of(j * rows, rows), rows)

        def pick(items, full, wide):
            return lambda k, p: (
                part_of(full, items[k], slot_rows(p), width)
                if k < len(items)
                else wide.at[slot_rows(p)]
            )

        exchange = PlaneExchange(
            pick(came, rows_out, picked_pair), pick(came, x_here, pair_here), es
        )

        def done(k):
            if k == 0:
                picked_pair[...] = jnp.dot(
                    select[...], pair_all[...], preferred_element_type=jnp.float32
                ).astype(jnp.bfloat16)
                exchange.start(len(came))
                exchange.keep(len(came))
            else:
                c, at, wide = came[k - 1]
                rows_out[c, :, at : at + wide] = jnp.dot(
                    select[...], x_all[c, :, at : at + wide], preferred_element_type=jnp.float32
                ).astype(jnp.bfloat16)
                exchange.start(k - 1)
                exchange.keep(k - 1)

        line = LineGather(
            lambda k: (
                pair_ref if k == 0 else part_of(sec_ref, came[k - 1], pl.ds(0, rows), width)
            ),
            lambda k, j: (
                pair_all.at[token_rows(j)]
                if k == 0
                else part_of(x_all, came[k - 1], token_rows(j), width)
            ),
            ls,
        )
        line.run(len(came) + 1, 3, done)
        turned[...] = select[...].T
        keep_turned = pltpu.make_async_copy(turned, turned_any, keeps.at[2])
        keep_turned.start()
        for fetch in fetches:
            fetch.wait()
        for k in range(len(came) + 1):
            exchange.wait(k)
        for k in range(len(came) + 1):
            exchange.finish(k)

        give_back = PlaneExchange(
            pick(sent, rows_out, pair_out), pick(sent, back, pair_back), es2
        )
        lane = lax.broadcasted_iota(jnp.int32, (block, extra), 1)

        def run_block(step, carry):
            at = block_at(step)
            here = block_rows(step)
            slot = step % 2
            load_grads(step).wait()

            @pl.when(step + 1 < pairs)
            def _():
                load_grads(step + 1).start()

            @pl.when(step >= 2)
            def _():
                for store in store_block(step - 2):
                    store.wait()

            chosen = (lane == own) | (lane == own + experts)
            prob = jnp.sum(
                jnp.where(chosen, pair_here[here].astype(jnp.float32), 0.0), axis=-1, keepdims=True
            )
            gate_h = jnp.zeros((block, hidden_units), jnp.float32)
            up_h = jnp.zeros((block, hidden_units), jnp.float32)
            for c in range(chunks):
                x = x_here[c, here]
                part = pl.ds(c * width, width)
                gate_h += jnp.dot(x, wg[part], preferred_element_type=jnp.float32)
                up_h += jnp.dot(x, wu[part], preferred_element_type=jnp.float32)
            sigmoid = jax.nn.sigmoid(gate_h)
            silu = gate_h * sigmoid
            active = (silu * up_h).astype(jnp.bfloat16)
            a_stage[slot] = active
            grad_active = jnp.zeros((block, hidden_units), jnp.float32)
            slot_gate = jnp.zeros((block, 1), jnp.float32)
            for c in range(chunks):
                part = pl.ds(c * width, width)
                out = jnp.dot(active, wd[:, part], preferred_element_type=jnp.float32)
                out = out.astype(jnp.bfloat16).astype(jnp.float32)
                grad = g_stage[slot, c].astype(jnp.float32)
                slot_gate += jnp.sum(out * grad, axis=-1, keepdims=True)
                v_stage[slot, c] = (prob * out).astype(jnp.bfloat16)
                grad_slot = (prob * grad).astype(jnp.bfloat16)
                s_stage[slot, c] = grad_slot
                grad_active += nt_dot(grad_slot, wd[:, part])
            grad_gate_h = grad_active * up_h * sigmoid * (1.0 + gate_h * (1.0 - sigmoid))
            grad_gate_h = grad_gate_h.astype(jnp.bfloat16)
            grad_up_h = (grad_active * silu).astype(jnp.bfloat16)
            grad_h[0, here] = grad_gate_h
            grad_h[1, here] = grad_up_h
            for store in store_block(step):
                store.start()
            top = slot_gate.astype(jnp.bfloat16).astype(jnp.float32)
            pair_out[here] = (
                jnp.where(lane == own, top, 0.0)
                + jnp.where(lane == own + experts, slot_gate - top, 0.0)
            ).astype(jnp.bfloat16)
            for c in range(chunks):
                part = pl.ds(c * width, width)
                rows_out[c, here] = (
                    nt_dot(grad_gate_h, wg[part]) + nt_dot(grad_up_h, wu[part])
                ).astype(jnp.bfloat16)
            for member in range(2):
                peer = 2 * at + member

                @pl.when(peer != plane)
                def _():
                    for k in [len(sent)] + list(range(early)):
                        give_back.copy(k, peer).start()

            return carry

        lax.fori_loop(0, pairs, run_block, 0)
        def store_grads(c, side):
            return pltpu.make_async_copy(
                d_stage.at[side], d_any.at[side, pl.ds(c * width, width)], d_s.at[side]
            )

        def weight_grads(c):
            x = x_here[c].T
            for side in range(2):
                if c:
                    store_grads(c - 1, side).wait()
                d_stage[side] = jnp.dot(
                    x, grad_h[side], preferred_element_type=jnp.float32
                ).astype(jnp.bfloat16)
                store_grads(c, side).start()

        for step in range(max(0, pairs - 2), pairs):
            for store in store_block(step):
                store.wait()
        mix = PlaneExchange(
            lambda k, p: v_any.at[0, slot_rows(p)], lambda k, p: mix_back.at[slot_rows(p)], es3
        )
        own_mix = pltpu.make_async_copy(
            v_any.at[0, slot_rows(plane)], mix_back.at[slot_rows(plane)], keeps.at[3]
        ) if with_mix else None
        give_back.start(early)
        for k in range(len(sent) + 1):
            give_back.keep(k)
        sums = LineReduce(
            lambda k, j: (
                part_of(x_all, sent[k], token_rows(j), width)
                if k < len(sent)
                else pair_all.at[token_rows(j)]
            ),
            lambda way, k, j: (
                inbox.at[
                    sent[k][0], j + 1 - way, :, pl.ds(sent[k][1], sent[k][2])
                ]
                if k < len(sent)
                else pair_box.at[j + 1 - way]
            ),
            ls2,
        )
        order = [len(sent)] + list(range(len(sent)))
        for at, k in enumerate(order):
            give_back.wait(k)
            if k < len(sent):
                c, low_col, wide = sent[k]
                x_all[c, :, low_col : low_col + wide] = jnp.dot(
                    turned[...],
                    back[c, :, low_col : low_col + wide],
                    preferred_element_type=jnp.float32,
                ).astype(jnp.bfloat16)
            else:
                pair_all[...] = jnp.dot(
                    turned[...], pair_back[...], preferred_element_type=jnp.float32
                ).astype(jnp.bfloat16)
            sums.begin(k)
            if k < len(sent) and early + 1 + k < len(sent):
                give_back.start(early + 1 + k)
            if at >= 1:
                sums.near(order[at - 1])
            if at >= 2:
                sums.far(order[at - 2])
            if at < chunks:
                weight_grads(at)
        if with_mix:
            mix.start(0)
            own_mix.start()
        sums.near(order[-1])
        for k in order[-2:]:
            sums.far(k)
        for k, (c, low_col, wide) in enumerate(sent):
            sums.result(k, summed.at[:, pl.ds(c * width + low_col, wide)])
        sums.result(len(sent), pair_sum)

        gate = prob_ref[...]
        grad_gate = pair_sum[:, 0:experts] + pair_sum[:, experts : 2 * experts]
        inner = jnp.sum(gate * grad_gate, axis=-1, keepdims=True)
        grad_logits = (gate * (grad_gate - inner)).astype(jnp.bfloat16)
        for c in range(chunks):
            part = pl.ds(c * width, width)
            router_sum[:, part] = lax.dot_general(
                grad_logits,
                sec_ref[c],
                (((0,), (0,)), ((), ())),
                preferred_element_type=jnp.float32,
            )
        grad_second = summed[...] + jnp.dot(
            grad_logits, r_ref[...], preferred_element_type=jnp.float32
        )
        state = hid_ref[...]
        scale = row_scale(state)
        norm_sum[...] = jnp.sum(grad_second * state * scale, axis=0, keepdims=True)
        scaled = grad_second * gain_ref[...]
        inner = jnp.mean(scaled * state, axis=-1, keepdims=True)
        total = scale * scaled - state * (scale * scale * scale * inner)
        total = total + g_ref[...].astype(jnp.float32)
        grad_hidden[...] = total
        total = total.astype(jnp.bfloat16)
        for piece in range(pieces):
            low[piece] = total[:, piece * cut : (piece + 1) * cut]
        keep_low = pltpu.make_async_copy(low, branch_any, keeps.at[1])
        keep_low.start()
        if with_mix:
            own_mix.wait()
            mix.wait(0)
            mix_out[...] = jnp.dot(
                turned[...], mix_back[...], preferred_element_type=jnp.float32
            ).astype(jnp.bfloat16)
            mix.finish(0)
        for side in range(2):
            store_grads(chunks - 1, side).wait()
        keep_turned.wait()
        keep_low.wait()
        for k in range(len(sent) + 1):
            sums.finish(k)
            give_back.finish(k)

    bf, fl = jnp.bfloat16, jnp.float32
    whole = pl.BlockSpec(memory_space=pltpu.VMEM)
    anywhere = pl.BlockSpec(memory_space=pl.ANY)
    outs = [
        jax.ShapeDtypeStruct((2, model, hidden_units), bf),
        jax.ShapeDtypeStruct((chunks, entries, width), bf),
        jax.ShapeDtypeStruct((entries, hidden_units), bf),
        jax.ShapeDtypeStruct((chunks, entries, width), bf),
        jax.ShapeDtypeStruct((rows, model), fl),
        jax.ShapeDtypeStruct((pieces, rows, cut), bf),
        jax.ShapeDtypeStruct((1, model), fl),
        jax.ShapeDtypeStruct((experts, model), fl),
        jax.ShapeDtypeStruct(select.shape[::-1], bf),
        jax.ShapeDtypeStruct((data * rows if with_mix else 16, width), bf),
    ]
    results = list(pl.pallas_call(
        kernel,
        out_shape=outs,
        in_specs=[whole] * 8 + [anywhere] * 4,
        out_specs=[anywhere] * 4 + [whole, anywhere, whole, whole, anywhere, whole],
        scratch_shapes=[
            vmem((chunks, data * rows, width), bf),
            vmem((data * rows, extra), bf),
            vmem((entries, extra), bf),
            vmem((entries, extra), bf),
            vmem((chunks, entries, width), bf),
            vmem((entries, extra), bf),
            vmem((chunks, entries, width), bf),
            vmem((entries, extra), bf),
            vmem((chunks, data + 1, rows, width), bf),
            vmem((data + 1, rows, extra), bf),
            vmem((rows, model), fl),
            vmem((rows, extra), fl),
            vmem(select.shape[::-1], bf),
            vmem((pieces, rows, cut), bf),
            vmem((model, hidden_units), bf),
            vmem((model, hidden_units), bf),
            vmem((hidden_units, model), bf),
            vmem((chunks, entries, width), bf),
            vmem((2, chunks, block, width), bf),
            vmem((2, chunks, block, width), bf),
            vmem((2, chunks, block, width), bf),
            vmem((2, block, hidden_units), bf),
            vmem((2, entries, hidden_units), bf),
            vmem((2, width, hidden_units), bf),
            vmem((entries if with_mix else 16, width), bf),
            dma(3),
            dma(2),
            dma(2, 3),
            dma(4),
            dma(2),
            dma(4, len(came) + 1, data - 1),
            dma(2, len(came) + 1, group),
            dma(4, len(sent) + 1, data),
            dma(2, len(sent) + 1, group),
            dma(2, 1, group),
        ],
        compiler_params=pltpu.CompilerParams(
            collective_id=3, has_side_effects=True, vmem_limit_bytes=VMEM_LIMIT
        ),
    )(
        second, pair, probs, hidden, out_grad, gain, w_router, select, grads_here,
        w_gate, w_up, w_down,
    ))
    return results


def expert_weight_grads(grad_h, grad_arrived, act, others, kv, small):
    chunks, entries, width = grad_arrived.shape
    hidden_units = act.shape[1]
    part = kv.shape[0] // 2
    passed = len(others) + 2 + len(small)

    def kernel(h_ref, s_ref, act_ref, *refs):
        sources = refs[:passed]
        gate_out, up_out, down_out = refs[passed : passed + 3]
        targets = refs[passed + 3 : 2 * passed + 3]
        turned = refs[2 * passed + 3]

        @pl.when(pl.program_id(0) == 0)
        def _():
            turned[...] = act_ref[...].T

        for source, target in zip(sources, targets):
            target[...] = source[...]
        gate_out[0] = h_ref[0].astype(jnp.float32)
        up_out[0] = h_ref[1].astype(jnp.float32)
        down_out[0] = jnp.dot(turned[...], s_ref[0], preferred_element_type=jnp.float32)

    tall = pl.BlockSpec((1, width, hidden_units), lambda c: (0, c, 0))

    def slab(lines, item, first=0):
        return pl.BlockSpec((lines // chunks, item.shape[1]), lambda c: (c + first, 0))

    slabs = [slab(item.shape[0], item) for item in others]
    half = slab(part, kv)
    whole = [pl.BlockSpec(item.shape, lambda c: (0, 0)) for item in small]
    return pl.pallas_call(
        kernel,
        grid=(chunks,),
        out_shape=[
            jax.ShapeDtypeStruct((1, chunks * width, hidden_units), jnp.float32),
            jax.ShapeDtypeStruct((1, chunks * width, hidden_units), jnp.float32),
            jax.ShapeDtypeStruct((1, hidden_units, chunks * width), jnp.float32),
        ]
        + [jax.ShapeDtypeStruct(item.shape, item.dtype) for item in others]
        + [jax.ShapeDtypeStruct((part, kv.shape[1]), kv.dtype)] * 2
        + [jax.ShapeDtypeStruct(item.shape, item.dtype) for item in small],
        in_specs=[
            pl.BlockSpec((2, width, hidden_units), lambda c: (0, c, 0)),
            pl.BlockSpec((1, entries, width), lambda c: (c, 0, 0)),
            pl.BlockSpec((entries, hidden_units), lambda c: (0, 0)),
        ]
        + slabs
        + [half, slab(part, kv, chunks)]
        + whole,
        out_specs=[tall, tall, pl.BlockSpec((1, hidden_units, width), lambda c: (0, 0, c))]
        + slabs
        + [half, half]
        + whole,
        scratch_shapes=[vmem((hidden_units, entries), jnp.bfloat16)],
        compiler_params=pltpu.CompilerParams(vmem_limit_bytes=VMEM_LIMIT),
    )(grad_h, grad_arrived, act, *others, kv, kv, *small)


def attention_backward(
    grad_branch, out_blocks, x, w_q, w_kv, q_raw, q_low, k_raw, k_low, v_low, lse, att,
    cos, sin, gain_q, gain_k, mixed, turned, tokens, gain, grad_hidden, hidden, norm2_sum, router_sum, first_mix,
    seq_len, with_mix,
):
    data, group = lax.axis_size("dp"), lax.axis_size("expert")
    pieces, rows, cut = grad_branch.shape
    chunks, total, width = x.shape
    model = chunks * width
    depth = model // data
    wide = w_q.shape[1]
    sharing, _, both, _ = w_kv.shape
    part = both // 2
    head = sharing * part
    heads = wide // head
    block = min(256, seq_len)
    scale = head ** (-0.5)
    entries = turned.shape[1]
    slots = entries // group
    orders = [order[::-1] for order in bit_orders(group)]
    orders = [orders[at % 2] for at in range(chunks)]
    steps = len(orders[0])

    def kernel(
        gb_ref, wo_any, x_any, wq_any, wkv_any, qr_any, ql_any, kr_any, kl_any, vl_any, lse_any, att_ref,
        cos_ref, sin_ref, gq_ref, gk_ref, mix_any, turned_any, tok_ref, gain_ref, gh_any, hid_ref, n2_ref, rt_any, fm_ref,
        tok_out, wo_out, wq_out, wkv_out, gq_out, gk_out, n1_out, n2_out, rt_out, layer_out,
        wo_ref, x_ref, wq_ref, wkv_ref, ql_ref, kr_ref, kl_ref, vl_ref, lse_ref, turned,
        big, row_terms, log_rows, dq_low, dk, dv, dkv_low, kv_box, raw_buf,
        wo_part, wo_box, w_part, w_box, kv_part, kv_inbox, dx_box, back,
        mix_part, mix_box, summed, dx_sum, vec, vec_plane, vec_half, vec_line, rt_acc, rt_box, rt_half, rt_line, gq_sum, gk_sum,
        loads, raw_load, keep_s, wo_s, w_s, kv_s, sib_s, dx_s, ex_s, mix_s, vp_s, vl_s, rp_s, rl_s, rg_s, gb_s,
    ):
        place, plane = lax.axis_index("dp"), lax.axis_index("expert")
        member = plane % sharing

        def branch(j):
            first = j * cut
            return big.at[first // width, :, pl.ds(first % width, cut)]

        fetches = [
            pltpu.make_async_copy(src, dst, loads.at[at])
            for at, (src, dst) in enumerate(
                (
                    (rt_any, rt_acc),
                    (wo_any, wo_ref),
                    (ql_any, ql_ref),
                    (kl_any, kl_ref),
                    (vl_any, vl_ref),
                    (lse_any, lse_ref),
                    (x_any, x_ref),
                    (kr_any, kr_ref),
                    (wq_any, wq_ref),
                    (wkv_any, wkv_ref),
                    (gh_any, tok_out),
                )
            )
        ]
        for fetch in fetches:
            fetch.start()
        if with_mix:
            turned_load = pltpu.make_async_copy(turned_any, turned, loads.at[len(fetches)])
            turned_load.start()

        def load_raw(h):
            mine = pl.ds(pl.multiple_of(h * head, head), head)
            return pltpu.make_async_copy(qr_any.at[:, mine], raw_buf.at[h % 2], raw_load.at[h % 2])

        load_raw(0).start()

        def slot_rows(p):
            return pl.ds(pl.multiple_of(p * slots, slots), slots)

        def token_rows(j):
            return pl.ds(pl.multiple_of(j * rows, rows), rows)

        exchange = PlaneExchange(
            lambda k, p: mix_any.at[k, slot_rows(p)], lambda k, p: back.at[k, slot_rows(p)], ex_s
        )
        wo_sum = LineReduce(
            lambda k, j: wo_part.at[j, pl.ds(k * (wide // 2), wide // 2)],
            lambda way, k, j: wo_box.at[j + 1 - way, pl.ds(k * (wide // 2), wide // 2)],
            wo_s,
        )
        w_sum = LineReduce(
            lambda k, j: w_part.at[k, j], lambda way, k, j: w_box.at[k, j + 1 - way], w_s
        )
        kv_sum = LineReduce(
            lambda k, j: kv_part.at[j], lambda way, k, j: kv_inbox.at[j + 1 - way], kv_s
        )
        reduce = PlaneReduce(
            lambda h, j: big.at[h, token_rows(j)], lambda h, n: dx_box.at[h, n], dx_s, orders
        )

        mix_sum = LineReduce(
            lambda k, j: mix_part.at[k, token_rows(j)],
            lambda way, k, j: mix_box.at[k, j + 1 - way],
            mix_s,
        )
        share = model // group

        def share_cols(j):
            return pl.ds(pl.multiple_of(j * share, share), share)

        router = PlaneReduce(
            lambda h, j: rt_acc.at[:, share_cols(j)], lambda h, n: rt_box.at[n], rp_s, orders[:1]
        )
        router_back = PlaneGather(
            lambda h: rt_half.at[1],
            lambda h, j: rt_out.at[:, share_cols(j)],
            rg_s,
            bit_orders(group)[:1],
        )

        def router_line(step):
            return remote(
                rt_half.at[0], rt_line.at[step], rl_s.at[0, step], rl_s.at[1, step],
                "dp", (place + step) % data,
            )

        def router_stage(at):
            if at < steps:
                router.advance(0, at)
            elif at == steps:
                router.result(0, rt_half.at[0])
                for step in range(1, data):
                    router_line(step).start()
            elif at == steps + 1:
                total = rt_half[0]
                for step in range(1, data):
                    router_line(step).wait_recv()
                    total = total + rt_line[step]
                rt_half[1] = total
                rt_out[:, share_cols(plane)] = total
                router_back.start()
            else:
                router_back.relay()

        def vec_across(mask):
            return remote(
                vec, vec_plane.at[mask], vp_s.at[0, mask], vp_s.at[1, mask],
                "expert", flipped(plane, mask),
            )

        def vec_along(step):
            return remote(
                vec_half, vec_line.at[step], vl_s.at[0, step], vl_s.at[1, step],
                "dp", (place + step) % data,
            )

        def x_block(j):
            first = j * depth
            inner = first % width
            return x_ref[first // width, :, inner : inner + depth]

        own_rows = token_rows(plane)
        for h in range(pieces):
            branch(h)[own_rows] = gb_ref[h]
        if with_mix:
            mix_part[0] = fm_ref[...]
        greet(far=True)
        if with_mix:
            mix_sum.begin(0)
        gather = PlaneGather(
            lambda h: gb_ref.at[h],
            lambda h, j: big.at[
                (h * cut) // width, token_rows(j), pl.ds((h * cut) % width, cut)
            ],
            gb_s,
            [bit_orders(group)[at % 2] for at in range(pieces)],
        )
        pairs = [range(h, min(h + 2, pieces)) for h in range(0, pieces, 2)]
        gather.start(pairs[0])
        fetches[0].wait()
        att_turned = att_ref[...].T

        def wo_piece(j):
            wo_part[j] = jnp.dot(
                att_turned, branch(j)[...], preferred_element_type=jnp.float32
            ).astype(jnp.bfloat16)
            for k in range(2):
                wo_sum.begin_block(k, j)

        for at, pair in enumerate(pairs):
            moves = [move for move in gather.moves() if move[0] in pair]
            first = [move for move in moves if move[1].bit_count() == 1]
            for move in first:
                gather.move(*move)
            if at + 1 < len(pairs):
                gather.start(pairs[at + 1])
            for move in moves[len(first) :]:
                gather.move(*move)
            for h in pair:
                wo_piece(h)
        router.start(0)
        if with_mix:
            if chunks > 1:
                exchange.start(1)
            mix_sum.near(0)
        fetches[1].wait()

        lane = lax.broadcasted_iota(jnp.int32, (block, head), 1)

        def attended_grad(at, carry):
            here = pl.ds(pl.multiple_of(at * block, block), block)
            value = jnp.zeros((block, wide), jnp.float32)
            for j in range(pieces):
                value += nt_dot(branch(j)[here], wo_ref[j])
            low = value.astype(jnp.bfloat16)
            dq_low[here] = low
            both_rows = low.astype(jnp.float32) * att_ref[here].astype(jnp.float32)
            terms = jnp.zeros((block, head), jnp.float32)
            for h in range(heads):
                term = jnp.sum(both_rows[:, h * head : (h + 1) * head], axis=-1, keepdims=True)
                terms = jnp.where(lane == h, term, terms)
            dk[here] = terms
            return carry

        lax.fori_loop(0, total // block, attended_grad, 0)
        for at in range(2, 7):
            fetches[at].wait()
        row_terms[...] = dk[...].T
        log_rows[...] = lse_ref[...].T * LOG2_E
        dk[...] = jnp.zeros_like(dk)
        dv[...] = jnp.zeros_like(dv)
        above = lax.broadcasted_iota(
            jnp.int32, (block, block), 0
        ) <= lax.broadcasted_iota(jnp.int32, (block, block), 1)

        def turned_dot(left, right):
            return lax.dot_general(
                left, right, (((0,), (0,)), ((), ())), preferred_element_type=jnp.float32
            )

        def unrotate(value, table):
            return value * cos_ref[table] - half_turn(value) * sin_ref[table]

        def norm_back(turned_grad, raw, gain):
            factor = row_scale(raw)
            gain_term = jnp.sum(turned_grad * raw * factor, axis=0, keepdims=True)
            scaled = turned_grad * gain
            inner = jnp.mean(scaled * raw, axis=-1, keepdims=True)
            return factor * scaled - raw * (factor * factor * factor * inner), gain_term

        gq_sum[...] = jnp.zeros_like(gq_sum)
        gk_sum[...] = jnp.zeros_like(gk_sum)

        def own_mix(k):
            return pltpu.make_async_copy(
                mix_any.at[k, slot_rows(plane)], back.at[k, slot_rows(plane)], keep_s.at[k]
            )

        def gather_mix(k):
            own_mix(k).wait()
            exchange.wait(k)
            mix_part[k] = jnp.dot(
                turned[...], back[k], preferred_element_type=jnp.float32
            ).astype(jnp.bfloat16)
            mix_sum.begin(k)

        if with_mix:
            for k in range(1, chunks):
                own_mix(k).start()
            turned_load.wait()
            mix_sum.far(0)

        def head_back(h, carry):
            mine = pl.ds(pl.multiple_of(h * head, head), head)
            load_raw(h).wait()

            @pl.when(h + 1 < heads)
            def _():
                load_raw(h + 1).start()

            for seq in range(total // seq_len):
                base = seq * seq_len
                for at in range(seq_len // block):
                    here = pl.ds(base + at * block, block)
                    query = ql_ref[here, mine]
                    grad = dq_low[here, mine]
                    log_sum = log_rows[pl.ds(h, 1), here]
                    row_term = row_terms[pl.ds(h, 1), here]
                    grad_query = jnp.zeros((block, head), jnp.float32)
                    for other in range(at + 1):
                        behind = pl.ds(base + other * block, block)
                        key = kl_ref[behind]
                        probs = jnp.exp2(nt_dot(key, query) * (scale * LOG2_E) - log_sum)
                        if other == at:
                            probs = jnp.where(above, probs, 0.0)
                        grad_probs = nt_dot(vl_ref[behind], grad)
                        grad_scores = (probs * (grad_probs - row_term)).astype(jnp.bfloat16)
                        dv[behind] += jnp.dot(
                            probs.astype(jnp.bfloat16), grad, preferred_element_type=jnp.float32
                        )
                        dk[behind] += jnp.dot(
                            grad_scores, query, preferred_element_type=jnp.float32
                        )
                        grad_query += turned_dot(grad_scores, key)
                    grad_query = grad_query * scale
                    table = pl.ds(at * block, block)
                    raw_grad, gain_term = norm_back(
                        unrotate(grad_query, table), raw_buf[h % 2, here], gq_ref[...]
                    )
                    gq_sum[...] += gain_term
                    dq_low[here, mine] = raw_grad.astype(jnp.bfloat16)
            low_turned = dq_low[:, mine].T
            for j in range(data):
                w_part[h, j] = jnp.dot(
                    low_turned, x_block(j), preferred_element_type=jnp.float32
                ).astype(jnp.bfloat16)
            w_sum.begin(h)

            if with_mix:

                @pl.when(h + 2 < chunks)
                def _():
                    exchange.start(h + 2)

            if with_mix and heads > 2:

                @pl.when((h >= 2) & (h - 1 < chunks))
                def _():
                    gather_mix(h - 1)

            @pl.when(h == heads - 2)
            def _():
                wo_sum.near(0)

            @pl.when(h == heads - 1)
            def _():
                wo_sum.near(1)
                wo_sum.far(0)

            return carry

        lax.fori_loop(0, heads, head_back, 0)
        if with_mix:
            for k in range(heads + 2, chunks):
                exchange.start(k)
        for at in range(7, len(fetches)):
            fetches[at].wait()
        for at in range(total // block):
            here = pl.ds(at * block, block)
            table = pl.ds((at * block) % seq_len, block)
            raw_grad, gain_term = norm_back(
                unrotate(dk[here] * scale, table), kr_ref[here], gk_ref[...]
            )
            gk_sum[...] += gain_term
            value_grad = dv[here]
            for m in range(sharing):
                cols = slice(m * part, (m + 1) * part)
                dkv_low[m, here] = jnp.concatenate(
                    [raw_grad[:, cols], value_grad[:, cols]], axis=1
                ).astype(jnp.bfloat16)

        def swap(mask):
            other = flipped(plane, mask)
            return remote(
                dkv_low.at[other % sharing],
                kv_box.at[member],
                sib_s.at[0, mask],
                sib_s.at[1, mask],
                "expert",
                other,
            )

        for mask in range(1, sharing):
            swap(mask).start()
        gather.finish()
        for j in range(data):
            first = j * depth
            c, inner = first // width, first % width

            def input_grad(at, carry):
                here = pl.ds(pl.multiple_of(at * block, block), block)
                value = nt_dot(dq_low[here], wq_ref[pl.ds(first, depth)])
                for m in range(sharing):
                    value += jnp.dot(
                        dkv_low[m, here], wkv_ref[m, j], preferred_element_type=jnp.float32
                    )
                big[c, here, inner : inner + depth] = value.astype(jnp.bfloat16)
                return carry

            lax.fori_loop(0, total // block, input_grad, 0)
            if inner + depth == width:
                reduce.start(c)
        kv_box[member] = dkv_low[member]
        for mask in range(1, sharing):
            other = kv_box.at[flipped(plane, mask) % sharing]
            remote(
                other, other, sib_s.at[0, mask], sib_s.at[1, mask], "expert", flipped(plane, mask)
            ).wait_recv()
        kv_turned = [kv_box[m].T for m in range(sharing)]
        for j in range(data):
            block_x = x_block(j)
            value = sum(
                jnp.dot(item, block_x, preferred_element_type=jnp.float32) for item in kv_turned
            )
            kv_part[j] = value.astype(jnp.bfloat16)
        kv_sum.begin(0)
        mixed_at = min(chunks, max(1, heads - 1)) if with_mix else chunks
        for k in range(mixed_at, chunks - 1):
            gather_mix(k)
        for c in range(chunks):
            reduce.advance(c, 0)
        if with_mix and mixed_at < chunks:
            gather_mix(chunks - 1)
        wo_sum.far(1)
        w_sum.near(0)
        for at in range(1, steps):
            for c in range(chunks):
                reduce.advance(c, at)
        router_stage(0)
        for c in range(chunks):
            reduce.result(c, dx_sum.at[:, pl.ds(c * width, width)])
        state = tok_ref[...].astype(jnp.float32)
        grad_normed = dx_sum[...]
        raw_grad, gain_term = norm_back(grad_normed, state, gain_ref[...])
        tok_out[...] += raw_grad
        vec[...] = jnp.zeros_like(vec)
        for c in range(chunks):
            cols = slice(c * width, (c + 1) * width)
            vec[c : c + 1, 0:width] = gain_term[:, cols]
            vec[chunks + c : chunks + c + 1, 0:width] = n2_ref[:, cols]
        vec[0:1, width : width + head] = gq_sum[...]
        vec[1:2, width : width + head] = gk_sum[...]
        for mask in range(1, group):
            vec_across(mask).start()
        sweeps = [(w_sum, h) for h in range(heads)] + [(kv_sum, 0)]
        if with_mix:
            for k in range(1, chunks):
                place_at = heads - mixed_at + 2 * k
                sweeps.insert(place_at if k < mixed_at else len(sweeps), (mix_sum, k))
        for at, (line, k) in enumerate(sweeps):
            if at == 2:
                all_sum = vec[...]
                for mask in range(1, group):
                    vec_across(mask).wait_recv()
                    all_sum = all_sum + vec_plane[mask]
                vec_half[...] = all_sum
                for step in range(1, data):
                    vec_along(step).start()
            if at:
                line.near(k)
                sweeps[at - 1][0].far(sweeps[at - 1][1])
                if at < steps + 3:
                    router_stage(at)
        sweeps[-1][0].far(sweeps[-1][1])
        for stage in range(max(1, min(len(sweeps), steps + 3)), steps + 3):
            router_stage(stage)
        for k in range(2):
            wo_sum.result(k, wo_out.at[pl.ds(k * (wide // 2), wide // 2)])
        for h in range(heads):
            w_sum.result(h, summed)
            wq_out[:, h * head : (h + 1) * head] = summed[...].T
        kv_sum.result(0, wkv_out)
        if with_mix:
            for k in range(chunks):
                mix_sum.result(k, dx_sum.at[:, pl.ds(k * width, width)])
            layer_out[...] = (hid_ref[...] + dx_sum[...]).astype(jnp.bfloat16)
        all_sum = vec_half[...]
        for step in range(1, data):
            vec_along(step).wait_recv()
            all_sum = all_sum + vec_line[step]
        for c in range(chunks):
            for q in range(width // 128):
                at, cols = c * (width // 128) + q, slice(q * 128, (q + 1) * 128)
                n1_out[at : at + 1] = all_sum[c : c + 1, cols]
                n2_out[at : at + 1] = all_sum[chunks + c : chunks + c + 1, cols]
        gq_out[...] = all_sum[0:1, width : width + head]
        gk_out[...] = all_sum[1:2, width : width + head]
        for mask in range(1, group):
            vec_across(mask).wait_send()
        for step in range(1, data):
            vec_along(step).wait_send()
            router_line(step).wait_send()
        router.finish(0)
        router_back.finish()
        for k in range(2):
            wo_sum.finish(k)
        for h in range(heads):
            w_sum.finish(h)
        kv_sum.finish(0)
        for mask in range(1, sharing):
            swap(mask).wait_send()
        for c in range(chunks):
            reduce.finish(c)
        if with_mix:
            for k in range(chunks):
                mix_sum.finish(k)
                if k:
                    exchange.finish(k)

    bf, fl = jnp.bfloat16, jnp.float32
    whole = pl.BlockSpec(memory_space=pltpu.VMEM)
    anywhere = pl.BlockSpec(memory_space=pl.ANY)
    mix_entries = entries if with_mix else 16
    mix_rows = rows if with_mix else 16
    mix_all = data * rows if with_mix else 16
    experts = router_sum.shape[0]
    share = model // group
    lines = whole_up(2 * chunks, 8)
    outs = [
        jax.ShapeDtypeStruct((rows, model), fl),
        jax.ShapeDtypeStruct((wide, cut), fl),
        jax.ShapeDtypeStruct((depth, wide), fl),
        jax.ShapeDtypeStruct((both, depth), fl),
        jax.ShapeDtypeStruct((1, head), fl),
        jax.ShapeDtypeStruct((1, head), fl),
        jax.ShapeDtypeStruct((model // 128, 128), fl),
        jax.ShapeDtypeStruct((model // 128, 128), fl),
        jax.ShapeDtypeStruct((experts, model), fl),
        jax.ShapeDtypeStruct((mix_rows, model), bf),
    ]
    return pl.pallas_call(
        kernel,
        out_shape=outs,
        in_specs=[whole]
        + [anywhere] * 10
        + [whole] * 5
        + [anywhere] * 2
        + [whole] * 2
        + [anywhere, whole if with_mix else anywhere, whole, anywhere]
        + [whole if with_mix else anywhere],
        out_specs=[whole] * len(outs),
        scratch_shapes=[
            vmem(out_blocks.shape, bf),
            vmem(x.shape, bf),
            vmem(w_q.shape, bf),
            vmem(w_kv.shape, bf),
            vmem(q_low.shape, bf),
            vmem(k_raw.shape, fl),
            vmem(k_low.shape, bf),
            vmem(v_low.shape, bf),
            vmem(lse.shape, fl),
            vmem(turned.shape if with_mix else (16, 128), bf),
            vmem((chunks, total, width), bf),
            vmem((head, total), fl),
            vmem((head, total), fl),
            vmem((total, wide), bf),
            vmem((total, head), fl),
            vmem((total, head), fl),
            vmem((sharing, total, both), bf),
            vmem((sharing, total, both), bf),
            vmem((2, total, head), fl),
            vmem((data, wide, cut), bf),
            vmem((data + 1, wide, cut), bf),
            vmem((heads, data, head, depth), bf),
            vmem((heads, data + 1, head, depth), bf),
            vmem((data, both, depth), bf),
            vmem((data + 1, both, depth), bf),
            vmem((chunks, group - 1, rows, width), bf),
            vmem((chunks, mix_entries, width), bf),
            vmem((chunks, mix_all, width), bf),
            vmem((chunks, data + 1, mix_rows, width), bf),
            vmem((head, depth), fl),
            vmem((rows, model), fl),
            vmem((lines, width + head), fl),
            vmem((group, lines, width + head), fl),
            vmem((lines, width + head), fl),
            vmem((data, lines, width + head), fl),
            vmem((experts, model), fl),
            vmem((group - 1, experts, share), fl),
            vmem((2, experts, share), fl),
            vmem((data, experts, share), fl),
            vmem((1, head), fl),
            vmem((1, head), fl),
            dma(12),
            dma(2),
            dma(chunks),
            dma(4, 2, data),
            dma(4, heads, data),
            dma(4, 1, data),
            dma(2, sharing),
            dma(2, chunks, group - 1),
            dma(2, chunks, group),
            dma(4, chunks, data),
            dma(2, group),
            dma(2, data),
            dma(2, 1, group - 1),
            dma(2, data),
            dma(2, 1, group),
            dma(2, pieces, group),
        ],
        compiler_params=pltpu.CompilerParams(
            collective_id=7, has_side_effects=True, vmem_limit_bytes=VMEM_LIMIT
        ),
    )(
        grad_branch, out_blocks, x, w_q, w_kv, q_raw, q_low, k_raw, k_low, v_low, lse, att,
        cos, sin, gain_q, gain_k, mixed, turned, tokens, gain, grad_hidden, hidden, norm2_sum, router_sum, first_mix,
    )


def rope_arrays(seq_len, head_dim):
    half = head_dim // 2
    frequency = ROPE_THETA ** (-(np.arange(half) * 2.0) / head_dim)
    angles = np.arange(seq_len)[:, None] * frequency[None, :]
    cos = np.concatenate([np.cos(angles), np.cos(angles)], axis=1).astype(np.float32)
    sin = np.concatenate([-np.sin(angles), np.sin(angles)], axis=1).astype(np.float32)
    return cos, sin


def row_scale(value):
    return lax.rsqrt(jnp.mean(value * value, axis=-1, keepdims=True) + NORM_EPS)


def half_turn(value):
    return pltpu.roll(value, value.shape[-1] // 2, value.ndim - 1)


def nt_dot(left, right):
    return lax.dot_general(
        left, right, (((1,), (1,)), ((), ())), preferred_element_type=jnp.float32
    )


def causal(start, rows, keys):
    at_row = lax.broadcasted_iota(jnp.int32, (rows, keys), 0) + start
    return lax.broadcasted_iota(jnp.int32, (rows, keys), 1) <= at_row


class Always:
    def __init__(self, order):
        self.order = order

    def __getitem__(self, at):
        return self.order


def front(
    tokens, gain, w_q, w_k, w_v, w_out, out_grad, slot_rows, cos, sin, gain_q, gain_k,
    gain2, router, hot, capacity, slots, seq_len,
):
    data, group = lax.axis_size("dp"), lax.axis_size("expert")
    rows, model = tokens.shape
    width = min(512, model)
    chunks = model // width
    depth, wide = w_q.shape
    cut = w_out.shape[1]
    part = w_k.shape[0]
    both = 2 * part
    head = gain_q.shape[1]
    sharing = head // part
    heads = wide // head
    total = group * rows
    block = min(256, seq_len)
    scale = head ** (-0.5)
    experts = router.shape[0]
    extra = whole_up(2 * experts, 128)
    entries = group * slots
    x_orders = bit_orders(group)
    x_orders = [x_orders[at % 2] for at in range(chunks)]
    b_orders = [Always(order[::-1]) for order in bit_orders(group)]
    steps = len(b_orders[0][0])
    halves = 2
    deep = depth // halves
    first_grad = 2 + halves
    first_out = first_grad + chunks - 1
    first_last = first_out + 1
    last = [item for item in halved(chunks, width, chunks - 1) if item[0] == chunks - 1]
    items = first_last + len(last)

    def kernel(
        tok_ref, gain_ref, wq_ref, wk_ref, wv_ref, wo_ref, og_ref, s_ref, cos_ref, sin_ref, gq_ref, gk_ref,
        gain2_ref, r_ref, hot_ref,
        x_any, wq_any, wkv_any, wo_any, g_any, sel_any, qr_any, ql_any, kr_any, kl_any, vl_any, lse_any,
        att_any, hidden, second, pair, probs,
        x_own, g_own, kv_own, x_all, wq_all, wkv_all, wo_all, g_all, s_all, picked, g_here, select,
        q_raw, q_low, k_raw, k_low, v_low, lse, att, acc, inbox,
        ps, ls, es, ks, bs, outs,
    ):
        place, plane = lax.axis_index("dp"), lax.axis_index("expert")
        member = plane % sharing
        state = tok_ref[...].astype(jnp.float32)
        normed = (state * row_scale(state) * gain_ref[...]).astype(jnp.bfloat16)
        mine = pl.ds(pl.multiple_of(place * rows, rows), rows)
        own_rows = pl.ds(pl.multiple_of(plane * rows, rows), rows)
        for c in range(chunks):
            x_own[c] = normed[:, c * width : (c + 1) * width]
            x_all[c, own_rows] = x_own[c]
            g_own[c] = og_ref[:, c * width : (c + 1) * width]
            g_all[c, mine] = g_own[c]
        kv_own[0:part] = wk_ref[...]
        kv_own[part:both] = wv_ref[...]
        wq_all[place] = wq_ref[...]
        wkv_all[member, place] = kv_own[...]
        wo_all[place] = wo_ref[...]
        s_all[place] = s_ref[...]
        greet()

        def token_rows(j):
            return pl.ds(pl.multiple_of(j * rows, rows), rows)

        def slot_rows_of(p):
            return pl.ds(pl.multiple_of(p * slots, slots), slots)

        gather = PlaneGather(
            lambda h: x_own.at[h], lambda h, j: x_all.at[h, token_rows(j)], ps, x_orders
        )

        def is_grad(k):
            return not isinstance(k, int) or first_grad <= k < first_out

        def own(k):
            if is_grad(k):
                return g_own.at[k - first_grad]
            if k == 0:
                return s_ref
            if k == 1:
                return kv_own
            if k < first_grad:
                return wq_ref.at[pl.ds((k - 2) * deep, deep)]
            if k >= first_last:
                return part_of(g_own, last[k - first_last], pl.ds(0, rows), width)
            return wo_ref

        def slot(k, j):
            if is_grad(k):
                return g_all.at[k - first_grad, token_rows(j)]
            if k == 0:
                return s_all.at[j]
            if k == 1:
                return wkv_all.at[member, j]
            if k < first_grad:
                return wq_all.at[j, pl.ds((k - 2) * deep, deep)]
            if k >= first_last:
                return part_of(g_all, last[k - first_last], token_rows(j), width)
            return wo_all.at[j]

        line = LineGather(own, slot, ls)
        def exchanged(ref):
            return lambda k, p: (
                part_of(ref, last[k - chunks + 1], slot_rows_of(p), width)
                if isinstance(k, int) and k >= chunks - 1
                else ref.at[k, slot_rows_of(p)]
            )

        exchange = PlaneExchange(exchanged(picked), exchanged(g_here), es)
        turns_of_grads = chunks - 1 + len(last)
        reduces = [
            PlaneReduce(lambda h, j: acc.at[h, j], lambda h, n: inbox.at[h, n], bs, order)
            for order in b_orders
        ]
        keeps = {}

        def keep(name, src, dst):
            keeps[name] = pltpu.make_async_copy(src, dst, outs.at[len(keeps)])
            keeps[name].start()

        def share(mask):
            return remote(
                wkv_all.at[member], wkv_all.at[member], ks.at[0, mask], ks.at[1, mask],
                "expert", flipped(plane, mask),
            )

        gather.start()
        for k in range(first_grad):
            line.start(k)
        moves = gather.moves()
        for s in range(1, data):
            line.step(0, s)
        wanted = lax.broadcasted_iota(jnp.int32, (slots, rows), 0).astype(jnp.float32)
        for j in range(data):
            for peer in range(group):
                row = s_all[j, pl.ds(pl.multiple_of(place * group, 8), group)][peer : peer + 1]
                row = jnp.where(row >= 0, row + j * capacity, -1.0)
                select[pl.ds(peer * slots, slots), pl.ds(j * rows, rows)] = jnp.where(
                    wanted == row, 1.0, 0.0
                ).astype(jnp.bfloat16)
        for k in range(first_grad, min(first_grad + 2, first_out)):
            line.start(k)
        taken = 0
        turns = [(k, s) for k in range(1, first_grad) for s in range(1, data)]
        for at, (k, s) in enumerate(turns):
            until = len(moves) * (at + 1) // len(turns)
            for move in moves[taken:until]:
                gather.move(*move)
            taken = until
            line.step(k, s)
            if k == 1 and s == data - 1:
                for mask in range(1, sharing):
                    share(mask).start()
        for k in range(first_grad + 2, first_out):
            line.start(k)
        for mask in range(1, sharing):
            other = wkv_all.at[flipped(plane, mask) % sharing]
            remote(
                other, other, ks.at[0, mask], ks.at[1, mask], "expert", flipped(plane, mask)
            ).wait_recv()
        keep("select", select, sel_any)
        keep("x", x_all, x_any)
        keep("wq", wq_all, wq_any)
        keep("wkv", wkv_all, wkv_any)

        def x_block(rows_here, j):
            first = j * depth
            inner = first % width
            return x_all[first // width, rows_here, inner : inner + depth]

        def project(at, carry):
            here = pl.ds(pl.multiple_of(at * block, block), block)
            table = pl.ds(pl.multiple_of((at * block) % seq_len, block), block)
            cos_here, sin_here = cos_ref[table], sin_ref[table]
            blocks = [x_block(here, j) for j in range(data)]
            raw = sum(
                jnp.dot(blocks[j], wq_all[j], preferred_element_type=jnp.float32)
                for j in range(data)
            )
            q_raw[here] = raw
            for h in range(heads):
                one = raw[:, h * head : (h + 1) * head]
                one = one * row_scale(one) * gq_ref[...]
                turned = one * cos_here + half_turn(one) * sin_here
                q_low[here, h * head : (h + 1) * head] = turned.astype(jnp.bfloat16)
            kv = [sum(nt_dot(blocks[j], wkv_all[m, j]) for j in range(data)) for m in range(sharing)]
            raw = jnp.concatenate([item[:, :part] for item in kv], axis=1)
            k_raw[here] = raw
            one = raw * row_scale(raw) * gk_ref[...]
            k_low[here] = (one * cos_here + half_turn(one) * sin_here).astype(jnp.bfloat16)
            v_low[here] = jnp.concatenate([item[:, part:] for item in kv], axis=1).astype(
                jnp.bfloat16
            )
            return carry

        lax.fori_loop(0, total // block, project, 0)
        keep("q_raw", q_raw, qr_any)
        keep("q_low", q_low, ql_any)
        keep("k_raw", k_raw, kr_any)
        keep("k_low", k_low, kl_any)
        keep("v_low", v_low, vl_any)
        lane = lax.broadcasted_iota(jnp.int32, (block, head), 1)
        below = causal(0, block, block)
        lse[...] = jnp.zeros_like(lse)

        def send_grads(c):
            picked[c] = jnp.dot(
                select[...], g_all[c], preferred_element_type=jnp.float32
            ).astype(jnp.bfloat16)
            exchange.start(c)
            exchange.keep(c)

        def attend(h, carry):
            cols = pl.ds(pl.multiple_of(h * head, head), head)
            count = 0
            for seq in range(total // seq_len):
                base = seq * seq_len
                for at in range(seq_len // block):
                    here = pl.ds(base + at * block, block)
                    query = q_low[here, cols]
                    tiles = []
                    if at:
                        tiles.append(pl.ds(base, at * block))
                    tiles.append(here)
                    scores = [nt_dot(query, k_low[tile]) for tile in tiles]
                    scores[-1] = jnp.where(below, scores[-1], -jnp.inf)
                    top = jnp.max(scores[-1], axis=-1, keepdims=True)
                    if at:
                        top = jnp.maximum(top, jnp.max(scores[0], axis=-1, keepdims=True))
                    raised = [jnp.exp2((score - top) * (scale * LOG2_E)) for score in scores]
                    norm = sum(jnp.sum(item, axis=-1, keepdims=True) for item in raised)
                    inverse = 1.0 / norm
                    att[here, cols] = sum(
                        jnp.dot(
                            (item * inverse).astype(jnp.bfloat16),
                            v_low[tile],
                            preferred_element_type=jnp.float32,
                        )
                        for item, tile in zip(raised, tiles)
                    ).astype(jnp.bfloat16)
                    lse[here] = jnp.where(lane == h, top * scale + jnp.log(norm), lse[here])
                    count += 1
                    if count < data:

                        @pl.when(h < chunks - 1)
                        def _():
                            line.step(first_grad + h, count)

            @pl.when(h < chunks - 1)
            def _():
                for s in range(count + 1, data):
                    line.step(first_grad + h, s)
                send_grads(h)

            @pl.when(h == 0)
            def _():
                line.start(first_out)

            return carry

        lax.fori_loop(0, heads, attend, 0)
        keep("lse", lse, lse_any)
        keep("att", att, att_any)
        for c in range(heads, chunks - 1):
            for s in range(1, data):
                line.step(first_grad + c, s)
            send_grads(c)
        for k in range(first_last, items):
            line.start(k)

        def send_last(n):
            c, at, wide = last[n]
            picked[c, :, at : at + wide] = jnp.dot(
                select[...], g_all[c, :, at : at + wide], preferred_element_type=jnp.float32
            ).astype(jnp.bfloat16)
            exchange.start(chunks - 1 + n)
            exchange.keep(chunks - 1 + n)

        tail = []
        for n in range(len(last)):
            tail += [(n, s) for s in range(1, data)]

        def arrivals(s):
            if s == 0:
                return [(place, place >= 0, reduces[0])]
            return [
                (place - s, place >= s, reduces[(s + 1) % 2]),
                (place + s, place + s < data, reduces[s % 2]),
            ]

        def each(s, act):
            for j, present, reduce in arrivals(s):

                @pl.when(present)
                def _():
                    act(j, reduce)

        def project_out(j, reduce):
            acc[j] = (
                jnp.dot(att[...], wo_all[j], preferred_element_type=jnp.float32)
                .astype(jnp.bfloat16)
                .reshape(group, rows, cut)
            )
            reduce.start(j)

        for turn in range(data + steps):
            if turn < data:
                if turn:
                    line.step(first_out, turn)
                each(turn, project_out)
            for at in range(steps):
                if 0 <= turn - 1 - at < data:
                    each(turn - 1 - at, lambda j, reduce: reduce.advance(j, at))
            if turn >= data - 1:
                count = -(-len(tail) // (data + steps - turn))
                for n, s in tail[:count]:
                    line.step(first_last + n, s)
                    if s == data - 1:
                        send_last(n)
                tail = tail[count:]
        keep("wo", wo_all, wo_any)

        def branch_piece(j, reduce):
            reduce.result(j, hidden.at[:, pl.ds(pl.multiple_of(j * cut, cut), cut)])

        for s in range(data):
            each(s, branch_piece)
        summed = hidden[...] + tok_ref[...].astype(jnp.float32)
        hidden[...] = summed
        low = (summed * row_scale(summed) * gain2_ref[...]).astype(jnp.bfloat16)
        for c in range(chunks):
            second[c] = low[:, c * width : (c + 1) * width]
        logits = nt_dot(low, r_ref[...])
        masked = jnp.where(hot_ref[...] > 0, logits, -jnp.inf)
        raised = jnp.exp(masked - jnp.max(masked, axis=-1, keepdims=True))
        gate = raised / jnp.sum(raised, axis=-1, keepdims=True)
        probs[...] = gate
        top = gate.astype(jnp.bfloat16).astype(jnp.float32)
        parts = [top, gate - top]
        if extra > 2 * experts:
            parts.append(jnp.zeros((rows, extra - 2 * experts), jnp.float32))
        pair[...] = jnp.concatenate(parts, axis=1).astype(jnp.bfloat16)
        for k in range(turns_of_grads):
            exchange.wait(k)
        keep("g", g_here, g_any)
        for k in range(items):
            line.finish(k)
        gather.finish()
        for mask in range(1, sharing):
            share(mask).wait_send()
        for k in range(turns_of_grads):
            exchange.finish(k)
        for s in range(data):
            each(s, lambda j, reduce: reduce.finish(j))
        for copy in keeps.values():
            copy.wait()

    bf, fl = jnp.bfloat16, jnp.float32
    whole = pl.BlockSpec(memory_space=pltpu.VMEM)
    anywhere = pl.BlockSpec(memory_space=pl.ANY)

    def shape(*dims, dtype=bf):
        return jax.ShapeDtypeStruct(dims, dtype)

    kept = [
        shape(chunks, total, width),
        shape(data, depth, wide),
        shape(sharing, data, both, depth),
        shape(data, wide, cut),
        shape(chunks, entries, width),
        shape(entries, data * rows),
        shape(total, wide, dtype=fl),
        shape(total, wide),
        shape(total, head, dtype=fl),
        shape(total, head),
        shape(total, head),
        shape(total, head, dtype=fl),
        shape(total, wide),
    ]
    small = [
        shape(rows, model, dtype=fl),
        shape(chunks, rows, width),
        shape(rows, extra),
        shape(rows, experts, dtype=fl),
    ]
    return pl.pallas_call(
        kernel,
        out_shape=kept + small,
        in_specs=[whole] * 15,
        out_specs=[anywhere] * len(kept) + [whole] * len(small),
        scratch_shapes=[
            vmem((chunks, rows, width), bf),
            vmem((chunks, rows, width), bf),
            vmem((both, depth), bf),
            vmem((chunks, total, width), bf),
            vmem((data, depth, wide), bf),
            vmem((sharing, data, both, depth), bf),
            vmem((data, wide, cut), bf),
            vmem((chunks, data * rows, width), bf),
            vmem((data, experts, rows), fl),
            vmem((chunks, entries, width), bf),
            vmem((chunks, entries, width), bf),
            vmem((entries, data * rows), bf),
            vmem((total, wide), fl),
            vmem((total, wide), bf),
            vmem((total, head), fl),
            vmem((total, head), bf),
            vmem((total, head), bf),
            vmem((total, head), fl),
            vmem((total, wide), bf),
            vmem((data, group, rows, cut), bf),
            vmem((data, group - 1, rows, cut), bf),
            dma(2, chunks, group),
            dma(4, items, data - 1),
            dma(2, chunks - 1 + len(last), group),
            dma(2, sharing),
            dma(2, data, group - 1),
            dma(len(kept)),
        ],
        compiler_params=pltpu.CompilerParams(
            collective_id=1, has_side_effects=True, vmem_limit_bytes=VMEM_LIMIT
        ),
    )(
        tokens, gain, w_q, w_k, w_v, w_out, out_grad, slot_rows, cos, sin, gain_q, gain_k,
        gain2, router, hot,
    )


def local(
    tokens,
    norm1_gain,
    w_query,
    key_weight,
    value_weight,
    w_out,
    query_gain,
    key_gain,
    norm2_gain,
    w_router,
    w_gate,
    w_up,
    w_down,
    routes,
    out_grad,
):
    data_count = lax.axis_size("dp")
    group_count = lax.axis_size("expert")
    group_index = lax.axis_index("expert")
    local_rows = tokens.shape[0]
    model_width = tokens.shape[1]
    head_dim = query_gain.shape[0]
    heads_here = w_query.shape[1] // head_dim
    top_count = routes.shape[1]
    expert_total = data_count * group_count
    capacity = max(2, (local_rows * top_count * 9 + 8 * expert_total - 1) // (8 * expert_total))
    data_index = lax.axis_index("dp")
    own_expert = data_index * group_count + group_index
    expert_ids = jnp.arange(expert_total)
    hot = jnp.any(routes[:, :, None] == expert_ids[None, None, :], axis=1)
    earlier = (jnp.arange(local_rows)[:, None] > jnp.arange(local_rows)[None, :]).astype(jnp.bfloat16)
    rank = jnp.dot(earlier, hot.astype(jnp.bfloat16), preferred_element_type=jnp.float32)
    slot_rows = jnp.where(hot, rank, -1.0).T
    slots = whole_up(data_count * capacity, 16)
    width_k = key_weight.shape[1]
    all_rows = group_count * local_rows
    seq_len = min(SEQ_LEN, all_rows)
    router = w_router.T
    cos_rows, sine_rows = [jnp.asarray(table) for table in rope_arrays(seq_len, head_dim)]
    (
        gathered, q_blocks, kv_blocks, out_blocks, grads_here, select, query_raw, queries, key_raw,
        keys_low, values_low, log_sum, attended, hidden, second, pair, gate_probs,
    ) = front(
        tokens, norm1_gain[None], w_query, key_weight.T, value_weight.T, w_out, out_grad, slot_rows,
        cos_rows, sine_rows, query_gain[None], key_gain[None], norm2_gain[None], router,
        hot.astype(jnp.float32), capacity, slots, seq_len,
    )
    q_cols = q_blocks.reshape(model_width, -1)
    with_mix = all_rows <= group_count * slots
    (
        grad_h, grad_arrived, act, mixed, grad_hidden, grad_branch, grad_norm2, grad_router,
        turned, first_mix,
    ) = expert_layer(
        second, pair, gate_probs, hidden, out_grad, norm2_gain[None], router, select, grads_here,
        w_gate[0], w_up[0], w_down[0], out_blocks.shape[2], with_mix,
    )
    (
        grad_tokens, grad_wo, grad_wq, grad_wkv, grad_query_gain, grad_key_gain, grad_norm1,
        grad_norm2, grad_router, output,
    ) = attention_backward(
        grad_branch, out_blocks, gathered, q_cols, kv_blocks, query_raw, queries, key_raw, keys_low,
        values_low, log_sum, attended, cos_rows, sine_rows, query_gain[None], key_gain[None],
        mixed, turned, tokens, norm1_gain[None], grad_hidden, hidden, grad_norm2, grad_router, first_mix,
        seq_len, with_mix,
    )
    if not with_mix:
        output = (hidden + combine(mixed, select, slots, 5)).astype(jnp.bfloat16)
    (
        grad_gate_w, grad_up_w, grad_down, output, grad_tokens, grad_wq, grad_wo, grad_router,
        grad_wk, grad_wv, grad_norm1, grad_norm2, grad_query_gain, grad_key_gain,
    ) = expert_weight_grads(
        grad_h, grad_arrived, act, [output, grad_tokens, grad_wq, grad_wo, grad_router], grad_wkv,
        [grad_norm1, grad_norm2, grad_query_gain, grad_key_gain],
    )
    return (
        output,
        grad_tokens,
        grad_norm1.reshape(-1),
        grad_wq,
        grad_wk.T,
        grad_wv.T,
        grad_wo,
        grad_query_gain.reshape(-1),
        grad_key_gain.reshape(-1),
        grad_norm2.reshape(-1),
        grad_router.T,
        grad_gate_w,
        grad_up_w,
        grad_down,
    )


def solution(mesh):
    placed = (
        P(("dp", "expert"), None),
        P(),
        P("dp", "expert"),
        P("dp", "expert"),
        P("dp", "expert"),
        P("expert", "dp"),
        P(),
        P(),
        P(),
        P(),
        P(("dp", "expert"), None, None),
        P(("dp", "expert"), None, None),
        P(("dp", "expert"), None, None),
        P(("dp", "expert"), None),
        P(("dp", "expert"), None),
    )
    return jax.shard_map(
        local,
        mesh=mesh,
        in_specs=placed,
        out_specs=(
            P(("dp", "expert"), None),
            P(("dp", "expert"), None),
            P(),
            P("dp", "expert"),
            P("dp", "expert"),
            P("dp", "expert"),
            P("expert", "dp"),
            P(),
            P(),
            P(),
            P(),
            P(("dp", "expert"), None, None),
            P(("dp", "expert"), None, None),
            P(("dp", "expert"), None, None),
        ),
        check_vma=False,
    )
```

```python
import jax
import jax.numpy as jnp
import numpy as np
from jax import lax
from jax.experimental import pallas as pl
from jax.experimental.pallas import tpu as pltpu
from jax.sharding import PartitionSpec as P

SEQ_LEN = 1024


NORM_EPS = 1e-06
ROPE_THETA = 1000000.0
LOG2_E = 1.4426950408889634


def whole_up(value, unit):
    return -(-value // unit) * unit


def whole_up(value, unit):
    return -(-value // unit) * unit


VMEM_LIMIT = 61 * 1024 * 1024


def flipped(index, mask):
    moved = index
    bit = 1
    while bit <= mask:
        if mask & bit:
            moved = moved + bit * (1 - 2 * ((index // bit) % 2))
        bit *= 2
    return moved


def remote(src, dst, send_sem, recv_sem, axis, target):
    return pltpu.make_async_remote_copy(
        src_ref=src,
        dst_ref=dst,
        send_sem=send_sem,
        recv_sem=recv_sem,
        device_id={axis: target},
        device_id_type=pl.DeviceIdType.MESH,
    )


def greet(line=True, plane=True, far=False):
    barrier = pltpu.get_barrier_semaphore()
    count = 0
    if line:
        size, me = lax.axis_size("dp"), lax.axis_index("dp")
        for step in range(1, size) if far else (1, size - 1):
            pl.semaphore_signal(
                barrier,
                inc=1,
                device_id={"dp": (me + step) % size},
                device_id_type=pl.DeviceIdType.MESH,
            )
            count += 1
    if plane:
        size, me = lax.axis_size("expert"), lax.axis_index("expert")
        for mask in range(1, size):
            pl.semaphore_signal(
                barrier,
                inc=1,
                device_id={"expert": flipped(me, mask)},
                device_id_type=pl.DeviceIdType.MESH,
            )
            count += 1
    pl.semaphore_wait(barrier, count)


class LineGather:
    def __init__(self, own, slot, sems):
        self.size, self.me = lax.axis_size("dp"), lax.axis_index("dp")
        self.own, self.slot, self.sems = own, slot, sems

    def copy(self, way, k, s, src, block):
        target = self.me + 1 if way == 0 else self.me - 1
        dst = self.slot(k, block)
        return remote(src, dst, self.sems.at[way, k, s], self.sems.at[2 + way, k, s], "dp", target)

    def can_send(self, way, s):
        if way == 0:
            return (self.me < self.size - 1) & (self.me - s >= 0)
        return (self.me > 0) & (self.me + s < self.size)

    def start(self, k):
        for way in range(2):

            @pl.when(self.can_send(way, 0))
            def _():
                self.copy(way, k, 0, self.own(k), self.me).start()

    def step(self, k, s):
        for way in range(2):
            block = self.me - s if way == 0 else self.me + s
            present = block >= 0 if way == 0 else block < self.size

            @pl.when(present)
            def _():
                self.copy(way, k, s - 1, self.slot(k, block), block).wait_recv()

            if s < self.size - 1:

                @pl.when(self.can_send(way, s))
                def _():
                    self.copy(way, k, s, self.slot(k, block), block).start()

    def finish(self, k):
        for s in range(self.size - 1):
            for way in range(2):

                @pl.when(self.can_send(way, s))
                def _():
                    self.copy(way, k, s, self.own(k), self.me).wait_send()

    def run(self, count, window, done):
        for k in range(min(window, count)):
            self.start(k)
        for k in range(count):
            for s in range(1, self.size):
                self.step(k, s)
            if k + window < count:
                self.start(k + window)
            done(k)
        for k in range(count):
            self.finish(k)


class LineReduce:
    def __init__(self, part, inbox, sems):
        self.size, self.me = lax.axis_size("dp"), lax.axis_index("dp")
        self.part, self.inbox, self.sems = part, inbox, sems

    def copy(self, way, k, j):
        target = self.me + 1 if way == 0 else self.me - 1
        return remote(
            self.part(k, j),
            self.inbox(way, k, j),
            self.sems.at[way, k, j],
            self.sems.at[2 + way, k, j],
            "dp",
            target,
        )

    def begin(self, k):
        last = self.size - 1
        for turn in range(last):
            for way, j, end in ((0, last - turn, 0), (1, turn, last)):

                @pl.when(self.me == end)
                def _():
                    self.copy(way, k, j).start()

    def begin_block(self, k, j):
        for way, end in ((0, 0), (1, self.size - 1)):
            if j != end:

                @pl.when(self.me == end)
                def _():
                    self.copy(way, k, j).start()

    def sweep(self, k, way):
        last = self.size - 1
        for turn in range(last):
            j = last - turn if way == 0 else turn
            inner = (self.me > 0) if way == 0 else (self.me < last)
            passing = (j > self.me) if way == 0 else (j < self.me)

            @pl.when(inner & (passing | (self.me == j)))
            def _():
                self.copy(way, k, j).wait_recv()

            @pl.when(inner & passing)
            def _():
                total = self.part(k, j)[...].astype(jnp.float32) + self.inbox(way, k, j)[
                    ...
                ].astype(jnp.float32)
                self.part(k, j)[...] = total.astype(self.part(k, j).dtype)
                self.copy(way, k, j).start()

    def near(self, k):
        @pl.when(self.me < self.size // 2)
        def _():
            self.sweep(k, 0)

        @pl.when(self.me >= self.size // 2)
        def _():
            self.sweep(k, 1)

    def far(self, k):
        @pl.when(self.me < self.size // 2)
        def _():
            self.sweep(k, 1)

        @pl.when(self.me >= self.size // 2)
        def _():
            self.sweep(k, 0)

    def result(self, k, out):
        last = self.size - 1
        out[...] = self.part(k, self.me)[...].astype(jnp.float32)

        @pl.when(self.me > 0)
        def _():
            out[...] += self.inbox(0, k, self.me)[...].astype(jnp.float32)

        @pl.when(self.me < last)
        def _():
            out[...] += self.inbox(1, k, self.me)[...].astype(jnp.float32)

    def finish(self, k):
        last = self.size - 1
        for j in range(self.size):
            for way in range(2):
                sent = (j > self.me) if way == 0 else (j < self.me)

                @pl.when(sent)
                def _():
                    self.copy(way, k, j).wait_send()


def bit_orders(size):
    bits = [1 << i for i in range(size.bit_length() - 1)]
    bits.reverse()
    half = max(1, len(bits) // 2)
    if len(bits) == 3:
        return [bits, [bits[1], bits[0], bits[2]]]
    return [bits, bits[half:] + bits[:half]]


class PlaneGather:
    def __init__(self, own, slot, sems, orders):
        self.size, self.me = lax.axis_size("expert"), lax.axis_index("expert")
        self.own, self.slot, self.sems, self.orders = own, slot, sems, orders

    def place(self, h, mask):
        return max(at for at, bit in enumerate(self.orders[h]) if mask & bit)

    def copy(self, h, mask):
        last = self.orders[h][self.place(h, mask)]
        block = flipped(self.me, mask - last)
        src = self.own(h) if mask == last else self.slot(h, block)
        return remote(
            src,
            self.slot(h, block),
            self.sems.at[0, h, mask],
            self.sems.at[1, h, mask],
            "expert",
            flipped(self.me, last),
        )

    def wait(self, h, mask):
        here = self.slot(h, flipped(self.me, mask))
        remote(
            here, here, self.sems.at[0, h, mask], self.sems.at[1, h, mask], "expert", flipped(self.me, 1)
        ).wait_recv()

    def start(self, some=None):
        for at in range(len(self.orders[0])):
            for h, order in enumerate(self.orders):
                if some is None or h in some:
                    self.copy(h, order[at]).start()

    def moves(self):
        found = [(h, mask) for h in range(len(self.orders)) for mask in range(1, self.size)]
        found.sort(key=lambda move: (move[1].bit_count(), self.place(*move), move[0]))
        return found

    def move(self, h, mask):
        self.wait(h, mask)
        for bit in self.orders[h][self.place(h, mask) + 1 :]:
            self.copy(h, mask | bit).start()

    def relay(self):
        for h, mask in self.moves():
            self.move(h, mask)

    def finish(self):
        for h in range(len(self.orders)):
            for mask in range(1, self.size):
                self.copy(h, mask).wait_send()


class PlaneReduce:
    def __init__(self, acc, inbox, sems, orders):
        self.size, self.me = lax.axis_size("expert"), lax.axis_index("expert")
        self.acc, self.inbox, self.sems, self.orders = acc, inbox, sems, orders

    def masks(self, h, at):
        later = self.orders[h][at + 1 :]
        found = [0]
        for bit in later:
            found = found + [mask | bit for mask in found]
        return sorted(found, key=lambda mask: (mask == 0, self.first(h, mask) if mask else 0))

    def first(self, h, mask):
        return min(at for at, bit in enumerate(self.orders[h]) if mask & bit)

    def number(self, h, at, mask):
        before = sum(self.size >> (step + 1) for step in range(at))
        return before + sorted(self.masks(h, at)).index(mask)

    def copy(self, h, at, mask):
        bit = self.orders[h][at]
        n = self.number(h, at, mask)
        return remote(
            self.acc(h, flipped(self.me, mask | bit)),
            self.inbox(h, n),
            self.sems.at[0, h, n],
            self.sems.at[1, h, n],
            "expert",
            flipped(self.me, bit),
        )

    def start(self, h):
        for mask in self.masks(h, 0):
            self.copy(h, 0, mask).start()

    def advance(self, h, at):
        for mask in self.masks(h, at):
            self.copy(h, at, mask).wait_recv()
            if mask:
                here = self.acc(h, flipped(self.me, mask))
                arrived = self.inbox(h, self.number(h, at, mask))
                here[...] = (
                    here[...].astype(jnp.float32) + arrived[...].astype(jnp.float32)
                ).astype(here.dtype)
                if self.first(h, mask) == at + 1:
                    self.copy(h, at + 1, mask - self.orders[h][at + 1]).start()

    def result(self, h, out):
        total = self.acc(h, self.me)[...].astype(jnp.float32)
        for at in range(len(self.orders[h])):
            total = total + self.inbox(h, self.number(h, at, 0))[...].astype(jnp.float32)
        out[...] = total

    def finish(self, h):
        for at in range(len(self.orders[h])):
            for mask in self.masks(h, at):
                self.copy(h, at, mask).wait_send()


def part_of(ref, item, rows, width):
    chunk, low, wide = item
    if wide == width:
        return ref.at[chunk, rows]
    return ref.at[chunk, rows, pl.ds(low, wide)]


def halved(chunks, width, at):
    items = []
    for c in range(chunks):
        if c == at and width >= 256:
            items += [(c, 0, width // 2), (c, width // 2, width // 2)]
        else:
            items.append((c, 0, width))
    return items


def vmem(shape, dtype):
    return pltpu.VMEM(shape, dtype)


def dma(*shape):
    return pltpu.SemaphoreType.DMA(shape)


def call(kernel, outs, scratch, number, *operands):
    whole = pl.BlockSpec(memory_space=pltpu.VMEM)
    return pl.pallas_call(
        kernel,
        out_shape=outs,
        in_specs=[whole] * len(operands),
        out_specs=jax.tree.map(lambda _: whole, outs),
        scratch_shapes=scratch,
        compiler_params=pltpu.CompilerParams(
            collective_id=number, has_side_effects=True, vmem_limit_bytes=VMEM_LIMIT
        ),
    )(*operands)


class PlaneExchange:
    def __init__(self, src, dst, sems):
        self.size, self.me = lax.axis_size("expert"), lax.axis_index("expert")
        self.src, self.dst, self.sems = src, dst, sems

    def copy(self, k, peer):
        return remote(
            self.src(k, peer),
            self.dst(k, self.me),
            self.sems.at[0, k, peer],
            self.sems.at[1, k, self.me],
            "expert",
            peer,
        )

    def peers(self):
        order = sorted(range(1, self.size), key=lambda mask: (mask == 1, -mask.bit_count()))
        return [flipped(self.me, mask) for mask in order]

    def start(self, k):
        for peer in self.peers():
            self.copy(k, peer).start()

    def keep(self, k):
        self.dst(k, self.me)[...] = self.src(k, self.me)[...]

    def wait(self, k):
        for peer in self.peers():
            here = self.dst(k, peer)
            remote(
                here, here, self.sems.at[0, k, peer], self.sems.at[1, k, peer], "expert", peer
            ).wait_recv()

    def finish(self, k):
        for peer in self.peers():
            self.copy(k, peer).wait_send()


def combine(values, select, slots, number):
    data, group = lax.axis_size("dp"), lax.axis_size("expert")
    chunks, entries, width = values.shape
    rows = select.shape[1] // data
    window = 1

    def kernel(v_ref, select, out_ref, turned, back, part, inbox, ls, es):
        greet()
        exchange = PlaneExchange(
            lambda k, p: v_ref.at[k, pl.ds(pl.multiple_of(p * slots, slots), slots)],
            lambda k, p: back.at[k, pl.ds(pl.multiple_of(p * slots, slots), slots)],
            es,
        )
        line = LineReduce(
            lambda k, j: part.at[k, pl.ds(pl.multiple_of(j * rows, rows), rows)],
            lambda way, k, j: inbox.at[k, j + 1 - way],
            ls,
        )
        for k in range(window):
            exchange.start(k)
        turned[...] = select[...].T
        for k in range(chunks):
            exchange.keep(k)
        for k in range(chunks):
            exchange.wait(k)
            if k + window < chunks:
                exchange.start(k + window)
            total = jnp.dot(
                turned[...], back[k], preferred_element_type=jnp.float32
            )
            part[k] = total.astype(jnp.bfloat16)
            line.begin(k)
            line.near(k)
            if k:
                line.far(k - 1)
        line.far(chunks - 1)
        for k in range(chunks):
            line.result(k, out_ref.at[:, pl.ds(k * width, width)])
            line.finish(k)
            exchange.finish(k)

    return call(
        kernel,
        jax.ShapeDtypeStruct((rows, chunks * width), jnp.float32),
        [
            vmem(select.shape[::-1], jnp.bfloat16),
            vmem(values.shape, jnp.bfloat16),
            vmem((chunks, data * rows, width), jnp.bfloat16),
            vmem((chunks, data + 1, rows, width), jnp.bfloat16),
            dma(4, chunks, data),
            dma(2, chunks, group),
        ],
        number,
        values,
        select,
    )


def expert_layer(
    second, pair, probs, hidden, out_grad, gain, w_router, select, grads_here,
    w_gate, w_up, w_down, cut, with_mix,
):
    data, group = lax.axis_size("dp"), lax.axis_size("expert")
    chunks, rows, width = second.shape
    model = chunks * width
    experts = w_router.shape[0]
    extra = pair.shape[1]
    entries = select.shape[0]
    slots = entries // group
    hidden_units = w_gate.shape[1]
    block = 2 * slots
    pieces = model // cut
    early = max(1, chunks // 2)
    came = halved(chunks, width, 0)
    sent = halved(chunks, width, chunks - 1)

    def kernel(
        sec_ref, pair_ref, prob_ref, hid_ref, g_ref, gain_ref, r_ref, select, gh_any, wg_any, wu_any, wd_any,
        d_any, s_any, a_any, v_any, grad_hidden, branch_any, norm_sum, router_sum, turned_any, mix_out,
        x_all, pair_all, picked_pair, pair_here, rows_out, pair_out, back, pair_back,
        inbox, pair_box, summed, pair_sum, turned, low, wg, wu, wd,
        x_here, g_stage, s_stage, v_stage, a_stage, grad_h, d_stage,
        mix_back, loads, g_load, stores, keeps, d_s, ls, es, ls2, es2, es3,
    ):
        place, plane = lax.axis_index("dp"), lax.axis_index("expert")
        own = place * group + plane
        pairs = group // 2
        fetches = [
            pltpu.make_async_copy(src, dst, loads.at[at])
            for at, (src, dst) in enumerate(((wg_any, wg), (wu_any, wu), (wd_any, wd)))
        ]

        def block_at(step):
            mask, at, bit = pairs - 1 - step, 0, 1
            while bit < pairs:
                at = at + bit * ((plane // (2 * bit) + mask // bit) % 2)
                bit *= 2
            return at

        def block_rows(step):
            at = block_at(step)
            return pl.ds(pl.multiple_of(at * block, block), block)

        def load_grads(step):
            slot = step % 2
            return pltpu.make_async_copy(
                gh_any.at[:, block_rows(step)], g_stage.at[slot], g_load.at[slot]
            )

        def store_block(step):
            slot, here = step % 2, block_rows(step)
            return [
                pltpu.make_async_copy(s_stage.at[slot], s_any.at[:, here], stores.at[slot, 0]),
                pltpu.make_async_copy(v_stage.at[slot], v_any.at[:, here], stores.at[slot, 1]),
                pltpu.make_async_copy(a_stage.at[slot], a_any.at[here], stores.at[slot, 2]),
            ]

        load_grads(0).start()
        for fetch in fetches:
            fetch.start()
        mine = pl.ds(pl.multiple_of(place * rows, rows), rows)
        for c in range(chunks):
            x_all[c, mine] = sec_ref[c]
        pair_all[mine] = pair_ref[...]
        greet()

        def slot_rows(p):
            return pl.ds(pl.multiple_of(p * slots, slots), slots)

        def token_rows(j):
            return pl.ds(pl.multiple_of(j * rows, rows), rows)

        def pick(items, full, wide):
            return lambda k, p: (
                part_of(full, items[k], slot_rows(p), width)
                if k < len(items)
                else wide.at[slot_rows(p)]
            )

        exchange = PlaneExchange(
            pick(came, rows_out, picked_pair), pick(came, x_here, pair_here), es
        )

        def done(k):
            if k == 0:
                picked_pair[...] = jnp.dot(
                    select[...], pair_all[...], preferred_element_type=jnp.float32
                ).astype(jnp.bfloat16)
                exchange.start(len(came))
                exchange.keep(len(came))
            else:
                c, at, wide = came[k - 1]
                rows_out[c, :, at : at + wide] = jnp.dot(
                    select[...], x_all[c, :, at : at + wide], preferred_element_type=jnp.float32
                ).astype(jnp.bfloat16)
                exchange.start(k - 1)
                exchange.keep(k - 1)

        line = LineGather(
            lambda k: (
                pair_ref if k == 0 else part_of(sec_ref, came[k - 1], pl.ds(0, rows), width)
            ),
            lambda k, j: (
                pair_all.at[token_rows(j)]
                if k == 0
                else part_of(x_all, came[k - 1], token_rows(j), width)
            ),
            ls,
        )
        line.run(len(came) + 1, 3, done)
        turned[...] = select[...].T
        keep_turned = pltpu.make_async_copy(turned, turned_any, keeps.at[2])
        keep_turned.start()
        for fetch in fetches:
            fetch.wait()
        for k in range(len(came) + 1):
            exchange.wait(k)
        for k in range(len(came) + 1):
            exchange.finish(k)

        give_back = PlaneExchange(
            pick(sent, rows_out, pair_out), pick(sent, back, pair_back), es2
        )
        lane = lax.broadcasted_iota(jnp.int32, (block, extra), 1)

        def run_block(step, carry):
            at = block_at(step)
            here = block_rows(step)
            slot = step % 2
            load_grads(step).wait()

            @pl.when(step + 1 < pairs)
            def _():
                load_grads(step + 1).start()

            @pl.when(step >= 2)
            def _():
                for store in store_block(step - 2):
                    store.wait()

            chosen = (lane == own) | (lane == own + experts)
            prob = jnp.sum(
                jnp.where(chosen, pair_here[here].astype(jnp.float32), 0.0), axis=-1, keepdims=True
            )
            gate_h = jnp.zeros((block, hidden_units), jnp.float32)
            up_h = jnp.zeros((block, hidden_units), jnp.float32)
            for c in range(chunks):
                x = x_here[c, here]
                part = pl.ds(c * width, width)
                gate_h += jnp.dot(x, wg[part], preferred_element_type=jnp.float32)
                up_h += jnp.dot(x, wu[part], preferred_element_type=jnp.float32)
            sigmoid = jax.nn.sigmoid(gate_h)
            silu = gate_h * sigmoid
            active = (silu * up_h).astype(jnp.bfloat16)
            a_stage[slot] = active
            grad_active = jnp.zeros((block, hidden_units), jnp.float32)
            slot_gate = jnp.zeros((block, 1), jnp.float32)
            for c in range(chunks):
                part = pl.ds(c * width, width)
                out = jnp.dot(active, wd[:, part], preferred_element_type=jnp.float32)
                out = out.astype(jnp.bfloat16).astype(jnp.float32)
                grad = g_stage[slot, c].astype(jnp.float32)
                slot_gate += jnp.sum(out * grad, axis=-1, keepdims=True)
                v_stage[slot, c] = (prob * out).astype(jnp.bfloat16)
                grad_slot = (prob * grad).astype(jnp.bfloat16)
                s_stage[slot, c] = grad_slot
                grad_active += nt_dot(grad_slot, wd[:, part])
            grad_gate_h = grad_active * up_h * sigmoid * (1.0 + gate_h * (1.0 - sigmoid))
            grad_gate_h = grad_gate_h.astype(jnp.bfloat16)
            grad_up_h = (grad_active * silu).astype(jnp.bfloat16)
            grad_h[0, here] = grad_gate_h
            grad_h[1, here] = grad_up_h
            for store in store_block(step):
                store.start()
            top = slot_gate.astype(jnp.bfloat16).astype(jnp.float32)
            pair_out[here] = (
                jnp.where(lane == own, top, 0.0)
                + jnp.where(lane == own + experts, slot_gate - top, 0.0)
            ).astype(jnp.bfloat16)
            for c in range(chunks):
                part = pl.ds(c * width, width)
                rows_out[c, here] = (
                    nt_dot(grad_gate_h, wg[part]) + nt_dot(grad_up_h, wu[part])
                ).astype(jnp.bfloat16)
            for member in range(2):
                peer = 2 * at + member

                @pl.when(peer != plane)
                def _():
                    for k in [len(sent)] + list(range(early)):
                        give_back.copy(k, peer).start()

            return carry

        lax.fori_loop(0, pairs, run_block, 0)
        def store_grads(c, side):
            return pltpu.make_async_copy(
                d_stage.at[side], d_any.at[side, pl.ds(c * width, width)], d_s.at[side]
            )

        def weight_grads(c):
            x = x_here[c].T
            for side in range(2):
                if c:
                    store_grads(c - 1, side).wait()
                d_stage[side] = jnp.dot(
                    x, grad_h[side], preferred_element_type=jnp.float32
                ).astype(jnp.bfloat16)
                store_grads(c, side).start()

        for step in range(max(0, pairs - 2), pairs):
            for store in store_block(step):
                store.wait()
        mix = PlaneExchange(
            lambda k, p: v_any.at[0, slot_rows(p)], lambda k, p: mix_back.at[slot_rows(p)], es3
        )
        own_mix = pltpu.make_async_copy(
            v_any.at[0, slot_rows(plane)], mix_back.at[slot_rows(plane)], keeps.at[3]
        ) if with_mix else None
        give_back.start(early)
        for k in range(len(sent) + 1):
            give_back.keep(k)
        sums = LineReduce(
            lambda k, j: (
                part_of(x_all, sent[k], token_rows(j), width)
                if k < len(sent)
                else pair_all.at[token_rows(j)]
            ),
            lambda way, k, j: (
                inbox.at[
                    sent[k][0], j + 1 - way, :, pl.ds(sent[k][1], sent[k][2])
                ]
                if k < len(sent)
                else pair_box.at[j + 1 - way]
            ),
            ls2,
        )
        order = [len(sent)] + list(range(len(sent)))

        def collect(k):
            if k < len(sent):
                c, low_col, wide = sent[k]
                sums.result(k, summed.at[:, pl.ds(c * width + low_col, wide)])
            else:
                sums.result(k, pair_sum)

        for at, k in enumerate(order):
            give_back.wait(k)
            if k < len(sent):
                c, low_col, wide = sent[k]
                x_all[c, :, low_col : low_col + wide] = jnp.dot(
                    turned[...],
                    back[c, :, low_col : low_col + wide],
                    preferred_element_type=jnp.float32,
                ).astype(jnp.bfloat16)
            else:
                pair_all[...] = jnp.dot(
                    turned[...], pair_back[...], preferred_element_type=jnp.float32
                ).astype(jnp.bfloat16)
            sums.begin(k)
            if k < len(sent) and early + 1 + k < len(sent):
                give_back.start(early + 1 + k)
            if at >= 1:
                sums.near(order[at - 1])
            if at >= 2:
                sums.far(order[at - 2])
                collect(order[at - 2])
            if at < chunks:
                weight_grads(at)
        if with_mix:
            mix.start(0)
            own_mix.start()
        sums.near(order[-1])
        for k in order[-2:]:
            sums.far(k)
            collect(k)

        gate = prob_ref[...]
        grad_gate = pair_sum[:, 0:experts] + pair_sum[:, experts : 2 * experts]
        inner = jnp.sum(gate * grad_gate, axis=-1, keepdims=True)
        grad_logits = (gate * (grad_gate - inner)).astype(jnp.bfloat16)
        for c in range(chunks):
            part = pl.ds(c * width, width)
            router_sum[:, part] = lax.dot_general(
                grad_logits,
                sec_ref[c],
                (((0,), (0,)), ((), ())),
                preferred_element_type=jnp.float32,
            )
        grad_second = summed[...] + jnp.dot(
            grad_logits, r_ref[...], preferred_element_type=jnp.float32
        )
        state = hid_ref[...]
        scale = row_scale(state)
        norm_sum[...] = jnp.sum(grad_second * state * scale, axis=0, keepdims=True)
        scaled = grad_second * gain_ref[...]
        inner = jnp.mean(scaled * state, axis=-1, keepdims=True)
        total = scale * scaled - state * (scale * scale * scale * inner)
        total = total + g_ref[...].astype(jnp.float32)
        grad_hidden[...] = total
        total = total.astype(jnp.bfloat16)
        for piece in range(pieces):
            low[piece] = total[:, piece * cut : (piece + 1) * cut]
        keep_low = pltpu.make_async_copy(low, branch_any, keeps.at[1])
        keep_low.start()
        if with_mix:
            own_mix.wait()
            mix.wait(0)
            mix_out[...] = jnp.dot(
                turned[...], mix_back[...], preferred_element_type=jnp.float32
            ).astype(jnp.bfloat16)
            mix.finish(0)
        for side in range(2):
            store_grads(chunks - 1, side).wait()
        keep_turned.wait()
        keep_low.wait()
        for k in range(len(sent) + 1):
            sums.finish(k)
            give_back.finish(k)

    bf, fl = jnp.bfloat16, jnp.float32
    whole = pl.BlockSpec(memory_space=pltpu.VMEM)
    anywhere = pl.BlockSpec(memory_space=pl.ANY)
    outs = [
        jax.ShapeDtypeStruct((2, model, hidden_units), bf),
        jax.ShapeDtypeStruct((chunks, entries, width), bf),
        jax.ShapeDtypeStruct((entries, hidden_units), bf),
        jax.ShapeDtypeStruct((chunks, entries, width), bf),
        jax.ShapeDtypeStruct((rows, model), fl),
        jax.ShapeDtypeStruct((pieces, rows, cut), bf),
        jax.ShapeDtypeStruct((1, model), fl),
        jax.ShapeDtypeStruct((experts, model), fl),
        jax.ShapeDtypeStruct(select.shape[::-1], bf),
        jax.ShapeDtypeStruct((data * rows if with_mix else 16, width), bf),
    ]
    results = list(pl.pallas_call(
        kernel,
        out_shape=outs,
        in_specs=[whole] * 8 + [anywhere] * 4,
        out_specs=[anywhere] * 4 + [whole, anywhere, whole, whole, anywhere, whole],
        scratch_shapes=[
            vmem((chunks, data * rows, width), bf),
            vmem((data * rows, extra), bf),
            vmem((entries, extra), bf),
            vmem((entries, extra), bf),
            vmem((chunks, entries, width), bf),
            vmem((entries, extra), bf),
            vmem((chunks, entries, width), bf),
            vmem((entries, extra), bf),
            vmem((chunks, data + 1, rows, width), bf),
            vmem((data + 1, rows, extra), bf),
            vmem((rows, model), fl),
            vmem((rows, extra), fl),
            vmem(select.shape[::-1], bf),
            vmem((pieces, rows, cut), bf),
            vmem((model, hidden_units), bf),
            vmem((model, hidden_units), bf),
            vmem((hidden_units, model), bf),
            vmem((chunks, entries, width), bf),
            vmem((2, chunks, block, width), bf),
            vmem((2, chunks, block, width), bf),
            vmem((2, chunks, block, width), bf),
            vmem((2, block, hidden_units), bf),
            vmem((2, entries, hidden_units), bf),
            vmem((2, width, hidden_units), bf),
            vmem((entries if with_mix else 16, width), bf),
            dma(3),
            dma(2),
            dma(2, 3),
            dma(4),
            dma(2),
            dma(4, len(came) + 1, data - 1),
            dma(2, len(came) + 1, group),
            dma(4, len(sent) + 1, data),
            dma(2, len(sent) + 1, group),
            dma(2, 1, group),
        ],
        compiler_params=pltpu.CompilerParams(
            collective_id=3, has_side_effects=True, vmem_limit_bytes=VMEM_LIMIT
        ),
    )(
        second, pair, probs, hidden, out_grad, gain, w_router, select, grads_here,
        w_gate, w_up, w_down,
    ))
    return results


def expert_weight_grads(grad_h, grad_arrived, act, others, kv, small):
    chunks, entries, width = grad_arrived.shape
    hidden_units = act.shape[1]
    part = kv.shape[0] // 2
    passed = len(others) + 2 + len(small)

    def kernel(h_ref, s_ref, act_ref, *refs):
        sources = refs[:passed]
        gate_out, up_out, down_out = refs[passed : passed + 3]
        targets = refs[passed + 3 : 2 * passed + 3]
        turned = refs[2 * passed + 3]

        @pl.when(pl.program_id(0) == 0)
        def _():
            turned[...] = act_ref[...].T

        for source, target in zip(sources, targets):
            target[...] = source[...]
        gate_out[0] = h_ref[0].astype(jnp.float32)
        up_out[0] = h_ref[1].astype(jnp.float32)
        down_out[0] = jnp.dot(turned[...], s_ref[0], preferred_element_type=jnp.float32)

    tall = pl.BlockSpec((1, width, hidden_units), lambda c: (0, c, 0))

    def slab(lines, item, first=0):
        return pl.BlockSpec((lines // chunks, item.shape[1]), lambda c: (c + first, 0))

    slabs = [slab(item.shape[0], item) for item in others]
    half = slab(part, kv)
    whole = [pl.BlockSpec(item.shape, lambda c: (0, 0)) for item in small]
    return pl.pallas_call(
        kernel,
        grid=(chunks,),
        out_shape=[
            jax.ShapeDtypeStruct((1, chunks * width, hidden_units), jnp.float32),
            jax.ShapeDtypeStruct((1, chunks * width, hidden_units), jnp.float32),
            jax.ShapeDtypeStruct((1, hidden_units, chunks * width), jnp.float32),
        ]
        + [jax.ShapeDtypeStruct(item.shape, item.dtype) for item in others]
        + [jax.ShapeDtypeStruct((part, kv.shape[1]), kv.dtype)] * 2
        + [jax.ShapeDtypeStruct(item.shape, item.dtype) for item in small],
        in_specs=[
            pl.BlockSpec((2, width, hidden_units), lambda c: (0, c, 0)),
            pl.BlockSpec((1, entries, width), lambda c: (c, 0, 0)),
            pl.BlockSpec((entries, hidden_units), lambda c: (0, 0)),
        ]
        + slabs
        + [half, slab(part, kv, chunks)]
        + whole,
        out_specs=[tall, tall, pl.BlockSpec((1, hidden_units, width), lambda c: (0, 0, c))]
        + slabs
        + [half, half]
        + whole,
        scratch_shapes=[vmem((hidden_units, entries), jnp.bfloat16)],
        compiler_params=pltpu.CompilerParams(vmem_limit_bytes=VMEM_LIMIT),
    )(grad_h, grad_arrived, act, *others, kv, kv, *small)


def attention_backward(
    grad_branch, out_blocks, x, w_q, w_kv, q_raw, q_low, k_raw, k_low, v_low, lse, att,
    cos, sin, gain_q, gain_k, mixed, turned, tokens, gain, grad_hidden, hidden, norm2_sum, router_sum, first_mix,
    seq_len, with_mix,
):
    data, group = lax.axis_size("dp"), lax.axis_size("expert")
    pieces, rows, cut = grad_branch.shape
    chunks, total, width = x.shape
    model = chunks * width
    depth = model // data
    wide = w_q.shape[1]
    sharing, _, both, _ = w_kv.shape
    part = both // 2
    head = sharing * part
    heads = wide // head
    block = min(256, seq_len)
    scale = head ** (-0.5)
    entries = turned.shape[1]
    slots = entries // group
    orders = [order[::-1] for order in bit_orders(group)]
    orders = [orders[at % 2] for at in range(chunks)]
    steps = len(orders[0])

    def kernel(
        gb_ref, wo_any, x_any, wq_any, wkv_any, qr_any, ql_any, kr_any, kl_any, vl_any, lse_any, att_ref,
        cos_ref, sin_ref, gq_ref, gk_ref, mix_any, turned_any, tok_ref, gain_ref, gh_any, hid_ref, n2_ref, rt_any, fm_ref,
        tok_out, wo_out, wq_out, wkv_out, gq_out, gk_out, n1_out, n2_out, rt_out, layer_out,
        wo_ref, x_ref, wq_ref, wkv_ref, ql_ref, kr_ref, kl_ref, vl_ref, lse_ref, turned,
        big, row_terms, log_rows, dq_low, dk, dv, dkv_low, kv_box, raw_buf,
        wo_part, wo_box, w_part, w_box, kv_part, kv_inbox, dx_box, back,
        mix_part, mix_box, summed, dx_sum, vec, vec_plane, vec_half, vec_line, rt_acc, rt_box, rt_half, rt_line, gq_sum, gk_sum,
        loads, raw_load, keep_s, wo_s, w_s, kv_s, sib_s, dx_s, ex_s, mix_s, vp_s, vl_s, rp_s, rl_s, rg_s, gb_s,
    ):
        place, plane = lax.axis_index("dp"), lax.axis_index("expert")
        member = plane % sharing

        def branch(j):
            first = j * cut
            return big.at[first // width, :, pl.ds(first % width, cut)]

        fetches = [
            pltpu.make_async_copy(src, dst, loads.at[at])
            for at, (src, dst) in enumerate(
                (
                    (rt_any, rt_acc),
                    (wo_any, wo_ref),
                    (ql_any, ql_ref),
                    (kl_any, kl_ref),
                    (vl_any, vl_ref),
                    (lse_any, lse_ref),
                    (x_any, x_ref),
                    (kr_any, kr_ref),
                    (wq_any, wq_ref),
                    (wkv_any, wkv_ref),
                    (gh_any, tok_out),
                )
            )
        ]
        for fetch in fetches:
            fetch.start()
        if with_mix:
            turned_load = pltpu.make_async_copy(turned_any, turned, loads.at[len(fetches)])
            turned_load.start()

        def load_raw(h):
            mine = pl.ds(pl.multiple_of(h * head, head), head)
            return pltpu.make_async_copy(qr_any.at[:, mine], raw_buf.at[h % 2], raw_load.at[h % 2])

        load_raw(0).start()

        def slot_rows(p):
            return pl.ds(pl.multiple_of(p * slots, slots), slots)

        def token_rows(j):
            return pl.ds(pl.multiple_of(j * rows, rows), rows)

        exchange = PlaneExchange(
            lambda k, p: mix_any.at[k, slot_rows(p)], lambda k, p: back.at[k, slot_rows(p)], ex_s
        )
        wo_sum = LineReduce(
            lambda k, j: wo_part.at[j, pl.ds(k * (wide // 2), wide // 2)],
            lambda way, k, j: wo_box.at[j + 1 - way, pl.ds(k * (wide // 2), wide // 2)],
            wo_s,
        )
        w_sum = LineReduce(
            lambda k, j: w_part.at[k, j], lambda way, k, j: w_box.at[k, j + 1 - way], w_s
        )
        kv_sum = LineReduce(
            lambda k, j: kv_part.at[j], lambda way, k, j: kv_inbox.at[j + 1 - way], kv_s
        )
        reduce = PlaneReduce(
            lambda h, j: big.at[h, token_rows(j)], lambda h, n: dx_box.at[h, n], dx_s, orders
        )

        mix_sum = LineReduce(
            lambda k, j: mix_part.at[k, token_rows(j)],
            lambda way, k, j: mix_box.at[k, j + 1 - way],
            mix_s,
        )
        share = model // group

        def share_cols(j):
            return pl.ds(pl.multiple_of(j * share, share), share)

        router = PlaneReduce(
            lambda h, j: rt_acc.at[:, share_cols(j)], lambda h, n: rt_box.at[n], rp_s, orders[:1]
        )
        router_back = PlaneGather(
            lambda h: rt_half.at[1],
            lambda h, j: rt_out.at[:, share_cols(j)],
            rg_s,
            bit_orders(group)[:1],
        )

        def router_line(step):
            return remote(
                rt_half.at[0], rt_line.at[step], rl_s.at[0, step], rl_s.at[1, step],
                "dp", (place + step) % data,
            )

        def router_stage(at):
            if at < steps:
                router.advance(0, at)
            elif at == steps:
                router.result(0, rt_half.at[0])
                for step in range(1, data):
                    router_line(step).start()
            elif at == steps + 1:
                total = rt_half[0]
                for step in range(1, data):
                    router_line(step).wait_recv()
                    total = total + rt_line[step]
                rt_half[1] = total
                rt_out[:, share_cols(plane)] = total
                router_back.start()
            else:
                router_back.relay()

        def vec_across(mask):
            return remote(
                vec, vec_plane.at[mask], vp_s.at[0, mask], vp_s.at[1, mask],
                "expert", flipped(plane, mask),
            )

        def vec_along(step):
            return remote(
                vec_half, vec_line.at[step], vl_s.at[0, step], vl_s.at[1, step],
                "dp", (place + step) % data,
            )

        def x_block(j):
            first = j * depth
            inner = first % width
            return x_ref[first // width, :, inner : inner + depth]

        own_rows = token_rows(plane)
        for h in range(pieces):
            branch(h)[own_rows] = gb_ref[h]
        if with_mix:
            mix_part[0] = fm_ref[...]
        greet(far=True)
        if with_mix:
            mix_sum.begin(0)
        gather = PlaneGather(
            lambda h: gb_ref.at[h],
            lambda h, j: big.at[
                (h * cut) // width, token_rows(j), pl.ds((h * cut) % width, cut)
            ],
            gb_s,
            [bit_orders(group)[at % 2] for at in range(pieces)],
        )
        pairs = [range(h, min(h + 2, pieces)) for h in range(0, pieces, 2)]
        gather.start(pairs[0])
        fetches[0].wait()
        att_turned = att_ref[...].T

        def wo_piece(j):
            wo_part[j] = jnp.dot(
                att_turned, branch(j)[...], preferred_element_type=jnp.float32
            ).astype(jnp.bfloat16)
            for k in range(2):
                wo_sum.begin_block(k, j)

        for at, pair in enumerate(pairs):
            moves = [move for move in gather.moves() if move[0] in pair]
            first = [move for move in moves if move[1].bit_count() == 1]
            for move in first:
                gather.move(*move)
            if at + 1 < len(pairs):
                gather.start(pairs[at + 1])
            for move in moves[len(first) :]:
                gather.move(*move)
            for h in pair:
                wo_piece(h)
        router.start(0)
        if with_mix:
            if chunks > 1:
                exchange.start(1)
            mix_sum.near(0)
        fetches[1].wait()

        lane = lax.broadcasted_iota(jnp.int32, (block, head), 1)

        def attended_grad(at, carry):
            here = pl.ds(pl.multiple_of(at * block, block), block)
            value = jnp.zeros((block, wide), jnp.float32)
            for j in range(pieces):
                value += nt_dot(branch(j)[here], wo_ref[j])
            low = value.astype(jnp.bfloat16)
            dq_low[here] = low
            both_rows = low.astype(jnp.float32) * att_ref[here].astype(jnp.float32)
            terms = jnp.zeros((block, head), jnp.float32)
            for h in range(heads):
                term = jnp.sum(both_rows[:, h * head : (h + 1) * head], axis=-1, keepdims=True)
                terms = jnp.where(lane == h, term, terms)
            dk[here] = terms
            return carry

        lax.fori_loop(0, total // block, attended_grad, 0)
        for at in range(2, 7):
            fetches[at].wait()
        row_terms[...] = dk[...].T
        log_rows[...] = lse_ref[...].T * LOG2_E
        dk[...] = jnp.zeros_like(dk)
        dv[...] = jnp.zeros_like(dv)
        above = lax.broadcasted_iota(
            jnp.int32, (block, block), 0
        ) <= lax.broadcasted_iota(jnp.int32, (block, block), 1)

        def turned_dot(left, right):
            return lax.dot_general(
                left, right, (((0,), (0,)), ((), ())), preferred_element_type=jnp.float32
            )

        def unrotate(value, table):
            return value * cos_ref[table] - half_turn(value) * sin_ref[table]

        def norm_back(turned_grad, raw, gain):
            factor = row_scale(raw)
            gain_term = jnp.sum(turned_grad * raw * factor, axis=0, keepdims=True)
            scaled = turned_grad * gain
            inner = jnp.mean(scaled * raw, axis=-1, keepdims=True)
            return factor * scaled - raw * (factor * factor * factor * inner), gain_term

        gq_sum[...] = jnp.zeros_like(gq_sum)
        gk_sum[...] = jnp.zeros_like(gk_sum)

        def own_mix(k):
            return pltpu.make_async_copy(
                mix_any.at[k, slot_rows(plane)], back.at[k, slot_rows(plane)], keep_s.at[k]
            )

        def gather_mix(k):
            own_mix(k).wait()
            exchange.wait(k)
            mix_part[k] = jnp.dot(
                turned[...], back[k], preferred_element_type=jnp.float32
            ).astype(jnp.bfloat16)
            mix_sum.begin(k)

        if with_mix:
            for k in range(1, chunks):
                own_mix(k).start()
            turned_load.wait()
            mix_sum.far(0)

        def head_back(h, carry):
            mine = pl.ds(pl.multiple_of(h * head, head), head)
            load_raw(h).wait()

            @pl.when(h + 1 < heads)
            def _():
                load_raw(h + 1).start()

            for seq in range(total // seq_len):
                base = seq * seq_len
                for at in range(seq_len // block):
                    here = pl.ds(base + at * block, block)
                    query = ql_ref[here, mine]
                    grad = dq_low[here, mine]
                    log_sum = log_rows[pl.ds(h, 1), here]
                    row_term = row_terms[pl.ds(h, 1), here]
                    grad_query = jnp.zeros((block, head), jnp.float32)
                    for other in range(at + 1):
                        behind = pl.ds(base + other * block, block)
                        key = kl_ref[behind]
                        probs = jnp.exp2(nt_dot(key, query) * (scale * LOG2_E) - log_sum)
                        if other == at:
                            probs = jnp.where(above, probs, 0.0)
                        grad_probs = nt_dot(vl_ref[behind], grad)
                        grad_scores = (probs * (grad_probs - row_term)).astype(jnp.bfloat16)
                        dv[behind] += jnp.dot(
                            probs.astype(jnp.bfloat16), grad, preferred_element_type=jnp.float32
                        )
                        dk[behind] += jnp.dot(
                            grad_scores, query, preferred_element_type=jnp.float32
                        )
                        grad_query += turned_dot(grad_scores, key)
                    grad_query = grad_query * scale
                    table = pl.ds(at * block, block)
                    raw_grad, gain_term = norm_back(
                        unrotate(grad_query, table), raw_buf[h % 2, here], gq_ref[...]
                    )
                    gq_sum[...] += gain_term
                    dq_low[here, mine] = raw_grad.astype(jnp.bfloat16)
            low_turned = dq_low[:, mine].T
            for j in range(data):
                w_part[h, j] = jnp.dot(
                    low_turned, x_block(j), preferred_element_type=jnp.float32
                ).astype(jnp.bfloat16)
            w_sum.begin(h)

            if with_mix:

                @pl.when(h + 2 < chunks)
                def _():
                    exchange.start(h + 2)

            if with_mix and heads > 2:

                @pl.when((h >= 2) & (h - 1 < chunks))
                def _():
                    gather_mix(h - 1)

            @pl.when(h == heads - 2)
            def _():
                wo_sum.near(0)

            @pl.when(h == heads - 1)
            def _():
                wo_sum.near(1)
                wo_sum.far(0)

            return carry

        lax.fori_loop(0, heads, head_back, 0)
        if with_mix:
            for k in range(heads + 2, chunks):
                exchange.start(k)
        for at in range(7, len(fetches)):
            fetches[at].wait()
        for at in range(total // block):
            here = pl.ds(at * block, block)
            table = pl.ds((at * block) % seq_len, block)
            raw_grad, gain_term = norm_back(
                unrotate(dk[here] * scale, table), kr_ref[here], gk_ref[...]
            )
            gk_sum[...] += gain_term
            value_grad = dv[here]
            for m in range(sharing):
                cols = slice(m * part, (m + 1) * part)
                dkv_low[m, here] = jnp.concatenate(
                    [raw_grad[:, cols], value_grad[:, cols]], axis=1
                ).astype(jnp.bfloat16)

        def swap(mask):
            other = flipped(plane, mask)
            return remote(
                dkv_low.at[other % sharing],
                kv_box.at[member],
                sib_s.at[0, mask],
                sib_s.at[1, mask],
                "expert",
                other,
            )

        for mask in range(1, sharing):
            swap(mask).start()
        gather.finish()
        for j in range(data):
            first = j * depth
            c, inner = first // width, first % width

            def input_grad(at, carry):
                here = pl.ds(pl.multiple_of(at * block, block), block)
                value = nt_dot(dq_low[here], wq_ref[pl.ds(first, depth)])
                for m in range(sharing):
                    value += jnp.dot(
                        dkv_low[m, here], wkv_ref[m, j], preferred_element_type=jnp.float32
                    )
                big[c, here, inner : inner + depth] = value.astype(jnp.bfloat16)
                return carry

            lax.fori_loop(0, total // block, input_grad, 0)
            if inner + depth == width:
                reduce.start(c)
        kv_box[member] = dkv_low[member]
        for mask in range(1, sharing):
            other = kv_box.at[flipped(plane, mask) % sharing]
            remote(
                other, other, sib_s.at[0, mask], sib_s.at[1, mask], "expert", flipped(plane, mask)
            ).wait_recv()
        kv_turned = [kv_box[m].T for m in range(sharing)]
        for j in range(data):
            block_x = x_block(j)
            value = sum(
                jnp.dot(item, block_x, preferred_element_type=jnp.float32) for item in kv_turned
            )
            kv_part[j] = value.astype(jnp.bfloat16)
        kv_sum.begin(0)
        mixed_at = min(chunks, max(1, heads - 1)) if with_mix else chunks
        for k in range(mixed_at, chunks - 1):
            gather_mix(k)
        for c in range(chunks):
            reduce.advance(c, 0)
        if with_mix and mixed_at < chunks:
            gather_mix(chunks - 1)
        wo_sum.far(1)
        w_sum.near(0)
        for at in range(1, steps):
            for c in range(chunks):
                reduce.advance(c, at)
        router_stage(0)
        for c in range(chunks):
            reduce.result(c, dx_sum.at[:, pl.ds(c * width, width)])
        state = tok_ref[...].astype(jnp.float32)
        grad_normed = dx_sum[...]
        raw_grad, gain_term = norm_back(grad_normed, state, gain_ref[...])
        tok_out[...] += raw_grad
        vec[...] = jnp.zeros_like(vec)
        for c in range(chunks):
            cols = slice(c * width, (c + 1) * width)
            vec[c : c + 1, 0:width] = gain_term[:, cols]
            vec[chunks + c : chunks + c + 1, 0:width] = n2_ref[:, cols]
        vec[0:1, width : width + head] = gq_sum[...]
        vec[1:2, width : width + head] = gk_sum[...]
        for mask in range(1, group):
            vec_across(mask).start()
        sweeps = [(w_sum, h) for h in range(heads)] + [(kv_sum, 0)]
        if with_mix:
            for k in range(1, chunks):
                place_at = heads - mixed_at + 2 * k
                sweeps.insert(place_at if k < mixed_at else len(sweeps), (mix_sum, k))

        def settle(line, k):
            if line is w_sum:
                w_sum.result(k, summed)
                wq_out[:, k * head : (k + 1) * head] = summed[...].T
            elif line is kv_sum:
                kv_sum.result(0, wkv_out)
            else:
                part_cols = pl.ds(k * width, width)
                mix_sum.result(k, dx_sum.at[:, part_cols])
                layer_out[:, part_cols] = (hid_ref[:, part_cols] + dx_sum[:, part_cols]).astype(
                    jnp.bfloat16
                )

        for k in range(2):
            wo_sum.result(k, wo_out.at[pl.ds(k * (wide // 2), wide // 2)])
        if with_mix:
            settle(mix_sum, 0)
        for at, (line, k) in enumerate(sweeps):
            if at == 2:
                all_sum = vec[...]
                for mask in range(1, group):
                    vec_across(mask).wait_recv()
                    all_sum = all_sum + vec_plane[mask]
                vec_half[...] = all_sum
                for step in range(1, data):
                    vec_along(step).start()
            if at:
                line.near(k)
                sweeps[at - 1][0].far(sweeps[at - 1][1])
                if at < steps + 3:
                    router_stage(at)
                settle(*sweeps[at - 1])
        sweeps[-1][0].far(sweeps[-1][1])
        settle(*sweeps[-1])
        for stage in range(max(1, min(len(sweeps), steps + 3)), steps + 3):
            router_stage(stage)
        all_sum = vec_half[...]
        for step in range(1, data):
            vec_along(step).wait_recv()
            all_sum = all_sum + vec_line[step]
        for c in range(chunks):
            for q in range(width // 128):
                at, cols = c * (width // 128) + q, slice(q * 128, (q + 1) * 128)
                n1_out[at : at + 1] = all_sum[c : c + 1, cols]
                n2_out[at : at + 1] = all_sum[chunks + c : chunks + c + 1, cols]
        gq_out[...] = all_sum[0:1, width : width + head]
        gk_out[...] = all_sum[1:2, width : width + head]
        for mask in range(1, group):
            vec_across(mask).wait_send()
        for step in range(1, data):
            vec_along(step).wait_send()
            router_line(step).wait_send()
        router.finish(0)
        router_back.finish()
        for k in range(2):
            wo_sum.finish(k)
        for h in range(heads):
            w_sum.finish(h)
        kv_sum.finish(0)
        for mask in range(1, sharing):
            swap(mask).wait_send()
        for c in range(chunks):
            reduce.finish(c)
        if with_mix:
            for k in range(chunks):
                mix_sum.finish(k)
                if k:
                    exchange.finish(k)

    bf, fl = jnp.bfloat16, jnp.float32
    whole = pl.BlockSpec(memory_space=pltpu.VMEM)
    anywhere = pl.BlockSpec(memory_space=pl.ANY)
    mix_entries = entries if with_mix else 16
    mix_rows = rows if with_mix else 16
    mix_all = data * rows if with_mix else 16
    experts = router_sum.shape[0]
    share = model // group
    lines = whole_up(2 * chunks, 8)
    outs = [
        jax.ShapeDtypeStruct((rows, model), fl),
        jax.ShapeDtypeStruct((wide, cut), fl),
        jax.ShapeDtypeStruct((depth, wide), fl),
        jax.ShapeDtypeStruct((both, depth), fl),
        jax.ShapeDtypeStruct((1, head), fl),
        jax.ShapeDtypeStruct((1, head), fl),
        jax.ShapeDtypeStruct((model // 128, 128), fl),
        jax.ShapeDtypeStruct((model // 128, 128), fl),
        jax.ShapeDtypeStruct((experts, model), fl),
        jax.ShapeDtypeStruct((mix_rows, model), bf),
    ]
    return pl.pallas_call(
        kernel,
        out_shape=outs,
        in_specs=[whole]
        + [anywhere] * 10
        + [whole] * 5
        + [anywhere] * 2
        + [whole] * 2
        + [anywhere, whole if with_mix else anywhere, whole, anywhere]
        + [whole if with_mix else anywhere],
        out_specs=[whole] * len(outs),
        scratch_shapes=[
            vmem(out_blocks.shape, bf),
            vmem(x.shape, bf),
            vmem(w_q.shape, bf),
            vmem(w_kv.shape, bf),
            vmem(q_low.shape, bf),
            vmem(k_raw.shape, fl),
            vmem(k_low.shape, bf),
            vmem(v_low.shape, bf),
            vmem(lse.shape, fl),
            vmem(turned.shape if with_mix else (16, 128), bf),
            vmem((chunks, total, width), bf),
            vmem((head, total), fl),
            vmem((head, total), fl),
            vmem((total, wide), bf),
            vmem((total, head), fl),
            vmem((total, head), fl),
            vmem((sharing, total, both), bf),
            vmem((sharing, total, both), bf),
            vmem((2, total, head), fl),
            vmem((data, wide, cut), bf),
            vmem((data + 1, wide, cut), bf),
            vmem((heads, data, head, depth), bf),
            vmem((heads, data + 1, head, depth), bf),
            vmem((data, both, depth), bf),
            vmem((data + 1, both, depth), bf),
            vmem((chunks, group - 1, rows, width), bf),
            vmem((chunks, mix_entries, width), bf),
            vmem((chunks, mix_all, width), bf),
            vmem((chunks, data + 1, mix_rows, width), bf),
            vmem((head, depth), fl),
            vmem((rows, model), fl),
            vmem((lines, width + head), fl),
            vmem((group, lines, width + head), fl),
            vmem((lines, width + head), fl),
            vmem((data, lines, width + head), fl),
            vmem((experts, model), fl),
            vmem((group - 1, experts, share), fl),
            vmem((2, experts, share), fl),
            vmem((data, experts, share), fl),
            vmem((1, head), fl),
            vmem((1, head), fl),
            dma(12),
            dma(2),
            dma(chunks),
            dma(4, 2, data),
            dma(4, heads, data),
            dma(4, 1, data),
            dma(2, sharing),
            dma(2, chunks, group - 1),
            dma(2, chunks, group),
            dma(4, chunks, data),
            dma(2, group),
            dma(2, data),
            dma(2, 1, group - 1),
            dma(2, data),
            dma(2, 1, group),
            dma(2, pieces, group),
        ],
        compiler_params=pltpu.CompilerParams(
            collective_id=7, has_side_effects=True, vmem_limit_bytes=VMEM_LIMIT
        ),
    )(
        grad_branch, out_blocks, x, w_q, w_kv, q_raw, q_low, k_raw, k_low, v_low, lse, att,
        cos, sin, gain_q, gain_k, mixed, turned, tokens, gain, grad_hidden, hidden, norm2_sum, router_sum, first_mix,
    )


def rope_arrays(seq_len, head_dim):
    half = head_dim // 2
    frequency = ROPE_THETA ** (-(np.arange(half) * 2.0) / head_dim)
    angles = np.arange(seq_len)[:, None] * frequency[None, :]
    cos = np.concatenate([np.cos(angles), np.cos(angles)], axis=1).astype(np.float32)
    sin = np.concatenate([-np.sin(angles), np.sin(angles)], axis=1).astype(np.float32)
    return cos, sin


def row_scale(value):
    return lax.rsqrt(jnp.mean(value * value, axis=-1, keepdims=True) + NORM_EPS)


def half_turn(value):
    return pltpu.roll(value, value.shape[-1] // 2, value.ndim - 1)


def nt_dot(left, right):
    return lax.dot_general(
        left, right, (((1,), (1,)), ((), ())), preferred_element_type=jnp.float32
    )


def causal(start, rows, keys):
    at_row = lax.broadcasted_iota(jnp.int32, (rows, keys), 0) + start
    return lax.broadcasted_iota(jnp.int32, (rows, keys), 1) <= at_row


class Always:
    def __init__(self, order):
        self.order = order

    def __getitem__(self, at):
        return self.order


def front(
    tokens, gain, w_q, w_k, w_v, w_out, out_grad, slot_rows, cos, sin, gain_q, gain_k,
    gain2, router, hot, capacity, slots, seq_len,
):
    data, group = lax.axis_size("dp"), lax.axis_size("expert")
    rows, model = tokens.shape
    width = min(512, model)
    chunks = model // width
    depth, wide = w_q.shape
    cut = w_out.shape[1]
    part = w_k.shape[0]
    both = 2 * part
    head = gain_q.shape[1]
    sharing = head // part
    heads = wide // head
    total = group * rows
    block = min(256, seq_len)
    scale = head ** (-0.5)
    experts = router.shape[0]
    extra = whole_up(2 * experts, 128)
    entries = group * slots
    x_orders = bit_orders(group)
    x_orders = [x_orders[at % 2] for at in range(chunks)]
    b_orders = [Always(order[::-1]) for order in bit_orders(group)]
    steps = len(b_orders[0][0])
    halves = 2
    deep = depth // halves
    first_grad = 2 + halves
    first_out = first_grad + chunks - 1
    first_last = first_out + 1
    last = [item for item in halved(chunks, width, chunks - 1) if item[0] == chunks - 1]
    items = first_last + len(last)

    def kernel(
        tok_ref, gain_ref, wq_ref, wk_ref, wv_ref, wo_ref, og_ref, s_ref, cos_ref, sin_ref, gq_ref, gk_ref,
        gain2_ref, r_ref, hot_ref,
        x_any, wq_any, wkv_any, wo_any, g_any, sel_any, qr_any, ql_any, kr_any, kl_any, vl_any, lse_any,
        att_any, hidden, second, pair, probs,
        x_own, g_own, kv_own, x_all, wq_all, wkv_all, wo_all, g_all, s_all, picked, g_here, select,
        q_raw, q_low, k_raw, k_low, v_low, lse, att, acc, inbox,
        ps, ls, es, ks, bs, outs,
    ):
        place, plane = lax.axis_index("dp"), lax.axis_index("expert")
        member = plane % sharing
        state = tok_ref[...].astype(jnp.float32)
        normed = (state * row_scale(state) * gain_ref[...]).astype(jnp.bfloat16)
        mine = pl.ds(pl.multiple_of(place * rows, rows), rows)
        own_rows = pl.ds(pl.multiple_of(plane * rows, rows), rows)
        for c in range(chunks):
            x_own[c] = normed[:, c * width : (c + 1) * width]
            x_all[c, own_rows] = x_own[c]
            g_own[c] = og_ref[:, c * width : (c + 1) * width]
            g_all[c, mine] = g_own[c]
        kv_own[0:part] = wk_ref[...]
        kv_own[part:both] = wv_ref[...]
        wq_all[place] = wq_ref[...]
        wkv_all[member, place] = kv_own[...]
        wo_all[place] = wo_ref[...]
        s_all[place] = s_ref[...]
        greet()

        def token_rows(j):
            return pl.ds(pl.multiple_of(j * rows, rows), rows)

        def slot_rows_of(p):
            return pl.ds(pl.multiple_of(p * slots, slots), slots)

        gather = PlaneGather(
            lambda h: x_own.at[h], lambda h, j: x_all.at[h, token_rows(j)], ps, x_orders
        )

        def is_grad(k):
            return not isinstance(k, int) or first_grad <= k < first_out

        def own(k):
            if is_grad(k):
                return g_own.at[k - first_grad]
            if k == 0:
                return s_ref
            if k == 1:
                return kv_own
            if k < first_grad:
                return wq_ref.at[pl.ds((k - 2) * deep, deep)]
            if k >= first_last:
                return part_of(g_own, last[k - first_last], pl.ds(0, rows), width)
            return wo_ref

        def slot(k, j):
            if is_grad(k):
                return g_all.at[k - first_grad, token_rows(j)]
            if k == 0:
                return s_all.at[j]
            if k == 1:
                return wkv_all.at[member, j]
            if k < first_grad:
                return wq_all.at[j, pl.ds((k - 2) * deep, deep)]
            if k >= first_last:
                return part_of(g_all, last[k - first_last], token_rows(j), width)
            return wo_all.at[j]

        line = LineGather(own, slot, ls)
        def exchanged(ref):
            return lambda k, p: (
                part_of(ref, last[k - chunks + 1], slot_rows_of(p), width)
                if isinstance(k, int) and k >= chunks - 1
                else ref.at[k, slot_rows_of(p)]
            )

        exchange = PlaneExchange(exchanged(picked), exchanged(g_here), es)
        turns_of_grads = chunks - 1 + len(last)
        reduces = [
            PlaneReduce(lambda h, j: acc.at[h, j], lambda h, n: inbox.at[h, n], bs, order)
            for order in b_orders
        ]
        keeps = {}

        def keep(name, src, dst):
            keeps[name] = pltpu.make_async_copy(src, dst, outs.at[len(keeps)])
            keeps[name].start()

        def share(mask):
            return remote(
                wkv_all.at[member], wkv_all.at[member], ks.at[0, mask], ks.at[1, mask],
                "expert", flipped(plane, mask),
            )

        gather.start()
        for k in range(first_grad):
            line.start(k)
        moves = gather.moves()
        for s in range(1, data):
            line.step(0, s)
        wanted = lax.broadcasted_iota(jnp.int32, (slots, rows), 0).astype(jnp.float32)
        for j in range(data):
            for peer in range(group):
                row = s_all[j, pl.ds(pl.multiple_of(place * group, 8), group)][peer : peer + 1]
                row = jnp.where(row >= 0, row + j * capacity, -1.0)
                select[pl.ds(peer * slots, slots), pl.ds(j * rows, rows)] = jnp.where(
                    wanted == row, 1.0, 0.0
                ).astype(jnp.bfloat16)
        for k in range(first_grad, min(first_grad + 2, first_out)):
            line.start(k)
        taken = 0
        turns = [(k, s) for k in range(1, first_grad) for s in range(1, data)]
        for at, (k, s) in enumerate(turns):
            until = len(moves) * (at + 1) // len(turns)
            for move in moves[taken:until]:
                gather.move(*move)
            taken = until
            line.step(k, s)
            if k == 1 and s == data - 1:
                for mask in range(1, sharing):
                    share(mask).start()
        for k in range(first_grad + 2, first_out):
            line.start(k)
        for mask in range(1, sharing):
            other = wkv_all.at[flipped(plane, mask) % sharing]
            remote(
                other, other, ks.at[0, mask], ks.at[1, mask], "expert", flipped(plane, mask)
            ).wait_recv()
        keep("select", select, sel_any)
        keep("x", x_all, x_any)
        keep("wq", wq_all, wq_any)
        keep("wkv", wkv_all, wkv_any)

        def x_block(rows_here, j):
            first = j * depth
            inner = first % width
            return x_all[first // width, rows_here, inner : inner + depth]

        def project(at, carry):
            here = pl.ds(pl.multiple_of(at * block, block), block)
            table = pl.ds(pl.multiple_of((at * block) % seq_len, block), block)
            cos_here, sin_here = cos_ref[table], sin_ref[table]
            blocks = [x_block(here, j) for j in range(data)]
            raw = sum(
                jnp.dot(blocks[j], wq_all[j], preferred_element_type=jnp.float32)
                for j in range(data)
            )
            q_raw[here] = raw
            for h in range(heads):
                one = raw[:, h * head : (h + 1) * head]
                one = one * row_scale(one) * gq_ref[...]
                turned = one * cos_here + half_turn(one) * sin_here
                q_low[here, h * head : (h + 1) * head] = turned.astype(jnp.bfloat16)
            kv = [sum(nt_dot(blocks[j], wkv_all[m, j]) for j in range(data)) for m in range(sharing)]
            raw = jnp.concatenate([item[:, :part] for item in kv], axis=1)
            k_raw[here] = raw
            one = raw * row_scale(raw) * gk_ref[...]
            k_low[here] = (one * cos_here + half_turn(one) * sin_here).astype(jnp.bfloat16)
            v_low[here] = jnp.concatenate([item[:, part:] for item in kv], axis=1).astype(
                jnp.bfloat16
            )
            return carry

        lax.fori_loop(0, total // block, project, 0)
        keep("q_raw", q_raw, qr_any)
        keep("q_low", q_low, ql_any)
        keep("k_raw", k_raw, kr_any)
        keep("k_low", k_low, kl_any)
        keep("v_low", v_low, vl_any)
        lane = lax.broadcasted_iota(jnp.int32, (block, head), 1)
        below = causal(0, block, block)
        lse[...] = jnp.zeros_like(lse)

        def send_grads(c):
            picked[c] = jnp.dot(
                select[...], g_all[c], preferred_element_type=jnp.float32
            ).astype(jnp.bfloat16)
            exchange.start(c)
            exchange.keep(c)

        def attend(h, carry):
            cols = pl.ds(pl.multiple_of(h * head, head), head)
            count = 0
            for seq in range(total // seq_len):
                base = seq * seq_len
                for at in range(seq_len // block):
                    here = pl.ds(base + at * block, block)
                    query = q_low[here, cols]
                    tiles = []
                    if at:
                        tiles.append(pl.ds(base, at * block))
                    tiles.append(here)
                    scores = [nt_dot(query, k_low[tile]) for tile in tiles]
                    scores[-1] = jnp.where(below, scores[-1], -jnp.inf)
                    top = jnp.max(scores[-1], axis=-1, keepdims=True)
                    if at:
                        top = jnp.maximum(top, jnp.max(scores[0], axis=-1, keepdims=True))
                    raised = [jnp.exp2((score - top) * (scale * LOG2_E)) for score in scores]
                    norm = sum(jnp.sum(item, axis=-1, keepdims=True) for item in raised)
                    inverse = 1.0 / norm
                    att[here, cols] = sum(
                        jnp.dot(
                            (item * inverse).astype(jnp.bfloat16),
                            v_low[tile],
                            preferred_element_type=jnp.float32,
                        )
                        for item, tile in zip(raised, tiles)
                    ).astype(jnp.bfloat16)
                    lse[here] = jnp.where(lane == h, top * scale + jnp.log(norm), lse[here])
                    count += 1
                    if count < data:

                        @pl.when(h < chunks - 1)
                        def _():
                            line.step(first_grad + h, count)

            @pl.when(h < chunks - 1)
            def _():
                for s in range(count + 1, data):
                    line.step(first_grad + h, s)
                send_grads(h)

            @pl.when(h == 0)
            def _():
                line.start(first_out)

            return carry

        lax.fori_loop(0, heads, attend, 0)
        keep("lse", lse, lse_any)
        keep("att", att, att_any)
        for c in range(heads, chunks - 1):
            for s in range(1, data):
                line.step(first_grad + c, s)
            send_grads(c)
        for k in range(first_last, items):
            line.start(k)

        def send_last(n):
            c, at, wide = last[n]
            picked[c, :, at : at + wide] = jnp.dot(
                select[...], g_all[c, :, at : at + wide], preferred_element_type=jnp.float32
            ).astype(jnp.bfloat16)
            exchange.start(chunks - 1 + n)
            exchange.keep(chunks - 1 + n)

        tail = []
        for n in range(len(last)):
            tail += [(n, s) for s in range(1, data)]

        def arrivals(s):
            if s == 0:
                return [(place, place >= 0, reduces[0])]
            return [
                (place - s, place >= s, reduces[(s + 1) % 2]),
                (place + s, place + s < data, reduces[s % 2]),
            ]

        def each(s, act):
            for j, present, reduce in arrivals(s):

                @pl.when(present)
                def _():
                    act(j, reduce)

        def project_out(j, reduce):
            acc[j] = (
                jnp.dot(att[...], wo_all[j], preferred_element_type=jnp.float32)
                .astype(jnp.bfloat16)
                .reshape(group, rows, cut)
            )
            reduce.start(j)

        for turn in range(data + steps):
            if turn < data:
                if turn:
                    line.step(first_out, turn)
                each(turn, project_out)
            for at in range(steps):
                if 0 <= turn - 1 - at < data:
                    each(turn - 1 - at, lambda j, reduce: reduce.advance(j, at))
            if turn >= data - 1:
                count = -(-len(tail) // (data + steps - turn))
                for n, s in tail[:count]:
                    line.step(first_last + n, s)
                    if s == data - 1:
                        send_last(n)
                tail = tail[count:]
        keep("wo", wo_all, wo_any)

        def branch_piece(j, reduce):
            reduce.result(j, hidden.at[:, pl.ds(pl.multiple_of(j * cut, cut), cut)])

        for s in range(data):
            each(s, branch_piece)
        summed = hidden[...] + tok_ref[...].astype(jnp.float32)
        hidden[...] = summed
        low = (summed * row_scale(summed) * gain2_ref[...]).astype(jnp.bfloat16)
        for c in range(chunks):
            second[c] = low[:, c * width : (c + 1) * width]
        logits = nt_dot(low, r_ref[...])
        masked = jnp.where(hot_ref[...] > 0, logits, -jnp.inf)
        raised = jnp.exp(masked - jnp.max(masked, axis=-1, keepdims=True))
        gate = raised / jnp.sum(raised, axis=-1, keepdims=True)
        probs[...] = gate
        top = gate.astype(jnp.bfloat16).astype(jnp.float32)
        parts = [top, gate - top]
        if extra > 2 * experts:
            parts.append(jnp.zeros((rows, extra - 2 * experts), jnp.float32))
        pair[...] = jnp.concatenate(parts, axis=1).astype(jnp.bfloat16)
        for k in range(turns_of_grads):
            exchange.wait(k)
        keep("g", g_here, g_any)
        for k in range(items):
            line.finish(k)
        gather.finish()
        for mask in range(1, sharing):
            share(mask).wait_send()
        for k in range(turns_of_grads):
            exchange.finish(k)
        for s in range(data):
            each(s, lambda j, reduce: reduce.finish(j))
        for copy in keeps.values():
            copy.wait()

    bf, fl = jnp.bfloat16, jnp.float32
    whole = pl.BlockSpec(memory_space=pltpu.VMEM)
    anywhere = pl.BlockSpec(memory_space=pl.ANY)

    def shape(*dims, dtype=bf):
        return jax.ShapeDtypeStruct(dims, dtype)

    kept = [
        shape(chunks, total, width),
        shape(data, depth, wide),
        shape(sharing, data, both, depth),
        shape(data, wide, cut),
        shape(chunks, entries, width),
        shape(entries, data * rows),
        shape(total, wide, dtype=fl),
        shape(total, wide),
        shape(total, head, dtype=fl),
        shape(total, head),
        shape(total, head),
        shape(total, head, dtype=fl),
        shape(total, wide),
    ]
    small = [
        shape(rows, model, dtype=fl),
        shape(chunks, rows, width),
        shape(rows, extra),
        shape(rows, experts, dtype=fl),
    ]
    return pl.pallas_call(
        kernel,
        out_shape=kept + small,
        in_specs=[whole] * 15,
        out_specs=[anywhere] * len(kept) + [whole] * len(small),
        scratch_shapes=[
            vmem((chunks, rows, width), bf),
            vmem((chunks, rows, width), bf),
            vmem((both, depth), bf),
            vmem((chunks, total, width), bf),
            vmem((data, depth, wide), bf),
            vmem((sharing, data, both, depth), bf),
            vmem((data, wide, cut), bf),
            vmem((chunks, data * rows, width), bf),
            vmem((data, experts, rows), fl),
            vmem((chunks, entries, width), bf),
            vmem((chunks, entries, width), bf),
            vmem((entries, data * rows), bf),
            vmem((total, wide), fl),
            vmem((total, wide), bf),
            vmem((total, head), fl),
            vmem((total, head), bf),
            vmem((total, head), bf),
            vmem((total, head), fl),
            vmem((total, wide), bf),
            vmem((data, group, rows, cut), bf),
            vmem((data, group - 1, rows, cut), bf),
            dma(2, chunks, group),
            dma(4, items, data - 1),
            dma(2, chunks - 1 + len(last), group),
            dma(2, sharing),
            dma(2, data, group - 1),
            dma(len(kept)),
        ],
        compiler_params=pltpu.CompilerParams(
            collective_id=1, has_side_effects=True, vmem_limit_bytes=VMEM_LIMIT
        ),
    )(
        tokens, gain, w_q, w_k, w_v, w_out, out_grad, slot_rows, cos, sin, gain_q, gain_k,
        gain2, router, hot,
    )


def local(
    tokens,
    norm1_gain,
    w_query,
    key_weight,
    value_weight,
    w_out,
    query_gain,
    key_gain,
    norm2_gain,
    w_router,
    w_gate,
    w_up,
    w_down,
    routes,
    out_grad,
):
    data_count = lax.axis_size("dp")
    group_count = lax.axis_size("expert")
    group_index = lax.axis_index("expert")
    local_rows = tokens.shape[0]
    model_width = tokens.shape[1]
    head_dim = query_gain.shape[0]
    heads_here = w_query.shape[1] // head_dim
    top_count = routes.shape[1]
    expert_total = data_count * group_count
    capacity = max(2, (local_rows * top_count * 9 + 8 * expert_total - 1) // (8 * expert_total))
    data_index = lax.axis_index("dp")
    own_expert = data_index * group_count + group_index
    expert_ids = jnp.arange(expert_total)
    hot = jnp.any(routes[:, :, None] == expert_ids[None, None, :], axis=1)
    earlier = (jnp.arange(local_rows)[:, None] > jnp.arange(local_rows)[None, :]).astype(jnp.bfloat16)
    rank = jnp.dot(earlier, hot.astype(jnp.bfloat16), preferred_element_type=jnp.float32)
    slot_rows = jnp.where(hot, rank, -1.0).T
    slots = whole_up(data_count * capacity, 16)
    width_k = key_weight.shape[1]
    all_rows = group_count * local_rows
    seq_len = min(SEQ_LEN, all_rows)
    router = w_router.T
    cos_rows, sine_rows = [jnp.asarray(table) for table in rope_arrays(seq_len, head_dim)]
    (
        gathered, q_blocks, kv_blocks, out_blocks, grads_here, select, query_raw, queries, key_raw,
        keys_low, values_low, log_sum, attended, hidden, second, pair, gate_probs,
    ) = front(
        tokens, norm1_gain[None], w_query, key_weight.T, value_weight.T, w_out, out_grad, slot_rows,
        cos_rows, sine_rows, query_gain[None], key_gain[None], norm2_gain[None], router,
        hot.astype(jnp.float32), capacity, slots, seq_len,
    )
    q_cols = q_blocks.reshape(model_width, -1)
    with_mix = all_rows <= group_count * slots
    (
        grad_h, grad_arrived, act, mixed, grad_hidden, grad_branch, grad_norm2, grad_router,
        turned, first_mix,
    ) = expert_layer(
        second, pair, gate_probs, hidden, out_grad, norm2_gain[None], router, select, grads_here,
        w_gate[0], w_up[0], w_down[0], out_blocks.shape[2], with_mix,
    )
    (
        grad_tokens, grad_wo, grad_wq, grad_wkv, grad_query_gain, grad_key_gain, grad_norm1,
        grad_norm2, grad_router, output,
    ) = attention_backward(
        grad_branch, out_blocks, gathered, q_cols, kv_blocks, query_raw, queries, key_raw, keys_low,
        values_low, log_sum, attended, cos_rows, sine_rows, query_gain[None], key_gain[None],
        mixed, turned, tokens, norm1_gain[None], grad_hidden, hidden, grad_norm2, grad_router, first_mix,
        seq_len, with_mix,
    )
    if not with_mix:
        output = (hidden + combine(mixed, select, slots, 5)).astype(jnp.bfloat16)
    (
        grad_gate_w, grad_up_w, grad_down, output, grad_tokens, grad_wq, grad_wo, grad_router,
        grad_wk, grad_wv, grad_norm1, grad_norm2, grad_query_gain, grad_key_gain,
    ) = expert_weight_grads(
        grad_h, grad_arrived, act, [output, grad_tokens, grad_wq, grad_wo, grad_router], grad_wkv,
        [grad_norm1, grad_norm2, grad_query_gain, grad_key_gain],
    )
    return (
        output,
        grad_tokens,
        grad_norm1.reshape(-1),
        grad_wq,
        grad_wk.T,
        grad_wv.T,
        grad_wo,
        grad_query_gain.reshape(-1),
        grad_key_gain.reshape(-1),
        grad_norm2.reshape(-1),
        grad_router.T,
        grad_gate_w,
        grad_up_w,
        grad_down,
    )


def solution(mesh):
    placed = (
        P(("dp", "expert"), None),
        P(),
        P("dp", "expert"),
        P("dp", "expert"),
        P("dp", "expert"),
        P("expert", "dp"),
        P(),
        P(),
        P(),
        P(),
        P(("dp", "expert"), None, None),
        P(("dp", "expert"), None, None),
        P(("dp", "expert"), None, None),
        P(("dp", "expert"), None),
        P(("dp", "expert"), None),
    )
    return jax.shard_map(
        local,
        mesh=mesh,
        in_specs=placed,
        out_specs=(
            P(("dp", "expert"), None),
            P(("dp", "expert"), None),
            P(),
            P("dp", "expert"),
            P("dp", "expert"),
            P("dp", "expert"),
            P("expert", "dp"),
            P(),
            P(),
            P(),
            P(),
            P(("dp", "expert"), None, None),
            P(("dp", "expert"), None, None),
            P(("dp", "expert"), None, None),
        ),
        check_vma=False,
    )
```

```python
import jax
import jax.numpy as jnp
import numpy as np
from jax import lax
from jax.experimental import pallas as pl
from jax.experimental.pallas import tpu as pltpu
from jax.sharding import PartitionSpec as P

SEQ_LEN = 1024


NORM_EPS = 1e-06
ROPE_THETA = 1000000.0
LOG2_E = 1.4426950408889634


def whole_up(value, unit):
    return -(-value // unit) * unit


def whole_up(value, unit):
    return -(-value // unit) * unit


VMEM_LIMIT = 61 * 1024 * 1024


def flipped(index, mask):
    moved = index
    bit = 1
    while bit <= mask:
        if mask & bit:
            moved = moved + bit * (1 - 2 * ((index // bit) % 2))
        bit *= 2
    return moved


def remote(src, dst, send_sem, recv_sem, axis, target):
    return pltpu.make_async_remote_copy(
        src_ref=src,
        dst_ref=dst,
        send_sem=send_sem,
        recv_sem=recv_sem,
        device_id={axis: target},
        device_id_type=pl.DeviceIdType.MESH,
    )


def greet(line=True, plane=True, far=False):
    barrier = pltpu.get_barrier_semaphore()
    count = 0
    if line:
        size, me = lax.axis_size("dp"), lax.axis_index("dp")
        for step in range(1, size) if far else (1, size - 1):
            pl.semaphore_signal(
                barrier,
                inc=1,
                device_id={"dp": (me + step) % size},
                device_id_type=pl.DeviceIdType.MESH,
            )
            count += 1
    if plane:
        size, me = lax.axis_size("expert"), lax.axis_index("expert")
        for mask in range(1, size):
            pl.semaphore_signal(
                barrier,
                inc=1,
                device_id={"expert": flipped(me, mask)},
                device_id_type=pl.DeviceIdType.MESH,
            )
            count += 1
    pl.semaphore_wait(barrier, count)


class LineGather:
    def __init__(self, own, slot, sems):
        self.size, self.me = lax.axis_size("dp"), lax.axis_index("dp")
        self.own, self.slot, self.sems = own, slot, sems

    def copy(self, way, k, s, src, block):
        target = self.me + 1 if way == 0 else self.me - 1
        dst = self.slot(k, block)
        return remote(src, dst, self.sems.at[way, k, s], self.sems.at[2 + way, k, s], "dp", target)

    def can_send(self, way, s):
        if way == 0:
            return (self.me < self.size - 1) & (self.me - s >= 0)
        return (self.me > 0) & (self.me + s < self.size)

    def start(self, k):
        for way in range(2):

            @pl.when(self.can_send(way, 0))
            def _():
                self.copy(way, k, 0, self.own(k), self.me).start()

    def step(self, k, s):
        for way in range(2):
            block = self.me - s if way == 0 else self.me + s
            present = block >= 0 if way == 0 else block < self.size

            @pl.when(present)
            def _():
                self.copy(way, k, s - 1, self.slot(k, block), block).wait_recv()

            if s < self.size - 1:

                @pl.when(self.can_send(way, s))
                def _():
                    self.copy(way, k, s, self.slot(k, block), block).start()

    def finish(self, k):
        for s in range(self.size - 1):
            for way in range(2):

                @pl.when(self.can_send(way, s))
                def _():
                    self.copy(way, k, s, self.own(k), self.me).wait_send()

    def run(self, count, window, done):
        for k in range(min(window, count)):
            self.start(k)
        for k in range(count):
            for s in range(1, self.size):
                self.step(k, s)
            if k + window < count:
                self.start(k + window)
            done(k)
        for k in range(count):
            self.finish(k)


class LineReduce:
    def __init__(self, part, inbox, sems):
        self.size, self.me = lax.axis_size("dp"), lax.axis_index("dp")
        self.part, self.inbox, self.sems = part, inbox, sems

    def copy(self, way, k, j):
        target = self.me + 1 if way == 0 else self.me - 1
        return remote(
            self.part(k, j),
            self.inbox(way, k, j),
            self.sems.at[way, k, j],
            self.sems.at[2 + way, k, j],
            "dp",
            target,
        )

    def begin(self, k):
        last = self.size - 1
        for turn in range(last):
            for way, j, end in ((0, last - turn, 0), (1, turn, last)):

                @pl.when(self.me == end)
                def _():
                    self.copy(way, k, j).start()

    def begin_block(self, k, j):
        for way, end in ((0, 0), (1, self.size - 1)):
            if j != end:

                @pl.when(self.me == end)
                def _():
                    self.copy(way, k, j).start()

    def sweep(self, k, way):
        last = self.size - 1
        for turn in range(last):
            j = last - turn if way == 0 else turn
            inner = (self.me > 0) if way == 0 else (self.me < last)
            passing = (j > self.me) if way == 0 else (j < self.me)

            @pl.when(inner & (passing | (self.me == j)))
            def _():
                self.copy(way, k, j).wait_recv()

            @pl.when(inner & passing)
            def _():
                total = self.part(k, j)[...].astype(jnp.float32) + self.inbox(way, k, j)[
                    ...
                ].astype(jnp.float32)
                self.part(k, j)[...] = total.astype(self.part(k, j).dtype)
                self.copy(way, k, j).start()

    def near(self, k):
        @pl.when(self.me < self.size // 2)
        def _():
            self.sweep(k, 0)

        @pl.when(self.me >= self.size // 2)
        def _():
            self.sweep(k, 1)

    def far(self, k):
        @pl.when(self.me < self.size // 2)
        def _():
            self.sweep(k, 1)

        @pl.when(self.me >= self.size // 2)
        def _():
            self.sweep(k, 0)

    def result(self, k, out):
        last = self.size - 1
        out[...] = self.part(k, self.me)[...].astype(jnp.float32)

        @pl.when(self.me > 0)
        def _():
            out[...] += self.inbox(0, k, self.me)[...].astype(jnp.float32)

        @pl.when(self.me < last)
        def _():
            out[...] += self.inbox(1, k, self.me)[...].astype(jnp.float32)

    def finish(self, k):
        last = self.size - 1
        for j in range(self.size):
            for way in range(2):
                sent = (j > self.me) if way == 0 else (j < self.me)

                @pl.when(sent)
                def _():
                    self.copy(way, k, j).wait_send()


def bit_orders(size):
    bits = [1 << i for i in range(size.bit_length() - 1)]
    bits.reverse()
    half = max(1, len(bits) // 2)
    if len(bits) == 3:
        return [bits, [bits[1], bits[0], bits[2]]]
    return [bits, bits[half:] + bits[:half]]


class PlaneGather:
    def __init__(self, own, slot, sems, orders):
        self.size, self.me = lax.axis_size("expert"), lax.axis_index("expert")
        self.own, self.slot, self.sems, self.orders = own, slot, sems, orders

    def place(self, h, mask):
        return max(at for at, bit in enumerate(self.orders[h]) if mask & bit)

    def copy(self, h, mask):
        last = self.orders[h][self.place(h, mask)]
        block = flipped(self.me, mask - last)
        src = self.own(h) if mask == last else self.slot(h, block)
        return remote(
            src,
            self.slot(h, block),
            self.sems.at[0, h, mask],
            self.sems.at[1, h, mask],
            "expert",
            flipped(self.me, last),
        )

    def wait(self, h, mask):
        here = self.slot(h, flipped(self.me, mask))
        remote(
            here, here, self.sems.at[0, h, mask], self.sems.at[1, h, mask], "expert", flipped(self.me, 1)
        ).wait_recv()

    def start(self, some=None):
        for at in range(len(self.orders[0])):
            for h, order in enumerate(self.orders):
                if some is None or h in some:
                    self.copy(h, order[at]).start()

    def moves(self):
        found = [(h, mask) for h in range(len(self.orders)) for mask in range(1, self.size)]
        found.sort(key=lambda move: (move[1].bit_count(), self.place(*move), move[0]))
        return found

    def move(self, h, mask):
        self.wait(h, mask)
        for bit in self.orders[h][self.place(h, mask) + 1 :]:
            self.copy(h, mask | bit).start()

    def relay(self):
        for h, mask in self.moves():
            self.move(h, mask)

    def finish(self):
        for h in range(len(self.orders)):
            for mask in range(1, self.size):
                self.copy(h, mask).wait_send()


class PlaneReduce:
    def __init__(self, acc, inbox, sems, orders):
        self.size, self.me = lax.axis_size("expert"), lax.axis_index("expert")
        self.acc, self.inbox, self.sems, self.orders = acc, inbox, sems, orders

    def masks(self, h, at):
        later = self.orders[h][at + 1 :]
        found = [0]
        for bit in later:
            found = found + [mask | bit for mask in found]
        return sorted(found, key=lambda mask: (mask == 0, self.first(h, mask) if mask else 0))

    def first(self, h, mask):
        return min(at for at, bit in enumerate(self.orders[h]) if mask & bit)

    def number(self, h, at, mask):
        before = sum(self.size >> (step + 1) for step in range(at))
        return before + sorted(self.masks(h, at)).index(mask)

    def copy(self, h, at, mask):
        bit = self.orders[h][at]
        n = self.number(h, at, mask)
        return remote(
            self.acc(h, flipped(self.me, mask | bit)),
            self.inbox(h, n),
            self.sems.at[0, h, n],
            self.sems.at[1, h, n],
            "expert",
            flipped(self.me, bit),
        )

    def start(self, h):
        for mask in self.masks(h, 0):
            self.copy(h, 0, mask).start()

    def advance(self, h, at):
        for mask in self.masks(h, at):
            self.copy(h, at, mask).wait_recv()
            if mask:
                here = self.acc(h, flipped(self.me, mask))
                arrived = self.inbox(h, self.number(h, at, mask))
                here[...] = (
                    here[...].astype(jnp.float32) + arrived[...].astype(jnp.float32)
                ).astype(here.dtype)
                if self.first(h, mask) == at + 1:
                    self.copy(h, at + 1, mask - self.orders[h][at + 1]).start()

    def result(self, h, out):
        total = self.acc(h, self.me)[...].astype(jnp.float32)
        for at in range(len(self.orders[h])):
            total = total + self.inbox(h, self.number(h, at, 0))[...].astype(jnp.float32)
        out[...] = total

    def finish(self, h):
        for at in range(len(self.orders[h])):
            for mask in self.masks(h, at):
                self.copy(h, at, mask).wait_send()


def part_of(ref, item, rows, width):
    chunk, low, wide = item
    if wide == width:
        return ref.at[chunk, rows]
    return ref.at[chunk, rows, pl.ds(low, wide)]


def halved(chunks, width, at):
    items = []
    for c in range(chunks):
        if c == at and width >= 256:
            items += [(c, 0, width // 2), (c, width // 2, width // 2)]
        else:
            items.append((c, 0, width))
    return items


def vmem(shape, dtype):
    return pltpu.VMEM(shape, dtype)


def dma(*shape):
    return pltpu.SemaphoreType.DMA(shape)


def call(kernel, outs, scratch, number, *operands):
    whole = pl.BlockSpec(memory_space=pltpu.VMEM)
    return pl.pallas_call(
        kernel,
        out_shape=outs,
        in_specs=[whole] * len(operands),
        out_specs=jax.tree.map(lambda _: whole, outs),
        scratch_shapes=scratch,
        compiler_params=pltpu.CompilerParams(
            collective_id=number, has_side_effects=True, vmem_limit_bytes=VMEM_LIMIT
        ),
    )(*operands)


class PlaneExchange:
    def __init__(self, src, dst, sems):
        self.size, self.me = lax.axis_size("expert"), lax.axis_index("expert")
        self.src, self.dst, self.sems = src, dst, sems

    def copy(self, k, peer):
        return remote(
            self.src(k, peer),
            self.dst(k, self.me),
            self.sems.at[0, k, peer],
            self.sems.at[1, k, self.me],
            "expert",
            peer,
        )

    def peers(self):
        order = sorted(range(1, self.size), key=lambda mask: (mask == 1, -mask.bit_count()))
        return [flipped(self.me, mask) for mask in order]

    def start(self, k):
        for peer in self.peers():
            self.copy(k, peer).start()

    def keep(self, k):
        self.dst(k, self.me)[...] = self.src(k, self.me)[...]

    def wait(self, k):
        for peer in self.peers():
            here = self.dst(k, peer)
            remote(
                here, here, self.sems.at[0, k, peer], self.sems.at[1, k, peer], "expert", peer
            ).wait_recv()

    def finish(self, k):
        for peer in self.peers():
            self.copy(k, peer).wait_send()


def combine(values, select, slots, number):
    data, group = lax.axis_size("dp"), lax.axis_size("expert")
    chunks, entries, width = values.shape
    rows = select.shape[1] // data
    window = 1

    def kernel(v_ref, select, out_ref, turned, back, part, inbox, ls, es):
        greet()
        exchange = PlaneExchange(
            lambda k, p: v_ref.at[k, pl.ds(pl.multiple_of(p * slots, slots), slots)],
            lambda k, p: back.at[k, pl.ds(pl.multiple_of(p * slots, slots), slots)],
            es,
        )
        line = LineReduce(
            lambda k, j: part.at[k, pl.ds(pl.multiple_of(j * rows, rows), rows)],
            lambda way, k, j: inbox.at[k, j + 1 - way],
            ls,
        )
        for k in range(window):
            exchange.start(k)
        turned[...] = select[...].T
        for k in range(chunks):
            exchange.keep(k)
        for k in range(chunks):
            exchange.wait(k)
            if k + window < chunks:
                exchange.start(k + window)
            total = jnp.dot(
                turned[...], back[k], preferred_element_type=jnp.float32
            )
            part[k] = total.astype(jnp.bfloat16)
            line.begin(k)
            line.near(k)
            if k:
                line.far(k - 1)
        line.far(chunks - 1)
        for k in range(chunks):
            line.result(k, out_ref.at[:, pl.ds(k * width, width)])
            line.finish(k)
            exchange.finish(k)

    return call(
        kernel,
        jax.ShapeDtypeStruct((rows, chunks * width), jnp.float32),
        [
            vmem(select.shape[::-1], jnp.bfloat16),
            vmem(values.shape, jnp.bfloat16),
            vmem((chunks, data * rows, width), jnp.bfloat16),
            vmem((chunks, data + 1, rows, width), jnp.bfloat16),
            dma(4, chunks, data),
            dma(2, chunks, group),
        ],
        number,
        values,
        select,
    )


def expert_layer(
    second, pair, probs, hidden, out_grad, gain, w_router, select, grads_here,
    w_gate, w_up, w_down, cut, with_mix,
):
    data, group = lax.axis_size("dp"), lax.axis_size("expert")
    chunks, rows, width = second.shape
    model = chunks * width
    experts = w_router.shape[0]
    extra = pair.shape[1]
    entries = select.shape[0]
    slots = entries // group
    hidden_units = w_gate.shape[1]
    block = 2 * slots
    pieces = model // cut
    early = max(1, chunks // 2)
    came = halved(chunks, width, 0)
    sent = halved(chunks, width, chunks - 1)

    def kernel(
        sec_ref, pair_ref, prob_ref, hid_ref, g_ref, gain_ref, r_ref, select, gh_any, wg_any, wu_any, wd_any,
        d_any, s_any, a_any, v_any, grad_hidden, branch_any, norm_sum, router_sum, turned_any, mix_out,
        x_all, pair_all, picked_pair, pair_here, rows_out, pair_out, back, pair_back,
        inbox, pair_box, summed, pair_sum, turned, low, wg, wu, wd,
        x_here, g_stage, s_stage, v_stage, a_stage, grad_h, d_stage,
        mix_back, loads, g_load, stores, keeps, d_s, ls, es, ls2, es2, es3,
    ):
        place, plane = lax.axis_index("dp"), lax.axis_index("expert")
        own = place * group + plane
        pairs = group // 2
        fetches = [
            pltpu.make_async_copy(src, dst, loads.at[at])
            for at, (src, dst) in enumerate(((wg_any, wg), (wu_any, wu), (wd_any, wd)))
        ]

        def block_at(step):
            mask, at, bit = pairs - 1 - step, 0, 1
            while bit < pairs:
                at = at + bit * ((plane // (2 * bit) + mask // bit) % 2)
                bit *= 2
            return at

        def block_rows(step):
            at = block_at(step)
            return pl.ds(pl.multiple_of(at * block, block), block)

        def load_grads(step):
            slot = step % 2
            return pltpu.make_async_copy(
                gh_any.at[:, block_rows(step)], g_stage.at[slot], g_load.at[slot]
            )

        def store_block(step):
            slot, here = step % 2, block_rows(step)
            return [
                pltpu.make_async_copy(s_stage.at[slot], s_any.at[:, here], stores.at[slot, 0]),
                pltpu.make_async_copy(v_stage.at[slot], v_any.at[:, here], stores.at[slot, 1]),
                pltpu.make_async_copy(a_stage.at[slot], a_any.at[here], stores.at[slot, 2]),
            ]

        load_grads(0).start()
        for fetch in fetches:
            fetch.start()
        mine = pl.ds(pl.multiple_of(place * rows, rows), rows)
        for c in range(chunks):
            x_all[c, mine] = sec_ref[c]
        pair_all[mine] = pair_ref[...]
        greet()

        def slot_rows(p):
            return pl.ds(pl.multiple_of(p * slots, slots), slots)

        def token_rows(j):
            return pl.ds(pl.multiple_of(j * rows, rows), rows)

        def pick(items, full, wide):
            return lambda k, p: (
                part_of(full, items[k], slot_rows(p), width)
                if k < len(items)
                else wide.at[slot_rows(p)]
            )

        exchange = PlaneExchange(
            pick(came, rows_out, picked_pair), pick(came, x_here, pair_here), es
        )

        def done(k):
            if k == 0:
                picked_pair[...] = jnp.dot(
                    select[...], pair_all[...], preferred_element_type=jnp.float32
                ).astype(jnp.bfloat16)
                exchange.start(len(came))
                exchange.keep(len(came))
            else:
                c, at, wide = came[k - 1]
                rows_out[c, :, at : at + wide] = jnp.dot(
                    select[...], x_all[c, :, at : at + wide], preferred_element_type=jnp.float32
                ).astype(jnp.bfloat16)
                exchange.start(k - 1)
                exchange.keep(k - 1)

        line = LineGather(
            lambda k: (
                pair_ref if k == 0 else part_of(sec_ref, came[k - 1], pl.ds(0, rows), width)
            ),
            lambda k, j: (
                pair_all.at[token_rows(j)]
                if k == 0
                else part_of(x_all, came[k - 1], token_rows(j), width)
            ),
            ls,
        )
        line.run(len(came) + 1, 3, done)
        turned[...] = select[...].T
        keep_turned = pltpu.make_async_copy(turned, turned_any, keeps.at[2])
        keep_turned.start()
        for fetch in fetches:
            fetch.wait()
        for k in range(len(came) + 1):
            exchange.wait(k)
        for k in range(len(came) + 1):
            exchange.finish(k)

        give_back = PlaneExchange(
            pick(sent, rows_out, pair_out), pick(sent, back, pair_back), es2
        )
        lane = lax.broadcasted_iota(jnp.int32, (block, extra), 1)

        def run_block(step, carry):
            at = block_at(step)
            here = block_rows(step)
            slot = step % 2
            load_grads(step).wait()

            @pl.when(step + 1 < pairs)
            def _():
                load_grads(step + 1).start()

            @pl.when(step >= 2)
            def _():
                for store in store_block(step - 2):
                    store.wait()

            chosen = (lane == own) | (lane == own + experts)
            prob = jnp.sum(
                jnp.where(chosen, pair_here[here].astype(jnp.float32), 0.0), axis=-1, keepdims=True
            )
            gate_h = jnp.zeros((block, hidden_units), jnp.float32)
            up_h = jnp.zeros((block, hidden_units), jnp.float32)
            for c in range(chunks):
                x = x_here[c, here]
                part = pl.ds(c * width, width)
                gate_h += jnp.dot(x, wg[part], preferred_element_type=jnp.float32)
                up_h += jnp.dot(x, wu[part], preferred_element_type=jnp.float32)
            sigmoid = jax.nn.sigmoid(gate_h)
            silu = gate_h * sigmoid
            active = (silu * up_h).astype(jnp.bfloat16)
            a_stage[slot] = active
            grad_active = jnp.zeros((block, hidden_units), jnp.float32)
            slot_gate = jnp.zeros((block, 1), jnp.float32)
            for c in range(chunks):
                part = pl.ds(c * width, width)
                out = jnp.dot(active, wd[:, part], preferred_element_type=jnp.float32)
                out = out.astype(jnp.bfloat16).astype(jnp.float32)
                grad = g_stage[slot, c].astype(jnp.float32)
                slot_gate += jnp.sum(out * grad, axis=-1, keepdims=True)
                v_stage[slot, c] = (prob * out).astype(jnp.bfloat16)
                grad_slot = (prob * grad).astype(jnp.bfloat16)
                s_stage[slot, c] = grad_slot
                grad_active += nt_dot(grad_slot, wd[:, part])
            grad_gate_h = grad_active * up_h * sigmoid * (1.0 + gate_h * (1.0 - sigmoid))
            grad_gate_h = grad_gate_h.astype(jnp.bfloat16)
            grad_up_h = (grad_active * silu).astype(jnp.bfloat16)
            grad_h[0, here] = grad_gate_h
            grad_h[1, here] = grad_up_h
            for store in store_block(step):
                store.start()
            top = slot_gate.astype(jnp.bfloat16).astype(jnp.float32)
            pair_out[here] = (
                jnp.where(lane == own, top, 0.0)
                + jnp.where(lane == own + experts, slot_gate - top, 0.0)
            ).astype(jnp.bfloat16)
            for c in range(chunks):
                part = pl.ds(c * width, width)
                rows_out[c, here] = (
                    nt_dot(grad_gate_h, wg[part]) + nt_dot(grad_up_h, wu[part])
                ).astype(jnp.bfloat16)
            for member in range(2):
                peer = 2 * at + member

                @pl.when(peer != plane)
                def _():
                    for k in [len(sent)] + list(range(early)):
                        give_back.copy(k, peer).start()

            return carry

        lax.fori_loop(0, pairs, run_block, 0)
        def store_grads(c, side):
            return pltpu.make_async_copy(
                d_stage.at[side], d_any.at[side, pl.ds(c * width, width)], d_s.at[side]
            )

        def weight_grads(c):
            x = x_here[c].T
            for side in range(2):
                if c:
                    store_grads(c - 1, side).wait()
                d_stage[side] = jnp.dot(
                    x, grad_h[side], preferred_element_type=jnp.float32
                ).astype(jnp.bfloat16)
                store_grads(c, side).start()

        for step in range(max(0, pairs - 2), pairs):
            for store in store_block(step):
                store.wait()
        mix = PlaneExchange(
            lambda k, p: v_any.at[0, slot_rows(p)], lambda k, p: mix_back.at[slot_rows(p)], es3
        )
        own_mix = pltpu.make_async_copy(
            v_any.at[0, slot_rows(plane)], mix_back.at[slot_rows(plane)], keeps.at[3]
        ) if with_mix else None
        give_back.start(early)
        for k in range(len(sent) + 1):
            give_back.keep(k)
        sums = LineReduce(
            lambda k, j: (
                part_of(x_all, sent[k], token_rows(j), width)
                if k < len(sent)
                else pair_all.at[token_rows(j)]
            ),
            lambda way, k, j: (
                inbox.at[
                    sent[k][0], j + 1 - way, :, pl.ds(sent[k][1], sent[k][2])
                ]
                if k < len(sent)
                else pair_box.at[j + 1 - way]
            ),
            ls2,
        )
        order = [len(sent)] + list(range(len(sent)))

        def collect(k):
            if k < len(sent):
                c, low_col, wide = sent[k]
                sums.result(k, summed.at[:, pl.ds(c * width + low_col, wide)])
            else:
                sums.result(k, pair_sum)

        for at, k in enumerate(order):
            give_back.wait(k)
            if k < len(sent):
                c, low_col, wide = sent[k]
                x_all[c, :, low_col : low_col + wide] = jnp.dot(
                    turned[...],
                    back[c, :, low_col : low_col + wide],
                    preferred_element_type=jnp.float32,
                ).astype(jnp.bfloat16)
            else:
                pair_all[...] = jnp.dot(
                    turned[...], pair_back[...], preferred_element_type=jnp.float32
                ).astype(jnp.bfloat16)
            sums.begin(k)
            if k < len(sent) and early + 1 + k < len(sent):
                give_back.start(early + 1 + k)
            if at >= 1:
                sums.near(order[at - 1])
            if at >= 2:
                sums.far(order[at - 2])
                collect(order[at - 2])
            if at == 0:
                weight_grads(0)
            if at + 1 < chunks:
                weight_grads(at + 1)
        if with_mix:
            mix.start(0)
            own_mix.start()
        sums.near(order[-1])
        for k in order[-2:]:
            sums.far(k)
            collect(k)

        gate = prob_ref[...]
        grad_gate = pair_sum[:, 0:experts] + pair_sum[:, experts : 2 * experts]
        inner = jnp.sum(gate * grad_gate, axis=-1, keepdims=True)
        grad_logits = (gate * (grad_gate - inner)).astype(jnp.bfloat16)
        for c in range(chunks):
            part = pl.ds(c * width, width)
            router_sum[:, part] = lax.dot_general(
                grad_logits,
                sec_ref[c],
                (((0,), (0,)), ((), ())),
                preferred_element_type=jnp.float32,
            )
        grad_second = summed[...] + jnp.dot(
            grad_logits, r_ref[...], preferred_element_type=jnp.float32
        )
        state = hid_ref[...]
        scale = row_scale(state)
        norm_sum[...] = jnp.sum(grad_second * state * scale, axis=0, keepdims=True)
        scaled = grad_second * gain_ref[...]
        inner = jnp.mean(scaled * state, axis=-1, keepdims=True)
        total = scale * scaled - state * (scale * scale * scale * inner)
        total = total + g_ref[...].astype(jnp.float32)
        grad_hidden[...] = total
        total = total.astype(jnp.bfloat16)
        for piece in range(pieces):
            low[piece] = total[:, piece * cut : (piece + 1) * cut]
        keep_low = pltpu.make_async_copy(low, branch_any, keeps.at[1])
        keep_low.start()
        if with_mix:
            own_mix.wait()
            mix.wait(0)
            mix_out[...] = jnp.dot(
                turned[...], mix_back[...], preferred_element_type=jnp.float32
            ).astype(jnp.bfloat16)
            mix.finish(0)
        for side in range(2):
            store_grads(chunks - 1, side).wait()
        keep_turned.wait()
        keep_low.wait()
        for k in range(len(sent) + 1):
            sums.finish(k)
            give_back.finish(k)

    bf, fl = jnp.bfloat16, jnp.float32
    whole = pl.BlockSpec(memory_space=pltpu.VMEM)
    anywhere = pl.BlockSpec(memory_space=pl.ANY)
    outs = [
        jax.ShapeDtypeStruct((2, model, hidden_units), bf),
        jax.ShapeDtypeStruct((chunks, entries, width), bf),
        jax.ShapeDtypeStruct((entries, hidden_units), bf),
        jax.ShapeDtypeStruct((chunks, entries, width), bf),
        jax.ShapeDtypeStruct((rows, model), fl),
        jax.ShapeDtypeStruct((pieces, rows, cut), bf),
        jax.ShapeDtypeStruct((1, model), fl),
        jax.ShapeDtypeStruct((experts, model), fl),
        jax.ShapeDtypeStruct(select.shape[::-1], bf),
        jax.ShapeDtypeStruct((data * rows if with_mix else 16, width), bf),
    ]
    results = list(pl.pallas_call(
        kernel,
        out_shape=outs,
        in_specs=[whole] * 8 + [anywhere] * 4,
        out_specs=[anywhere] * 4 + [whole, anywhere, whole, whole, anywhere, whole],
        scratch_shapes=[
            vmem((chunks, data * rows, width), bf),
            vmem((data * rows, extra), bf),
            vmem((entries, extra), bf),
            vmem((entries, extra), bf),
            vmem((chunks, entries, width), bf),
            vmem((entries, extra), bf),
            vmem((chunks, entries, width), bf),
            vmem((entries, extra), bf),
            vmem((chunks, data + 1, rows, width), bf),
            vmem((data + 1, rows, extra), bf),
            vmem((rows, model), fl),
            vmem((rows, extra), fl),
            vmem(select.shape[::-1], bf),
            vmem((pieces, rows, cut), bf),
            vmem((model, hidden_units), bf),
            vmem((model, hidden_units), bf),
            vmem((hidden_units, model), bf),
            vmem((chunks, entries, width), bf),
            vmem((2, chunks, block, width), bf),
            vmem((2, chunks, block, width), bf),
            vmem((2, chunks, block, width), bf),
            vmem((2, block, hidden_units), bf),
            vmem((2, entries, hidden_units), bf),
            vmem((2, width, hidden_units), bf),
            vmem((entries if with_mix else 16, width), bf),
            dma(3),
            dma(2),
            dma(2, 3),
            dma(4),
            dma(2),
            dma(4, len(came) + 1, data - 1),
            dma(2, len(came) + 1, group),
            dma(4, len(sent) + 1, data),
            dma(2, len(sent) + 1, group),
            dma(2, 1, group),
        ],
        compiler_params=pltpu.CompilerParams(
            collective_id=3, has_side_effects=True, vmem_limit_bytes=VMEM_LIMIT
        ),
    )(
        second, pair, probs, hidden, out_grad, gain, w_router, select, grads_here,
        w_gate, w_up, w_down,
    ))
    return results


def expert_weight_grads(grad_h, grad_arrived, act, others, kv, small):
    chunks, entries, width = grad_arrived.shape
    hidden_units = act.shape[1]
    part = kv.shape[0] // 2
    passed = len(others) + 2 + len(small)

    def kernel(h_ref, s_ref, act_ref, *refs):
        sources = refs[:passed]
        gate_out, up_out, down_out = refs[passed : passed + 3]
        targets = refs[passed + 3 : 2 * passed + 3]
        turned = refs[2 * passed + 3]

        @pl.when(pl.program_id(0) == 0)
        def _():
            turned[...] = act_ref[...].T

        for source, target in zip(sources, targets):
            target[...] = source[...]
        gate_out[0] = h_ref[0].astype(jnp.float32)
        up_out[0] = h_ref[1].astype(jnp.float32)
        down_out[0] = jnp.dot(turned[...], s_ref[0], preferred_element_type=jnp.float32)

    tall = pl.BlockSpec((1, width, hidden_units), lambda c: (0, c, 0))

    def slab(lines, item, first=0):
        return pl.BlockSpec((lines // chunks, item.shape[1]), lambda c: (c + first, 0))

    slabs = [slab(item.shape[0], item) for item in others]
    half = slab(part, kv)
    whole = [pl.BlockSpec(item.shape, lambda c: (0, 0)) for item in small]
    return pl.pallas_call(
        kernel,
        grid=(chunks,),
        out_shape=[
            jax.ShapeDtypeStruct((1, chunks * width, hidden_units), jnp.float32),
            jax.ShapeDtypeStruct((1, chunks * width, hidden_units), jnp.float32),
            jax.ShapeDtypeStruct((1, hidden_units, chunks * width), jnp.float32),
        ]
        + [jax.ShapeDtypeStruct(item.shape, item.dtype) for item in others]
        + [jax.ShapeDtypeStruct((part, kv.shape[1]), kv.dtype)] * 2
        + [jax.ShapeDtypeStruct(item.shape, item.dtype) for item in small],
        in_specs=[
            pl.BlockSpec((2, width, hidden_units), lambda c: (0, c, 0)),
            pl.BlockSpec((1, entries, width), lambda c: (c, 0, 0)),
            pl.BlockSpec((entries, hidden_units), lambda c: (0, 0)),
        ]
        + slabs
        + [half, slab(part, kv, chunks)]
        + whole,
        out_specs=[tall, tall, pl.BlockSpec((1, hidden_units, width), lambda c: (0, 0, c))]
        + slabs
        + [half, half]
        + whole,
        scratch_shapes=[vmem((hidden_units, entries), jnp.bfloat16)],
        compiler_params=pltpu.CompilerParams(vmem_limit_bytes=VMEM_LIMIT),
    )(grad_h, grad_arrived, act, *others, kv, kv, *small)


def attention_backward(
    grad_branch, out_blocks, x, w_q, w_kv, q_raw, q_low, k_raw, k_low, v_low, lse, att,
    cos, sin, gain_q, gain_k, mixed, turned, tokens, gain, grad_hidden, hidden, norm2_sum, router_sum, first_mix,
    seq_len, with_mix,
):
    data, group = lax.axis_size("dp"), lax.axis_size("expert")
    pieces, rows, cut = grad_branch.shape
    chunks, total, width = x.shape
    model = chunks * width
    depth = model // data
    wide = w_q.shape[1]
    sharing, _, both, _ = w_kv.shape
    part = both // 2
    head = sharing * part
    heads = wide // head
    block = min(256, seq_len)
    scale = head ** (-0.5)
    entries = turned.shape[1]
    slots = entries // group
    orders = [order[::-1] for order in bit_orders(group)]
    orders = [orders[at % 2] for at in range(chunks)]
    steps = len(orders[0])

    def kernel(
        gb_ref, wo_any, x_any, wq_any, wkv_any, qr_any, ql_any, kr_any, kl_any, vl_any, lse_any, att_ref,
        cos_ref, sin_ref, gq_ref, gk_ref, mix_any, turned_any, tok_ref, gain_ref, gh_any, hid_ref, n2_ref, rt_any, fm_ref,
        tok_out, wo_out, wq_out, wkv_out, gq_out, gk_out, n1_out, n2_out, rt_out, layer_out,
        wo_ref, x_ref, wq_ref, wkv_ref, ql_ref, kr_ref, kl_ref, vl_ref, lse_ref, turned,
        big, row_terms, log_rows, dq_low, dk, dv, dkv_low, kv_box, raw_buf,
        wo_part, wo_box, w_part, w_box, kv_part, kv_inbox, dx_box, back,
        mix_part, mix_box, summed, dx_sum, vec, vec_plane, vec_half, vec_line, rt_acc, rt_box, rt_half, rt_line, gq_sum, gk_sum,
        loads, raw_load, keep_s, wo_s, w_s, kv_s, sib_s, dx_s, ex_s, mix_s, vp_s, vl_s, rp_s, rl_s, rg_s, gb_s,
    ):
        place, plane = lax.axis_index("dp"), lax.axis_index("expert")
        member = plane % sharing

        def branch(j):
            first = j * cut
            return big.at[first // width, :, pl.ds(first % width, cut)]

        fetches = [
            pltpu.make_async_copy(src, dst, loads.at[at])
            for at, (src, dst) in enumerate(
                (
                    (rt_any, rt_acc),
                    (wo_any, wo_ref),
                    (ql_any, ql_ref),
                    (kl_any, kl_ref),
                    (vl_any, vl_ref),
                    (lse_any, lse_ref),
                    (x_any, x_ref),
                    (kr_any, kr_ref),
                    (wq_any, wq_ref),
                    (wkv_any, wkv_ref),
                    (gh_any, tok_out),
                )
            )
        ]
        for fetch in fetches:
            fetch.start()
        if with_mix:
            turned_load = pltpu.make_async_copy(turned_any, turned, loads.at[len(fetches)])
            turned_load.start()

        def load_raw(h):
            mine = pl.ds(pl.multiple_of(h * head, head), head)
            return pltpu.make_async_copy(qr_any.at[:, mine], raw_buf.at[h % 2], raw_load.at[h % 2])

        load_raw(0).start()

        def slot_rows(p):
            return pl.ds(pl.multiple_of(p * slots, slots), slots)

        def token_rows(j):
            return pl.ds(pl.multiple_of(j * rows, rows), rows)

        exchange = PlaneExchange(
            lambda k, p: mix_any.at[k, slot_rows(p)], lambda k, p: back.at[k, slot_rows(p)], ex_s
        )
        wo_sum = LineReduce(
            lambda k, j: wo_part.at[j, pl.ds(k * (wide // 2), wide // 2)],
            lambda way, k, j: wo_box.at[j + 1 - way, pl.ds(k * (wide // 2), wide // 2)],
            wo_s,
        )
        w_sum = LineReduce(
            lambda k, j: w_part.at[k, j], lambda way, k, j: w_box.at[k, j + 1 - way], w_s
        )
        kv_sum = LineReduce(
            lambda k, j: kv_part.at[j], lambda way, k, j: kv_inbox.at[j + 1 - way], kv_s
        )
        reduce = PlaneReduce(
            lambda h, j: big.at[h, token_rows(j)], lambda h, n: dx_box.at[h, n], dx_s, orders
        )

        mix_sum = LineReduce(
            lambda k, j: mix_part.at[k, token_rows(j)],
            lambda way, k, j: mix_box.at[k, j + 1 - way],
            mix_s,
        )
        share = model // group

        def share_cols(j):
            return pl.ds(pl.multiple_of(j * share, share), share)

        router = PlaneReduce(
            lambda h, j: rt_acc.at[:, share_cols(j)], lambda h, n: rt_box.at[n], rp_s, orders[:1]
        )
        router_back = PlaneGather(
            lambda h: rt_half.at[1],
            lambda h, j: rt_out.at[:, share_cols(j)],
            rg_s,
            bit_orders(group)[:1],
        )

        def router_line(step):
            return remote(
                rt_half.at[0], rt_line.at[step], rl_s.at[0, step], rl_s.at[1, step],
                "dp", (place + step) % data,
            )

        def router_stage(at):
            if at < steps:
                router.advance(0, at)
            elif at == steps:
                router.result(0, rt_half.at[0])
                for step in range(1, data):
                    router_line(step).start()
            elif at == steps + 1:
                total = rt_half[0]
                for step in range(1, data):
                    router_line(step).wait_recv()
                    total = total + rt_line[step]
                rt_half[1] = total
                rt_out[:, share_cols(plane)] = total
                router_back.start()
            else:
                router_back.relay()

        def vec_across(mask):
            return remote(
                vec, vec_plane.at[mask], vp_s.at[0, mask], vp_s.at[1, mask],
                "expert", flipped(plane, mask),
            )

        def vec_along(step):
            return remote(
                vec_half, vec_line.at[step], vl_s.at[0, step], vl_s.at[1, step],
                "dp", (place + step) % data,
            )

        def x_block(j):
            first = j * depth
            inner = first % width
            return x_ref[first // width, :, inner : inner + depth]

        own_rows = token_rows(plane)
        for h in range(pieces):
            branch(h)[own_rows] = gb_ref[h]
        if with_mix:
            mix_part[0] = fm_ref[...]
        greet(far=True)
        if with_mix:
            mix_sum.begin(0)
        gather = PlaneGather(
            lambda h: gb_ref.at[h],
            lambda h, j: big.at[
                (h * cut) // width, token_rows(j), pl.ds((h * cut) % width, cut)
            ],
            gb_s,
            [bit_orders(group)[at % 2] for at in range(pieces)],
        )
        pairs = [range(h, min(h + 2, pieces)) for h in range(0, pieces, 2)]
        gather.start(pairs[0])
        fetches[0].wait()
        att_turned = att_ref[...].T

        def wo_piece(j):
            wo_part[j] = jnp.dot(
                att_turned, branch(j)[...], preferred_element_type=jnp.float32
            ).astype(jnp.bfloat16)
            for k in range(2):
                wo_sum.begin_block(k, j)

        for at, pair in enumerate(pairs):
            moves = [move for move in gather.moves() if move[0] in pair]
            first = [move for move in moves if move[1].bit_count() == 1]
            for move in first:
                gather.move(*move)
            if at + 1 < len(pairs):
                gather.start(pairs[at + 1])
            for move in moves[len(first) :]:
                gather.move(*move)
            for h in pair:
                wo_piece(h)
        router.start(0)
        if with_mix:
            if chunks > 1:
                exchange.start(1)
            mix_sum.near(0)
        fetches[1].wait()

        lane = lax.broadcasted_iota(jnp.int32, (block, head), 1)

        def attended_grad(at, carry):
            here = pl.ds(pl.multiple_of(at * block, block), block)
            value = jnp.zeros((block, wide), jnp.float32)
            for j in range(pieces):
                value += nt_dot(branch(j)[here], wo_ref[j])
            low = value.astype(jnp.bfloat16)
            dq_low[here] = low
            both_rows = low.astype(jnp.float32) * att_ref[here].astype(jnp.float32)
            terms = jnp.zeros((block, head), jnp.float32)
            for h in range(heads):
                term = jnp.sum(both_rows[:, h * head : (h + 1) * head], axis=-1, keepdims=True)
                terms = jnp.where(lane == h, term, terms)
            dk[here] = terms
            return carry

        lax.fori_loop(0, total // block, attended_grad, 0)
        for at in range(2, 7):
            fetches[at].wait()
        row_terms[...] = dk[...].T
        log_rows[...] = lse_ref[...].T * LOG2_E
        dk[...] = jnp.zeros_like(dk)
        dv[...] = jnp.zeros_like(dv)
        above = lax.broadcasted_iota(
            jnp.int32, (block, block), 0
        ) <= lax.broadcasted_iota(jnp.int32, (block, block), 1)

        def turned_dot(left, right):
            return lax.dot_general(
                left, right, (((0,), (0,)), ((), ())), preferred_element_type=jnp.float32
            )

        def unrotate(value, table):
            return value * cos_ref[table] - half_turn(value) * sin_ref[table]

        def norm_back(turned_grad, raw, gain):
            factor = row_scale(raw)
            gain_term = jnp.sum(turned_grad * raw * factor, axis=0, keepdims=True)
            scaled = turned_grad * gain
            inner = jnp.mean(scaled * raw, axis=-1, keepdims=True)
            return factor * scaled - raw * (factor * factor * factor * inner), gain_term

        gq_sum[...] = jnp.zeros_like(gq_sum)
        gk_sum[...] = jnp.zeros_like(gk_sum)

        def own_mix(k):
            return pltpu.make_async_copy(
                mix_any.at[k, slot_rows(plane)], back.at[k, slot_rows(plane)], keep_s.at[k]
            )

        def gather_mix(k):
            own_mix(k).wait()
            exchange.wait(k)
            mix_part[k] = jnp.dot(
                turned[...], back[k], preferred_element_type=jnp.float32
            ).astype(jnp.bfloat16)
            mix_sum.begin(k)

        if with_mix:
            for k in range(1, chunks):
                own_mix(k).start()
            turned_load.wait()
            mix_sum.far(0)

        def head_back(h, carry):
            mine = pl.ds(pl.multiple_of(h * head, head), head)
            load_raw(h).wait()

            @pl.when(h + 1 < heads)
            def _():
                load_raw(h + 1).start()

            for seq in range(total // seq_len):
                base = seq * seq_len
                for at in range(seq_len // block):
                    here = pl.ds(base + at * block, block)
                    query = ql_ref[here, mine]
                    grad = dq_low[here, mine]
                    log_sum = log_rows[pl.ds(h, 1), here]
                    row_term = row_terms[pl.ds(h, 1), here]
                    grad_query = jnp.zeros((block, head), jnp.float32)
                    for other in range(at + 1):
                        behind = pl.ds(base + other * block, block)
                        key = kl_ref[behind]
                        probs = jnp.exp2(nt_dot(key, query) * (scale * LOG2_E) - log_sum)
                        if other == at:
                            probs = jnp.where(above, probs, 0.0)
                        grad_probs = nt_dot(vl_ref[behind], grad)
                        grad_scores = (probs * (grad_probs - row_term)).astype(jnp.bfloat16)
                        dv[behind] += jnp.dot(
                            probs.astype(jnp.bfloat16), grad, preferred_element_type=jnp.float32
                        )
                        dk[behind] += jnp.dot(
                            grad_scores, query, preferred_element_type=jnp.float32
                        )
                        grad_query += turned_dot(grad_scores, key)
                    grad_query = grad_query * scale
                    table = pl.ds(at * block, block)
                    raw_grad, gain_term = norm_back(
                        unrotate(grad_query, table), raw_buf[h % 2, here], gq_ref[...]
                    )
                    gq_sum[...] += gain_term
                    dq_low[here, mine] = raw_grad.astype(jnp.bfloat16)
            low_turned = dq_low[:, mine].T
            for j in range(data):
                w_part[h, j] = jnp.dot(
                    low_turned, x_block(j), preferred_element_type=jnp.float32
                ).astype(jnp.bfloat16)
            w_sum.begin(h)

            if with_mix:

                @pl.when(h + 2 < chunks)
                def _():
                    exchange.start(h + 2)

            if with_mix and heads > 2:

                @pl.when((h >= 2) & (h - 1 < chunks))
                def _():
                    gather_mix(h - 1)

            @pl.when(h == heads - 2)
            def _():
                wo_sum.near(0)

            @pl.when(h == heads - 1)
            def _():
                wo_sum.near(1)
                wo_sum.far(0)

            return carry

        lax.fori_loop(0, heads, head_back, 0)
        if with_mix:
            for k in range(heads + 2, chunks):
                exchange.start(k)
        for at in range(7, len(fetches)):
            fetches[at].wait()
        for at in range(total // block):
            here = pl.ds(at * block, block)
            table = pl.ds((at * block) % seq_len, block)
            raw_grad, gain_term = norm_back(
                unrotate(dk[here] * scale, table), kr_ref[here], gk_ref[...]
            )
            gk_sum[...] += gain_term
            value_grad = dv[here]
            for m in range(sharing):
                cols = slice(m * part, (m + 1) * part)
                dkv_low[m, here] = jnp.concatenate(
                    [raw_grad[:, cols], value_grad[:, cols]], axis=1
                ).astype(jnp.bfloat16)

        def swap(mask):
            other = flipped(plane, mask)
            return remote(
                dkv_low.at[other % sharing],
                kv_box.at[member],
                sib_s.at[0, mask],
                sib_s.at[1, mask],
                "expert",
                other,
            )

        for mask in range(1, sharing):
            swap(mask).start()
        gather.finish()
        for j in range(data):
            first = j * depth
            c, inner = first // width, first % width

            def input_grad(at, carry):
                here = pl.ds(pl.multiple_of(at * block, block), block)
                value = nt_dot(dq_low[here], wq_ref[pl.ds(first, depth)])
                for m in range(sharing):
                    value += jnp.dot(
                        dkv_low[m, here], wkv_ref[m, j], preferred_element_type=jnp.float32
                    )
                big[c, here, inner : inner + depth] = value.astype(jnp.bfloat16)
                return carry

            lax.fori_loop(0, total // block, input_grad, 0)
            if inner + depth == width:
                reduce.start(c)
        kv_box[member] = dkv_low[member]
        for mask in range(1, sharing):
            other = kv_box.at[flipped(plane, mask) % sharing]
            remote(
                other, other, sib_s.at[0, mask], sib_s.at[1, mask], "expert", flipped(plane, mask)
            ).wait_recv()
        kv_turned = [kv_box[m].T for m in range(sharing)]
        for j in range(data):
            block_x = x_block(j)
            value = sum(
                jnp.dot(item, block_x, preferred_element_type=jnp.float32) for item in kv_turned
            )
            kv_part[j] = value.astype(jnp.bfloat16)
        kv_sum.begin(0)
        mixed_at = min(chunks, max(1, heads - 1)) if with_mix else chunks
        for k in range(mixed_at, chunks - 1):
            gather_mix(k)
        for c in range(chunks):
            reduce.advance(c, 0)
        if with_mix and mixed_at < chunks:
            gather_mix(chunks - 1)
        wo_sum.far(1)
        w_sum.near(0)
        for at in range(1, steps):
            for c in range(chunks):
                reduce.advance(c, at)
        router_stage(0)
        for c in range(chunks):
            reduce.result(c, dx_sum.at[:, pl.ds(c * width, width)])
        state = tok_ref[...].astype(jnp.float32)
        grad_normed = dx_sum[...]
        raw_grad, gain_term = norm_back(grad_normed, state, gain_ref[...])
        tok_out[...] += raw_grad
        vec[...] = jnp.zeros_like(vec)
        for c in range(chunks):
            cols = slice(c * width, (c + 1) * width)
            vec[c : c + 1, 0:width] = gain_term[:, cols]
            vec[chunks + c : chunks + c + 1, 0:width] = n2_ref[:, cols]
        vec[0:1, width : width + head] = gq_sum[...]
        vec[1:2, width : width + head] = gk_sum[...]
        for mask in range(1, group):
            vec_across(mask).start()
        sweeps = [(w_sum, h) for h in range(heads)] + [(kv_sum, 0)]
        if with_mix:
            for k in range(1, chunks):
                place_at = heads - mixed_at + 2 * k
                sweeps.insert(place_at if k < mixed_at else len(sweeps), (mix_sum, k))

        def settle(line, k):
            if line is w_sum:
                w_sum.result(k, summed)
                wq_out[:, k * head : (k + 1) * head] = summed[...].T
            elif line is kv_sum:
                kv_sum.result(0, wkv_out)
            else:
                part_cols = pl.ds(k * width, width)
                mix_sum.result(k, dx_sum.at[:, part_cols])
                layer_out[:, part_cols] = (hid_ref[:, part_cols] + dx_sum[:, part_cols]).astype(
                    jnp.bfloat16
                )

        for k in range(2):
            wo_sum.result(k, wo_out.at[pl.ds(k * (wide // 2), wide // 2)])
        if with_mix:
            settle(mix_sum, 0)
        for at, (line, k) in enumerate(sweeps):
            if at == 2:
                all_sum = vec[...]
                for mask in range(1, group):
                    vec_across(mask).wait_recv()
                    all_sum = all_sum + vec_plane[mask]
                vec_half[...] = all_sum
                for step in range(1, data):
                    vec_along(step).start()
            if at:
                line.near(k)
                sweeps[at - 1][0].far(sweeps[at - 1][1])
                if at < steps + 3:
                    router_stage(at)
                settle(*sweeps[at - 1])
        sweeps[-1][0].far(sweeps[-1][1])
        settle(*sweeps[-1])
        for stage in range(max(1, min(len(sweeps), steps + 3)), steps + 3):
            router_stage(stage)
        all_sum = vec_half[...]
        for step in range(1, data):
            vec_along(step).wait_recv()
            all_sum = all_sum + vec_line[step]
        for c in range(chunks):
            for q in range(width // 128):
                at, cols = c * (width // 128) + q, slice(q * 128, (q + 1) * 128)
                n1_out[at : at + 1] = all_sum[c : c + 1, cols]
                n2_out[at : at + 1] = all_sum[chunks + c : chunks + c + 1, cols]
        gq_out[...] = all_sum[0:1, width : width + head]
        gk_out[...] = all_sum[1:2, width : width + head]
        for mask in range(1, group):
            vec_across(mask).wait_send()
        for step in range(1, data):
            vec_along(step).wait_send()
            router_line(step).wait_send()
        router.finish(0)
        router_back.finish()
        for k in range(2):
            wo_sum.finish(k)
        for h in range(heads):
            w_sum.finish(h)
        kv_sum.finish(0)
        for mask in range(1, sharing):
            swap(mask).wait_send()
        for c in range(chunks):
            reduce.finish(c)
        if with_mix:
            for k in range(chunks):
                mix_sum.finish(k)
                if k:
                    exchange.finish(k)

    bf, fl = jnp.bfloat16, jnp.float32
    whole = pl.BlockSpec(memory_space=pltpu.VMEM)
    anywhere = pl.BlockSpec(memory_space=pl.ANY)
    mix_entries = entries if with_mix else 16
    mix_rows = rows if with_mix else 16
    mix_all = data * rows if with_mix else 16
    experts = router_sum.shape[0]
    share = model // group
    lines = whole_up(2 * chunks, 8)
    outs = [
        jax.ShapeDtypeStruct((rows, model), fl),
        jax.ShapeDtypeStruct((wide, cut), fl),
        jax.ShapeDtypeStruct((depth, wide), fl),
        jax.ShapeDtypeStruct((both, depth), fl),
        jax.ShapeDtypeStruct((1, head), fl),
        jax.ShapeDtypeStruct((1, head), fl),
        jax.ShapeDtypeStruct((model // 128, 128), fl),
        jax.ShapeDtypeStruct((model // 128, 128), fl),
        jax.ShapeDtypeStruct((experts, model), fl),
        jax.ShapeDtypeStruct((mix_rows, model), bf),
    ]
    return pl.pallas_call(
        kernel,
        out_shape=outs,
        in_specs=[whole]
        + [anywhere] * 10
        + [whole] * 5
        + [anywhere] * 2
        + [whole] * 2
        + [anywhere, whole if with_mix else anywhere, whole, anywhere]
        + [whole if with_mix else anywhere],
        out_specs=[whole] * len(outs),
        scratch_shapes=[
            vmem(out_blocks.shape, bf),
            vmem(x.shape, bf),
            vmem(w_q.shape, bf),
            vmem(w_kv.shape, bf),
            vmem(q_low.shape, bf),
            vmem(k_raw.shape, fl),
            vmem(k_low.shape, bf),
            vmem(v_low.shape, bf),
            vmem(lse.shape, fl),
            vmem(turned.shape if with_mix else (16, 128), bf),
            vmem((chunks, total, width), bf),
            vmem((head, total), fl),
            vmem((head, total), fl),
            vmem((total, wide), bf),
            vmem((total, head), fl),
            vmem((total, head), fl),
            vmem((sharing, total, both), bf),
            vmem((sharing, total, both), bf),
            vmem((2, total, head), fl),
            vmem((data, wide, cut), bf),
            vmem((data + 1, wide, cut), bf),
            vmem((heads, data, head, depth), bf),
            vmem((heads, data + 1, head, depth), bf),
            vmem((data, both, depth), bf),
            vmem((data + 1, both, depth), bf),
            vmem((chunks, group - 1, rows, width), bf),
            vmem((chunks, mix_entries, width), bf),
            vmem((chunks, mix_all, width), bf),
            vmem((chunks, data + 1, mix_rows, width), bf),
            vmem((head, depth), fl),
            vmem((rows, model), fl),
            vmem((lines, width + head), fl),
            vmem((group, lines, width + head), fl),
            vmem((lines, width + head), fl),
            vmem((data, lines, width + head), fl),
            vmem((experts, model), fl),
            vmem((group - 1, experts, share), fl),
            vmem((2, experts, share), fl),
            vmem((data, experts, share), fl),
            vmem((1, head), fl),
            vmem((1, head), fl),
            dma(12),
            dma(2),
            dma(chunks),
            dma(4, 2, data),
            dma(4, heads, data),
            dma(4, 1, data),
            dma(2, sharing),
            dma(2, chunks, group - 1),
            dma(2, chunks, group),
            dma(4, chunks, data),
            dma(2, group),
            dma(2, data),
            dma(2, 1, group - 1),
            dma(2, data),
            dma(2, 1, group),
            dma(2, pieces, group),
        ],
        compiler_params=pltpu.CompilerParams(
            collective_id=7, has_side_effects=True, vmem_limit_bytes=VMEM_LIMIT
        ),
    )(
        grad_branch, out_blocks, x, w_q, w_kv, q_raw, q_low, k_raw, k_low, v_low, lse, att,
        cos, sin, gain_q, gain_k, mixed, turned, tokens, gain, grad_hidden, hidden, norm2_sum, router_sum, first_mix,
    )


def rope_arrays(seq_len, head_dim):
    half = head_dim // 2
    frequency = ROPE_THETA ** (-(np.arange(half) * 2.0) / head_dim)
    angles = np.arange(seq_len)[:, None] * frequency[None, :]
    cos = np.concatenate([np.cos(angles), np.cos(angles)], axis=1).astype(np.float32)
    sin = np.concatenate([-np.sin(angles), np.sin(angles)], axis=1).astype(np.float32)
    return cos, sin


def row_scale(value):
    return lax.rsqrt(jnp.mean(value * value, axis=-1, keepdims=True) + NORM_EPS)


def half_turn(value):
    return pltpu.roll(value, value.shape[-1] // 2, value.ndim - 1)


def nt_dot(left, right):
    return lax.dot_general(
        left, right, (((1,), (1,)), ((), ())), preferred_element_type=jnp.float32
    )


def causal(start, rows, keys):
    at_row = lax.broadcasted_iota(jnp.int32, (rows, keys), 0) + start
    return lax.broadcasted_iota(jnp.int32, (rows, keys), 1) <= at_row


class Always:
    def __init__(self, order):
        self.order = order

    def __getitem__(self, at):
        return self.order


def front(
    tokens, gain, w_q, w_k, w_v, w_out, out_grad, slot_rows, cos, sin, gain_q, gain_k,
    gain2, router, hot, capacity, slots, seq_len,
):
    data, group = lax.axis_size("dp"), lax.axis_size("expert")
    rows, model = tokens.shape
    width = min(512, model)
    chunks = model // width
    depth, wide = w_q.shape
    cut = w_out.shape[1]
    part = w_k.shape[0]
    both = 2 * part
    head = gain_q.shape[1]
    sharing = head // part
    heads = wide // head
    total = group * rows
    block = min(256, seq_len)
    scale = head ** (-0.5)
    experts = router.shape[0]
    extra = whole_up(2 * experts, 128)
    entries = group * slots
    x_orders = bit_orders(group)
    x_orders = [x_orders[at % 2] for at in range(chunks)]
    b_orders = [Always(order[::-1]) for order in bit_orders(group)]
    steps = len(b_orders[0][0])
    halves = 2
    deep = depth // halves
    first_grad = 2 + halves
    first_out = first_grad + chunks - 1
    first_last = first_out + 1
    last = [item for item in halved(chunks, width, chunks - 1) if item[0] == chunks - 1]
    items = first_last + len(last)

    def kernel(
        tok_ref, gain_ref, wq_ref, wk_ref, wv_ref, wo_ref, og_ref, s_ref, cos_ref, sin_ref, gq_ref, gk_ref,
        gain2_ref, r_ref, hot_ref,
        x_any, wq_any, wkv_any, wo_any, g_any, sel_any, qr_any, ql_any, kr_any, kl_any, vl_any, lse_any,
        att_any, hidden, second, pair, probs,
        x_own, g_own, kv_own, x_all, wq_all, wkv_all, wo_all, g_all, s_all, picked, g_here, select,
        q_raw, q_low, k_raw, k_low, v_low, lse, att, acc, inbox,
        ps, ls, es, ks, bs, outs,
    ):
        place, plane = lax.axis_index("dp"), lax.axis_index("expert")
        member = plane % sharing
        state = tok_ref[...].astype(jnp.float32)
        normed = (state * row_scale(state) * gain_ref[...]).astype(jnp.bfloat16)
        mine = pl.ds(pl.multiple_of(place * rows, rows), rows)
        own_rows = pl.ds(pl.multiple_of(plane * rows, rows), rows)
        for c in range(chunks):
            x_own[c] = normed[:, c * width : (c + 1) * width]
            x_all[c, own_rows] = x_own[c]
            g_own[c] = og_ref[:, c * width : (c + 1) * width]
            g_all[c, mine] = g_own[c]
        kv_own[0:part] = wk_ref[...]
        kv_own[part:both] = wv_ref[...]
        wq_all[place] = wq_ref[...]
        wkv_all[member, place] = kv_own[...]
        wo_all[place] = wo_ref[...]
        s_all[place] = s_ref[...]
        greet()

        def token_rows(j):
            return pl.ds(pl.multiple_of(j * rows, rows), rows)

        def slot_rows_of(p):
            return pl.ds(pl.multiple_of(p * slots, slots), slots)

        gather = PlaneGather(
            lambda h: x_own.at[h], lambda h, j: x_all.at[h, token_rows(j)], ps, x_orders
        )

        def is_grad(k):
            return not isinstance(k, int) or first_grad <= k < first_out

        def own(k):
            if is_grad(k):
                return g_own.at[k - first_grad]
            if k == 0:
                return s_ref
            if k == 1:
                return kv_own
            if k < first_grad:
                return wq_ref.at[pl.ds((k - 2) * deep, deep)]
            if k >= first_last:
                return part_of(g_own, last[k - first_last], pl.ds(0, rows), width)
            return wo_ref

        def slot(k, j):
            if is_grad(k):
                return g_all.at[k - first_grad, token_rows(j)]
            if k == 0:
                return s_all.at[j]
            if k == 1:
                return wkv_all.at[member, j]
            if k < first_grad:
                return wq_all.at[j, pl.ds((k - 2) * deep, deep)]
            if k >= first_last:
                return part_of(g_all, last[k - first_last], token_rows(j), width)
            return wo_all.at[j]

        line = LineGather(own, slot, ls)
        def exchanged(ref):
            return lambda k, p: (
                part_of(ref, last[k - chunks + 1], slot_rows_of(p), width)
                if isinstance(k, int) and k >= chunks - 1
                else ref.at[k, slot_rows_of(p)]
            )

        exchange = PlaneExchange(exchanged(picked), exchanged(g_here), es)
        turns_of_grads = chunks - 1 + len(last)
        reduces = [
            PlaneReduce(lambda h, j: acc.at[h, j], lambda h, n: inbox.at[h, n], bs, order)
            for order in b_orders
        ]
        keeps = {}

        def keep(name, src, dst):
            keeps[name] = pltpu.make_async_copy(src, dst, outs.at[len(keeps)])
            keeps[name].start()

        def share(mask):
            return remote(
                wkv_all.at[member], wkv_all.at[member], ks.at[0, mask], ks.at[1, mask],
                "expert", flipped(plane, mask),
            )

        gather.start()
        for k in range(first_grad):
            line.start(k)
        moves = gather.moves()
        for s in range(1, data):
            line.step(0, s)
        wanted = lax.broadcasted_iota(jnp.int32, (slots, rows), 0).astype(jnp.float32)
        for j in range(data):
            for peer in range(group):
                row = s_all[j, pl.ds(pl.multiple_of(place * group, 8), group)][peer : peer + 1]
                row = jnp.where(row >= 0, row + j * capacity, -1.0)
                select[pl.ds(peer * slots, slots), pl.ds(j * rows, rows)] = jnp.where(
                    wanted == row, 1.0, 0.0
                ).astype(jnp.bfloat16)
        for k in range(first_grad, min(first_grad + 2, first_out)):
            line.start(k)
        taken = 0
        turns = [(k, s) for k in range(1, first_grad) for s in range(1, data)]
        for at, (k, s) in enumerate(turns):
            until = len(moves) * (at + 1) // len(turns)
            for move in moves[taken:until]:
                gather.move(*move)
            taken = until
            line.step(k, s)
            if k == 1 and s == data - 1:
                for mask in range(1, sharing):
                    share(mask).start()
        for k in range(first_grad + 2, first_out):
            line.start(k)
        for mask in range(1, sharing):
            other = wkv_all.at[flipped(plane, mask) % sharing]
            remote(
                other, other, ks.at[0, mask], ks.at[1, mask], "expert", flipped(plane, mask)
            ).wait_recv()
        keep("select", select, sel_any)
        keep("x", x_all, x_any)
        keep("wq", wq_all, wq_any)
        keep("wkv", wkv_all, wkv_any)

        def x_block(rows_here, j):
            first = j * depth
            inner = first % width
            return x_all[first // width, rows_here, inner : inner + depth]

        def project(at, carry):
            here = pl.ds(pl.multiple_of(at * block, block), block)
            table = pl.ds(pl.multiple_of((at * block) % seq_len, block), block)
            cos_here, sin_here = cos_ref[table], sin_ref[table]
            blocks = [x_block(here, j) for j in range(data)]
            raw = sum(
                jnp.dot(blocks[j], wq_all[j], preferred_element_type=jnp.float32)
                for j in range(data)
            )
            q_raw[here] = raw
            for h in range(heads):
                one = raw[:, h * head : (h + 1) * head]
                one = one * row_scale(one) * gq_ref[...]
                turned = one * cos_here + half_turn(one) * sin_here
                q_low[here, h * head : (h + 1) * head] = turned.astype(jnp.bfloat16)
            kv = [sum(nt_dot(blocks[j], wkv_all[m, j]) for j in range(data)) for m in range(sharing)]
            raw = jnp.concatenate([item[:, :part] for item in kv], axis=1)
            k_raw[here] = raw
            one = raw * row_scale(raw) * gk_ref[...]
            k_low[here] = (one * cos_here + half_turn(one) * sin_here).astype(jnp.bfloat16)
            v_low[here] = jnp.concatenate([item[:, part:] for item in kv], axis=1).astype(
                jnp.bfloat16
            )
            return carry

        lax.fori_loop(0, total // block, project, 0)
        keep("q_raw", q_raw, qr_any)
        keep("q_low", q_low, ql_any)
        keep("k_raw", k_raw, kr_any)
        keep("k_low", k_low, kl_any)
        keep("v_low", v_low, vl_any)
        lane = lax.broadcasted_iota(jnp.int32, (block, head), 1)
        below = causal(0, block, block)
        lse[...] = jnp.zeros_like(lse)

        def send_grads(c):
            picked[c] = jnp.dot(
                select[...], g_all[c], preferred_element_type=jnp.float32
            ).astype(jnp.bfloat16)
            exchange.start(c)
            exchange.keep(c)

        def attend(h, carry):
            cols = pl.ds(pl.multiple_of(h * head, head), head)
            count = 0
            for seq in range(total // seq_len):
                base = seq * seq_len
                for at in range(seq_len // block):
                    here = pl.ds(base + at * block, block)
                    query = q_low[here, cols]
                    tiles = []
                    if at:
                        tiles.append(pl.ds(base, at * block))
                    tiles.append(here)
                    scores = [nt_dot(query, k_low[tile]) for tile in tiles]
                    scores[-1] = jnp.where(below, scores[-1], -jnp.inf)
                    top = jnp.max(scores[-1], axis=-1, keepdims=True)
                    if at:
                        top = jnp.maximum(top, jnp.max(scores[0], axis=-1, keepdims=True))
                    raised = [jnp.exp2((score - top) * (scale * LOG2_E)) for score in scores]
                    norm = sum(jnp.sum(item, axis=-1, keepdims=True) for item in raised)
                    inverse = 1.0 / norm
                    att[here, cols] = sum(
                        jnp.dot(
                            (item * inverse).astype(jnp.bfloat16),
                            v_low[tile],
                            preferred_element_type=jnp.float32,
                        )
                        for item, tile in zip(raised, tiles)
                    ).astype(jnp.bfloat16)
                    lse[here] = jnp.where(lane == h, top * scale + jnp.log(norm), lse[here])
                    count += 1
                    if count < data:

                        @pl.when(h < chunks - 1)
                        def _():
                            line.step(first_grad + h, count)

            @pl.when(h < chunks - 1)
            def _():
                for s in range(count + 1, data):
                    line.step(first_grad + h, s)
                send_grads(h)

            @pl.when(h == 0)
            def _():
                line.start(first_out)

            return carry

        lax.fori_loop(0, heads, attend, 0)
        keep("lse", lse, lse_any)
        keep("att", att, att_any)
        for c in range(heads, chunks - 1):
            for s in range(1, data):
                line.step(first_grad + c, s)
            send_grads(c)
        for k in range(first_last, items):
            line.start(k)

        def send_last(n):
            c, at, wide = last[n]
            picked[c, :, at : at + wide] = jnp.dot(
                select[...], g_all[c, :, at : at + wide], preferred_element_type=jnp.float32
            ).astype(jnp.bfloat16)
            exchange.start(chunks - 1 + n)
            exchange.keep(chunks - 1 + n)

        tail = []
        for n in range(len(last)):
            tail += [(n, s) for s in range(1, data)]

        def arrivals(s):
            if s == 0:
                return [(place, place >= 0, reduces[0])]
            return [
                (place - s, place >= s, reduces[(s + 1) % 2]),
                (place + s, place + s < data, reduces[s % 2]),
            ]

        def each(s, act):
            for j, present, reduce in arrivals(s):

                @pl.when(present)
                def _():
                    act(j, reduce)

        def project_out(j, reduce):
            acc[j] = (
                jnp.dot(att[...], wo_all[j], preferred_element_type=jnp.float32)
                .astype(jnp.bfloat16)
                .reshape(group, rows, cut)
            )
            reduce.start(j)

        for turn in range(data + steps):
            if turn < data:
                if turn:
                    line.step(first_out, turn)
                each(turn, project_out)
            for at in range(steps):
                if 0 <= turn - 1 - at < data:
                    each(turn - 1 - at, lambda j, reduce: reduce.advance(j, at))
            if turn >= data - 1:
                count = -(-len(tail) // (data + steps - turn))
                for n, s in tail[:count]:
                    line.step(first_last + n, s)
                    if s == data - 1:
                        send_last(n)
                tail = tail[count:]
        keep("wo", wo_all, wo_any)

        def branch_piece(j, reduce):
            reduce.result(j, hidden.at[:, pl.ds(pl.multiple_of(j * cut, cut), cut)])

        for s in range(data):
            each(s, branch_piece)
        summed = hidden[...] + tok_ref[...].astype(jnp.float32)
        hidden[...] = summed
        low = (summed * row_scale(summed) * gain2_ref[...]).astype(jnp.bfloat16)
        for c in range(chunks):
            second[c] = low[:, c * width : (c + 1) * width]
        logits = nt_dot(low, r_ref[...])
        masked = jnp.where(hot_ref[...] > 0, logits, -jnp.inf)
        raised = jnp.exp(masked - jnp.max(masked, axis=-1, keepdims=True))
        gate = raised / jnp.sum(raised, axis=-1, keepdims=True)
        probs[...] = gate
        top = gate.astype(jnp.bfloat16).astype(jnp.float32)
        parts = [top, gate - top]
        if extra > 2 * experts:
            parts.append(jnp.zeros((rows, extra - 2 * experts), jnp.float32))
        pair[...] = jnp.concatenate(parts, axis=1).astype(jnp.bfloat16)
        for k in range(turns_of_grads):
            exchange.wait(k)
        keep("g", g_here, g_any)
        for k in range(items):
            line.finish(k)
        gather.finish()
        for mask in range(1, sharing):
            share(mask).wait_send()
        for k in range(turns_of_grads):
            exchange.finish(k)
        for s in range(data):
            each(s, lambda j, reduce: reduce.finish(j))
        for copy in keeps.values():
            copy.wait()

    bf, fl = jnp.bfloat16, jnp.float32
    whole = pl.BlockSpec(memory_space=pltpu.VMEM)
    anywhere = pl.BlockSpec(memory_space=pl.ANY)

    def shape(*dims, dtype=bf):
        return jax.ShapeDtypeStruct(dims, dtype)

    kept = [
        shape(chunks, total, width),
        shape(data, depth, wide),
        shape(sharing, data, both, depth),
        shape(data, wide, cut),
        shape(chunks, entries, width),
        shape(entries, data * rows),
        shape(total, wide, dtype=fl),
        shape(total, wide),
        shape(total, head, dtype=fl),
        shape(total, head),
        shape(total, head),
        shape(total, head, dtype=fl),
        shape(total, wide),
    ]
    small = [
        shape(rows, model, dtype=fl),
        shape(chunks, rows, width),
        shape(rows, extra),
        shape(rows, experts, dtype=fl),
    ]
    return pl.pallas_call(
        kernel,
        out_shape=kept + small,
        in_specs=[whole] * 15,
        out_specs=[anywhere] * len(kept) + [whole] * len(small),
        scratch_shapes=[
            vmem((chunks, rows, width), bf),
            vmem((chunks, rows, width), bf),
            vmem((both, depth), bf),
            vmem((chunks, total, width), bf),
            vmem((data, depth, wide), bf),
            vmem((sharing, data, both, depth), bf),
            vmem((data, wide, cut), bf),
            vmem((chunks, data * rows, width), bf),
            vmem((data, experts, rows), fl),
            vmem((chunks, entries, width), bf),
            vmem((chunks, entries, width), bf),
            vmem((entries, data * rows), bf),
            vmem((total, wide), fl),
            vmem((total, wide), bf),
            vmem((total, head), fl),
            vmem((total, head), bf),
            vmem((total, head), bf),
            vmem((total, head), fl),
            vmem((total, wide), bf),
            vmem((data, group, rows, cut), bf),
            vmem((data, group - 1, rows, cut), bf),
            dma(2, chunks, group),
            dma(4, items, data - 1),
            dma(2, chunks - 1 + len(last), group),
            dma(2, sharing),
            dma(2, data, group - 1),
            dma(len(kept)),
        ],
        compiler_params=pltpu.CompilerParams(
            collective_id=1, has_side_effects=True, vmem_limit_bytes=VMEM_LIMIT
        ),
    )(
        tokens, gain, w_q, w_k, w_v, w_out, out_grad, slot_rows, cos, sin, gain_q, gain_k,
        gain2, router, hot,
    )


def local(
    tokens,
    norm1_gain,
    w_query,
    key_weight,
    value_weight,
    w_out,
    query_gain,
    key_gain,
    norm2_gain,
    w_router,
    w_gate,
    w_up,
    w_down,
    routes,
    out_grad,
):
    data_count = lax.axis_size("dp")
    group_count = lax.axis_size("expert")
    group_index = lax.axis_index("expert")
    local_rows = tokens.shape[0]
    model_width = tokens.shape[1]
    head_dim = query_gain.shape[0]
    heads_here = w_query.shape[1] // head_dim
    top_count = routes.shape[1]
    expert_total = data_count * group_count
    capacity = max(2, (local_rows * top_count * 9 + 8 * expert_total - 1) // (8 * expert_total))
    data_index = lax.axis_index("dp")
    own_expert = data_index * group_count + group_index
    expert_ids = jnp.arange(expert_total)
    hot = jnp.any(routes[:, :, None] == expert_ids[None, None, :], axis=1)
    earlier = (jnp.arange(local_rows)[:, None] > jnp.arange(local_rows)[None, :]).astype(jnp.bfloat16)
    rank = jnp.dot(earlier, hot.astype(jnp.bfloat16), preferred_element_type=jnp.float32)
    slot_rows = jnp.where(hot, rank, -1.0).T
    slots = whole_up(data_count * capacity, 16)
    width_k = key_weight.shape[1]
    all_rows = group_count * local_rows
    seq_len = min(SEQ_LEN, all_rows)
    router = w_router.T
    cos_rows, sine_rows = [jnp.asarray(table) for table in rope_arrays(seq_len, head_dim)]
    (
        gathered, q_blocks, kv_blocks, out_blocks, grads_here, select, query_raw, queries, key_raw,
        keys_low, values_low, log_sum, attended, hidden, second, pair, gate_probs,
    ) = front(
        tokens, norm1_gain[None], w_query, key_weight.T, value_weight.T, w_out, out_grad, slot_rows,
        cos_rows, sine_rows, query_gain[None], key_gain[None], norm2_gain[None], router,
        hot.astype(jnp.float32), capacity, slots, seq_len,
    )
    q_cols = q_blocks.reshape(model_width, -1)
    with_mix = all_rows <= group_count * slots
    (
        grad_h, grad_arrived, act, mixed, grad_hidden, grad_branch, grad_norm2, grad_router,
        turned, first_mix,
    ) = expert_layer(
        second, pair, gate_probs, hidden, out_grad, norm2_gain[None], router, select, grads_here,
        w_gate[0], w_up[0], w_down[0], out_blocks.shape[2], with_mix,
    )
    (
        grad_tokens, grad_wo, grad_wq, grad_wkv, grad_query_gain, grad_key_gain, grad_norm1,
        grad_norm2, grad_router, output,
    ) = attention_backward(
        grad_branch, out_blocks, gathered, q_cols, kv_blocks, query_raw, queries, key_raw, keys_low,
        values_low, log_sum, attended, cos_rows, sine_rows, query_gain[None], key_gain[None],
        mixed, turned, tokens, norm1_gain[None], grad_hidden, hidden, grad_norm2, grad_router, first_mix,
        seq_len, with_mix,
    )
    if not with_mix:
        output = (hidden + combine(mixed, select, slots, 5)).astype(jnp.bfloat16)
    (
        grad_gate_w, grad_up_w, grad_down, output, grad_tokens, grad_wq, grad_wo, grad_router,
        grad_wk, grad_wv, grad_norm1, grad_norm2, grad_query_gain, grad_key_gain,
    ) = expert_weight_grads(
        grad_h, grad_arrived, act, [output, grad_tokens, grad_wq, grad_wo, grad_router], grad_wkv,
        [grad_norm1, grad_norm2, grad_query_gain, grad_key_gain],
    )
    return (
        output,
        grad_tokens,
        grad_norm1.reshape(-1),
        grad_wq,
        grad_wk.T,
        grad_wv.T,
        grad_wo,
        grad_query_gain.reshape(-1),
        grad_key_gain.reshape(-1),
        grad_norm2.reshape(-1),
        grad_router.T,
        grad_gate_w,
        grad_up_w,
        grad_down,
    )


def solution(mesh):
    placed = (
        P(("dp", "expert"), None),
        P(),
        P("dp", "expert"),
        P("dp", "expert"),
        P("dp", "expert"),
        P("expert", "dp"),
        P(),
        P(),
        P(),
        P(),
        P(("dp", "expert"), None, None),
        P(("dp", "expert"), None, None),
        P(("dp", "expert"), None, None),
        P(("dp", "expert"), None),
        P(("dp", "expert"), None),
    )
    return jax.shard_map(
        local,
        mesh=mesh,
        in_specs=placed,
        out_specs=(
            P(("dp", "expert"), None),
            P(("dp", "expert"), None),
            P(),
            P("dp", "expert"),
            P("dp", "expert"),
            P("dp", "expert"),
            P("expert", "dp"),
            P(),
            P(),
            P(),
            P(),
            P(("dp", "expert"), None, None),
            P(("dp", "expert"), None, None),
            P(("dp", "expert"), None, None),
        ),
        check_vma=False,
    )
```
